32 devices in a mesh: wide: 16 (over z, y, x), tensor: 2 (over core).
Axes of the slice: x: 2, y: 2, z: 4, core: 2. Of those that a mesh axis runs over, the one named last changes fastest.
Arguments:
- inputs: bfloat16 [50176, 512], P(('wide', 'tensor')), may hold values from -6 to 6
- cotangent: bfloat16 [50176, 512], P(('wide', 'tensor')), may hold values from -6 to 6
- window_order: int32 [128, 392], P('wide'), may hold values from 0 to 391, as said below
- region_ids: int32 [50176], P('wide'), may hold values from 0 to 7, as said below
- clip_threshold: float32 [], replicated, may hold values from 4 to 9
- norm1_gain: bfloat16 [512], replicated, may hold values from 0.25 to 1.75
- norm1_shift: bfloat16 [512], replicated, may hold values from -1.5 to 1.5
- qkv_weight: bfloat16 [512, 1536], P('wide', 'tensor'), may hold values from -1 to 1
- qv_bias: bfloat16 [2, 512], P(None, 'tensor'), may hold values from -2.5 to 2.5
- rel_table: bfloat16 [16, 2535], P('tensor'), may hold values from -3.5 to 3.5
- out_weight: bfloat16 [512, 512], P('tensor', 'wide'), may hold values from -1 to 1
- out_bias: bfloat16 [512], replicated, may hold values from -2.5 to 2.5
- norm2_gain: bfloat16 [512], replicated, may hold values from 0.25 to 1.75
- norm2_shift: bfloat16 [512], replicated, may hold values from -1.5 to 1.5
- expand_weight: bfloat16 [512, 2048], P('wide', 'tensor'), may hold values from -0.25 to 0.25
- expand_bias: bfloat16 [2048], P('tensor'), may hold values from -2.5 to 2.5
- reduce_weight: bfloat16 [2048, 512], P('tensor', 'wide'), may hold values from -0.125 to 0.125
- reduce_bias: bfloat16 [512], replicated, may hold values from -2.5 to 2.5
Outputs:
- layer_out: bfloat16 [50176, 512], P(('wide', 'tensor'))
- input_grad: bfloat16 [50176, 512], P(('wide', 'tensor'))
- norm1_gain_grad: float32 [512], replicated
- norm1_shift_grad: float32 [512], replicated
- qkv_weight_grad: float32 [512, 1536], P('wide', 'tensor')
- qv_bias_grad: float32 [2, 512], P(None, 'tensor')
- rel_table_grad: float32 [16, 2535], P('tensor')
- out_weight_grad: float32 [512, 512], P('tensor', 'wide')
- out_bias_grad: float32 [512], replicated
- norm2_gain_grad: float32 [512], replicated
- norm2_shift_grad: float32 [512], replicated
- expand_weight_grad: float32 [512, 2048], P('wide', 'tensor')
- expand_bias_grad: float32 [2048], P('tensor')
- reduce_weight_grad: float32 [2048, 512], P('tensor', 'wide')
- reduce_bias_grad: float32 [512], replicated
- head_maxima: float32 [16], P('tensor')
- clipped_qkv: float32 [512, 1536], P('wide', 'tensor')
- clipped_bias: float32 [2, 512], P(None, 'tensor')
The draws below stay inside these ranges and needn't reach their ends.
Inputs may be any that keep to these rules, and one draw needn't show every extreme that they name: `window_order`: each row is a permutation of the 392 positions of a window, counted frame by frame, row by row. `region_ids`: tokens of one window with equal ids lie in the same region of the shifted partition.
All inputs are finite; a program needn't handle non-finite values.
Results may differ from the reference program's by a relative error of at most 0.012.
The reference program's roundings to bfloat16 on the way count: a program that leaves them out, or rounds other values in their place, can miss the bound.
Values may be sent and summed in bfloat16 or wider, within the bound.
A program may use at most 320 MiB of HBM per device.

```python
import math
import jax
import jax.numpy as jnp
from jax import lax

D = 512
HEADS = 16
HD = 32
FF = 2048
WT = 8
WH = 7
WW = 7
WIN = 392
RT = 2535
WINDOWS = 128
TOKENS = 50176


def window_layout(key):
    order_key = jax.random.fold_in(key, 17)
    window_keys = jax.random.split(order_key, WINDOWS)
    return jax.vmap(lambda single: jax.random.permutation(single, WIN))(window_keys).astype(jnp.int32)


def draw_window_order(key, part):
    return window_layout(key)


def draw_region_ids(key, part):
    order = window_layout(key)
    slot = jnp.arange(WINDOWS, dtype=jnp.int32) % 8
    cut_frame = slot // 4 % 2
    cut_row = slot // 2 % 2
    cut_column = slot % 2
    frame_at = order // (WH * WW)
    row_at = order // WW % WH
    column_at = order % WW
    late_frame = (frame_at >= WT - WT // 2).astype(jnp.int32)
    late_row = (row_at >= WH - WH // 2).astype(jnp.int32)
    late_column = (column_at >= WW - WW // 2).astype(jnp.int32)
    region = 4 * cut_frame[:, None] * late_frame + 2 * cut_row[:, None] * late_row + cut_column[:, None] * late_column
    return region.astype(jnp.int32).reshape(TOKENS)


def draw_qkv_weight(key, part):
    noise_key = jax.random.fold_in(key, 3)
    scale_key = jax.random.fold_in(key, 5)
    base = jax.random.normal(noise_key, (D, 3 * D), jnp.float32)
    head_scale = jnp.exp(jax.random.uniform(scale_key, (HEADS, 2), jnp.float32, math.log(0.7), math.log(1.6)))
    column_scale = jnp.concatenate([head_scale, jnp.ones((HEADS, 1), jnp.float32)], axis=1)
    column_scale = jnp.broadcast_to(column_scale[:, :, None], (HEADS, 3, HD)).reshape(3 * D)
    return (base * column_scale[None, :] * D ** (-0.5)).astype(jnp.bfloat16)


def levels(rng, dims, pieces, low, high):
    level = 1.0
    for axis_at, parts in pieces:
        steps = jax.random.uniform(jax.random.fold_in(jax.random.fold_in(rng, 6), axis_at), (parts,), jnp.float32, low / len(pieces), high / len(pieces))
        level = level * jnp.repeat(jnp.exp(steps), dims[axis_at] // parts).reshape((-1,) + (1,) * (len(dims) - 1 - axis_at))
    return level


def scatter_about(rng, dims, scale, bound, cuts=(), kind=jnp.bfloat16):
    entries = jax.random.normal(rng, dims, jnp.float32) * scale
    if len(cuts) > 0:
        entries = levels(rng, dims, cuts, -0.22, 0.18) * entries
    return jnp.clip(entries, min=-bound, max=bound).astype(kind)


def setup_inputs(seed: int = 0) -> dict:
    key_list = jax.random.split(jax.random.key(seed), 19)
    inputs = scatter_about(key_list[0], (TOKENS, D), 1.0, 6.0, ((0, 32),))
    cotangent = scatter_about(key_list[1], (TOKENS, D), 1.0, 6.0, ((0, 32),))
    window_order = draw_window_order(jax.random.fold_in(key_list[18], 71), 0)
    region_ids = draw_region_ids(jax.random.fold_in(key_list[18], 71), 0)
    clip_threshold = jnp.clip(jax.random.uniform(key_list[4], (), jnp.float32, 4.0, 9.0), 4.0, 9.0)
    norm1_gain = jnp.clip(1.0 + 0.15 * jax.random.normal(key_list[5], (D,), jnp.float32), 0.25, 1.75).astype(jnp.bfloat16)
    norm1_shift = scatter_about(key_list[6], (D,), 0.3, 1.5)
    qkv_weight = draw_qkv_weight(jax.random.fold_in(key_list[18], 71), 0)
    qv_bias = scatter_about(key_list[8], (2, D), 0.5, 2.5, ((1, 2),))
    rel_table = scatter_about(key_list[9], (HEADS, RT), 0.7, 3.5, ((0, 2),))
    out_weight = scatter_about(key_list[10], (D, D), (D // 16) ** -0.5, 1.0, ((0, 2), (1, 16)))
    out_bias = scatter_about(key_list[11], (D,), 0.5, 2.5)
    norm2_gain = jnp.clip(1.0 + 0.15 * jax.random.normal(key_list[12], (D,), jnp.float32), 0.25, 1.75).astype(jnp.bfloat16)
    norm2_shift = scatter_about(key_list[13], (D,), 0.3, 1.5)
    expand_weight = scatter_about(key_list[14], (D, FF), D ** -0.5, 0.25, ((0, 16), (1, 2)))
    expand_bias = scatter_about(key_list[15], (FF,), 0.5, 2.5, ((0, 2),))
    reduce_weight = scatter_about(key_list[16], (FF, D), FF ** -0.5, 0.125, ((0, 2), (1, 16)))
    reduce_bias = scatter_about(key_list[17], (D,), 0.5, 2.5)
    return dict(inputs=inputs, cotangent=cotangent, window_order=window_order, region_ids=region_ids, clip_threshold=clip_threshold, norm1_gain=norm1_gain, norm1_shift=norm1_shift, qkv_weight=qkv_weight, qv_bias=qv_bias, rel_table=rel_table, out_weight=out_weight, out_bias=out_bias, norm2_gain=norm2_gain, norm2_shift=norm2_shift, expand_weight=expand_weight, expand_bias=expand_bias, reduce_weight=reduce_weight, reduce_bias=reduce_bias)


@jax.custom_vjp
def low(v):
    return lax.optimization_barrier(v.astype(jnp.bfloat16)).astype(jnp.float32)

@jax.custom_vjp
def low_back(v):
    return v

def low_keep(v):
    return (low(v), None)

def low_pass(kept, grad):
    return (grad,)

def back_keep(v):
    return (v, None)

def back_low(kept, grad):
    return (low(grad),)
low.defvjp(low_keep, low_pass)
low_back.defvjp(back_keep, back_low)
epsilon = 1e-05
masked = -100.0
highest = lax.Precision.HIGHEST

def layer_norm(rows, gain, shift):
    mean = lax.optimization_barrier(jnp.mean(rows, axis=-1, keepdims=True))
    centered = rows - mean
    spread = lax.optimization_barrier(jnp.mean(centered * centered, axis=-1, keepdims=True))
    return centered * lax.rsqrt(spread + epsilon) * gain + shift

def relative_index(order):
    frame_at = order // (WH * WW)
    row_at = order // WW % WH
    column_at = order % WW
    frame_off = frame_at[:, None] - frame_at[None, :] + (WT - 1)
    row_off = row_at[:, None] - row_at[None, :] + (WH - 1)
    column_off = column_at[:, None] - column_at[None, :] + (WW - 1)
    return ((frame_off * (2 * WH - 1) + row_off) * (2 * WW - 1) + column_off).astype(jnp.int32)

def group_layer(params, rows, order_group, region_group):
    gain1, shift1, qkv_full, bias_pair, table, out_full, out_shift, gain2, shift2, expand_full, expand_shift, reduce_full, reduce_shift = params
    count = order_group.shape[0]
    normed = low(layer_norm(rows, gain1, shift1))
    head_bias = jnp.stack([bias_pair[0].reshape(HEADS, HD), jnp.zeros((HEADS, HD), jnp.float32), bias_pair[1].reshape(HEADS, HD)], axis=1).reshape(3 * D)
    projected = low(low_back(jnp.dot(normed, qkv_full, precision=highest) + head_bias))
    split = projected.reshape(count, WIN, HEADS, 3, HD).transpose(3, 0, 2, 1, 4)
    queries = split[0]
    key_rows = split[1]
    value_rows = split[2]
    raw = jnp.einsum('ghqd,ghkd->ghqk', queries, key_rows, precision=highest) * HD ** (-0.5)
    index = jax.vmap(relative_index)(order_group)
    bias = jnp.take(table, index, axis=1).transpose(1, 0, 2, 3)
    same = region_group[:, :, None] == region_group[:, None, :]
    scores = low_back(raw + bias + jnp.where(same, 0.0, masked)[:, None])
    probs = low(jax.nn.softmax(scores, axis=-1))
    attended = jnp.einsum('ghqk,ghkd->ghqd', probs, value_rows, precision=highest)
    attended = low(low_back(attended.transpose(0, 2, 1, 3).reshape(count * WIN, D)))
    attention = low_back(jnp.dot(attended, out_full, precision=highest) + out_shift)
    middle = rows + attention
    normed2 = low(layer_norm(middle, gain2, shift2))
    hidden = low_back(jnp.dot(normed2, expand_full, precision=highest) + expand_shift)
    active = low(jax.nn.gelu(hidden, approximate=False))
    result = middle + jnp.dot(active, reduce_full, precision=highest) + reduce_shift
    return (result, lax.optimization_barrier(jnp.max(raw, axis=(0, 2, 3))))

def reference(inputs, cotangent, window_order, region_ids, clip_threshold, norm1_gain, norm1_shift, qkv_weight, qv_bias, rel_table, out_weight, out_bias, norm2_gain, norm2_shift, expand_weight, expand_bias, reduce_weight, reduce_bias):
    params = tuple((item.astype(jnp.float32) for item in (norm1_gain, norm1_shift, qkv_weight, qv_bias, rel_table, out_weight, out_bias, norm2_gain, norm2_shift, expand_weight, expand_bias, reduce_weight, reduce_bias)))
    groups = WINDOWS // 8
    rows = inputs.astype(jnp.float32).reshape(groups, 8 * WIN, D)
    orders = window_order.reshape(groups, 8, WIN)
    regions = region_ids.reshape(groups, 8, WIN)

    def whole(rows_in, params_in):

        def step(item):
            return group_layer(params_in, item[0], item[1], item[2])
        result, peaks = lax.map(jax.checkpoint(step), (rows_in, orders, regions))
        return (result, lax.optimization_barrier(jnp.max(peaks, axis=0)))
    result, backward, head_maxima = jax.vjp(whole, rows, params, has_aux=True)
    input_grad, grads = backward(cotangent.astype(jnp.float32).reshape(groups, 8 * WIN, D))
    factor = jnp.sqrt(clip_threshold / jnp.maximum(head_maxima, clip_threshold))
    column_factor = jnp.stack([factor, factor, jnp.ones_like(factor)], axis=1)
    clipped_qkv = (qkv_weight.astype(jnp.float32).reshape(D, HEADS, 3, HD) * column_factor[None, :, :, None]).reshape(D, 3 * D)
    bias_scale = jnp.stack([jnp.repeat(factor, HD), jnp.ones_like(jnp.repeat(factor, HD))], axis=0)
    clipped_bias = qv_bias.astype(jnp.float32) * bias_scale
    return (result.reshape(TOKENS, D).astype(jnp.bfloat16), input_grad.reshape(TOKENS, D).astype(jnp.bfloat16), grads[0], grads[1], grads[2], grads[3], grads[4], grads[5], grads[6], grads[7], grads[8], grads[9], grads[10], grads[11], grads[12], head_maxima, clipped_qkv, clipped_bias)
```

```python
import functools
import math

import jax
import jax.numpy as jnp
from jax import lax
from jax.experimental import pallas as pl
from jax.experimental.pallas import tpu as pltpu
from jax.sharding import PartitionSpec as P

D = 512
HEADS = 16
HD = 32
FF = 2048
WT = 8
WH = 7
WW = 7
SP = WH * WW
WIN = 392
RT = 2535
ROWS = 13 * 13
GRP = 4

epsilon = 1e-05
masked = -100.0
lowest = -1e30
LOG2E = 1.4426950408889634
SCALE = HD ** (-0.5)
WIDE_SEG = 13 * WW * WT
WIDE_PAD = 768
FLAT = ROWS * WT
FLAT_PAD = 1408

f32 = jnp.float32
bf16 = jnp.bfloat16
NN = (((1,), (0,)), ((), ()))
NT = (((1,), (1,)), ((), ()))

VMEM_LIMIT = 60 * 2**20


def dot(a, b, dims=NN):
    return lax.dot_general(a, b, dims, preferred_element_type=f32)


def chunks(total, size):
    starts = list(range(0, total - size + 1, size))
    sizes = [size] * len(starts)
    rest = total - size * len(starts)
    if rest:
        if rest < size // 2:
            sizes[-1] += rest
        else:
            starts.append(size * len(starts))
            sizes.append(rest)
    return list(zip(starts, sizes))


ROW_CHUNKS = chunks(WIN, 64)


def iota(shape, axis):
    return lax.broadcasted_iota(jnp.int32, shape, axis)


def head_lanes(hh):
    return (iota((1, GRP * HD), 1) // HD == hh).astype(f32).astype(bf16)


def picks_in(place_row):
    return (iota((WIN, WIN), 0) == place_row).astype(f32).astype(bf16)


def picks_out(place_column):
    return (iota((WIN, WIN), 1) == place_column).astype(f32).astype(bf16)


def moments(rows):
    mean = jnp.mean(rows, axis=-1, keepdims=True)
    centered = rows - mean
    spread = jnp.mean(centered * centered, axis=-1, keepdims=True)
    return centered, lax.rsqrt(spread + epsilon)


def one_hot_flat():
    column = iota((FLAT_PAD, WIDE_PAD), 1)
    target = column // (WW * WT) * (13 * WT) + column % (WW * WT)
    hit = (iota((FLAT_PAD, WIDE_PAD), 0) == target) & (column < WIDE_SEG)
    return hit.astype(f32).astype(bf16)


def table_kernel(flat_ref, bias_ref, wide_ref):
    spread = one_hot_flat()
    flat = flat_ref[...]
    for wi in range(WW):
        shift = (WW - 1 - wi) * WT
        moved = pltpu.roll(flat, FLAT_PAD - shift, 1) if shift else flat
        wide_ref[...] = dot(moved.astype(bf16), spread) * LOG2E
        for hi in range(WH):
            at = (hi * WW + wi) * WT
            off = (WH - 1 - hi) * WW * WT
            rows = wide_ref[:, off : off + WIN]
            bias_ref[:, at : at + WT, :] = rows.reshape(HEADS, WT, WIN)


def table_bias(table):
    parts = table.astype(f32).reshape(HEADS, 2 * WT - 1, ROWS)[:, :, ::-1]
    flat = jnp.stack([parts[:, WT - 1 - tj : 2 * WT - 1 - tj] for tj in range(WT)], axis=-1)
    flat = flat.reshape(HEADS * WT, FLAT)
    flat = jnp.pad(flat, ((0, 0), (0, FLAT_PAD - FLAT)))
    return pl.pallas_call(
        table_kernel,
        out_shape=jax.ShapeDtypeStruct((HEADS, WIN, WIN), f32),
        scratch_shapes=[pltpu.VMEM((HEADS * WT, WIDE_PAD), f32)],
        compiler_params=pltpu.CompilerParams(vmem_limit_bytes=VMEM_LIMIT),
        name="table_bias",
    )(flat)


def table_back(flat_grad):
    parts = flat_grad[:, :FLAT].reshape(HEADS, WT, ROWS, WT)
    total = jnp.zeros((HEADS, 2 * WT - 1, ROWS), f32)
    for tj in range(WT):
        low = WT - 1 - tj
        total = total + jnp.pad(parts[:, :, :, tj], ((0, 0), (low, WT - 1 - low), (0, 0)))
    return total[:, :, ::-1].reshape(HEADS, RT)


def attend_kernel(
    kr, kc, rr, rc, x_ref, w_ref, wb_ref, bias_ref, wo_ref, bo_ref, g1, s1, g2, s2,
    xc_ref, nrm_ref, qkv_ref, e_ref, linv_ref, att_ref, mid_ref, n2_ref, hm_ref,
    x_scr, mask_scr,
):
    w = pl.program_id(0)
    pick = picks_in(kr[0])
    canon = dot(pick, x_ref[...])
    xc_ref[...] = canon.astype(bf16)
    row_at = jnp.sum(jnp.where(iota((WIN, WIN), 0) == kr[0], rr[0], 0.0), axis=1, keepdims=True)
    column_at = jnp.sum(jnp.where(iota((WIN, WIN), 1) == kc[0], rc[0], 0.0), axis=0, keepdims=True)
    mask_scr[...] = jnp.where(row_at == column_at, 0.0, masked * LOG2E)
    for at, size in ROW_CHUNKS:
        rows = xc_ref[at : at + size, :].astype(f32)
        centered, rstd = moments(rows)
        nrm_ref[at : at + size, :] = (centered * rstd * g1[...] + s1[...]).astype(bf16)
    for part in range(3):
        cols = slice(part * D, (part + 1) * D)
        qkv_ref[:, cols] = (dot(nrm_ref[...], w_ref[:, cols]) + wb_ref[:, cols]).astype(bf16)

    @pl.when(w == 0)
    def _():
        hm_ref[...] = jnp.full(hm_ref.shape, lowest, f32)

    def group(g, carry):
        off = pl.multiple_of(g * (GRP * HD), GRP * HD)
        qg = qkv_ref[:, pl.ds(off, GRP * HD)]
        kg = qkv_ref[:, pl.ds(D + off, GRP * HD)]
        vg = qkv_ref[:, pl.ds(2 * D + off, GRP * HD)]
        for hh in range(GRP):
            h = g * GRP + hh
            lanes = head_lanes(hh)
            slot = x_scr.at[hh % 2]
            slot[...] = dot(qg * lanes, kg, NT)
            top = hm_ref[h]
            sums = []
            for at, size in ROW_CHUNKS:
                xx = slot[at : at + size, :]
                top = jnp.maximum(top, jnp.max(xx.reshape(size // 8, 8, WIN), axis=0))
                s = xx * (SCALE * LOG2E) + bias_ref[h, at : at + size, :] + mask_scr[at : at + size, :]
                p = jnp.exp2(s - jnp.max(s, axis=1, keepdims=True))
                sums.append(jnp.sum(p, axis=1, keepdims=True))
                e_ref[0, h, at : at + size, :] = p.astype(bf16)
            hm_ref[h] = top
            out = dot(e_ref[0, h], vg)
            inv = 1.0 / jnp.concatenate(sums, axis=0)
            here = iota((WIN, GRP * HD), 1) // HD == hh
            inv = jnp.broadcast_to(inv, (WIN, GRP * HD))
            if hh == 0:
                total, scale = out * inv, inv
            else:
                total = jnp.where(here, out * inv, total)
                scale = jnp.where(here, inv, scale)
        att_ref[:, pl.ds(off, GRP * HD)] = total.astype(bf16)
        linv_ref[:, pl.ds(off, GRP * HD)] = scale
        return carry

    lax.fori_loop(0, HEADS // GRP, group, 0)
    mid_ref[...] = xc_ref[...].astype(f32) + (dot(att_ref[...], wo_ref[...], NT) + bo_ref[...])
    for at, size in ROW_CHUNKS:
        centered, rstd = moments(mid_ref[at : at + size, :])
        n2_ref[at : at + size, :] = (centered * rstd * g2[...] + s2[...]).astype(bf16)


def gelu_both(hidden):
    z = jnp.abs(hidden) * (0.5**0.5)
    t = 1.0 / (1.0 + 0.3275911 * z)
    poly = 1.061405429
    for coefficient in (-1.453152027, 1.421413741, -0.284496736, 0.254829592):
        poly = poly * t + coefficient
    bell = jnp.exp2(hidden * hidden * (-0.5 * LOG2E))
    tail = 0.5 * poly * t * bell
    cdf = jnp.where(hidden >= 0.0, 1.0 - tail, tail)
    return hidden * cdf, cdf + hidden * bell * (1.0 / math.sqrt(2.0 * math.pi))


FC = 512


def feed_kernel(
    kr, kc, mid_ref, n2_ref, cot_ref, we_ref, be_ref, wr_ref, br_ref, g2,
    out_ref, mgrad_ref, dwe_ref, dwr_ref, dbe_ref, vec_ref,
    cc_scr, cT_scr, nT_scr, acc_scr, ng_scr,
):
    w = pl.program_id(0)

    @pl.when(w == 0)
    def _():
        dwe_ref[...] = jnp.zeros_like(dwe_ref)
        dwr_ref[...] = jnp.zeros_like(dwr_ref)
        dbe_ref[...] = jnp.zeros_like(dbe_ref)
        vec_ref[...] = jnp.zeros_like(vec_ref)

    canon = dot(picks_in(kr[0]), cot_ref[...])
    cc_scr[...] = canon.astype(bf16)
    cT_scr[...] = cc_scr[...].T
    nT_scr[...] = n2_ref[...].T

    def block(c, carry):
        off = pl.multiple_of(c * FC, FC)
        cols = pl.ds(off, FC)
        we = we_ref[:, cols]
        wr = wr_ref[:, cols]
        hidden = dot(n2_ref[...], we) + be_ref[:, cols]
        act, slope = gelu_both(hidden)
        act = act.astype(bf16)
        hg = (dot(cc_scr[...], wr) * slope).astype(bf16)
        feed = dot(act, wr, NT)
        back = dot(hg, we, NT)

        @pl.when(c == 0)
        def _():
            acc_scr[...] = feed
            ng_scr[...] = back

        @pl.when(c > 0)
        def _():
            acc_scr[...] += feed
            ng_scr[...] += back

        dwr_ref[:, cols] += dot(cT_scr[...], act)
        dwe_ref[:, cols] += dot(nT_scr[...], hg)
        dbe_ref[:, cols] += jnp.sum(hg.astype(f32), axis=0, keepdims=True)
        return carry

    lax.fori_loop(0, FF // FC, block, 0)
    for at, size in ROW_CHUNKS:
        rows = slice(at, at + size)
        mid = mid_ref[rows, :]
        cot = cc_scr[rows, :].astype(f32)
        acc_scr[rows, :] = mid + (acc_scr[rows, :] + br_ref[...])
        back = ng_scr[rows, :]
        centered, rstd = moments(mid)
        xhat = centered * rstd
        g = back * g2[...]
        mg = cot + rstd * (
            g - jnp.mean(g, axis=-1, keepdims=True) - xhat * jnp.mean(g * xhat, axis=-1, keepdims=True)
        )
        mgrad_ref[rows, :] = mg
        vec_ref[0:1, :] += jnp.sum(back * xhat, axis=0, keepdims=True)
        vec_ref[1:2, :] += jnp.sum(back, axis=0, keepdims=True)
        vec_ref[2:3, :] += jnp.sum(cot, axis=0, keepdims=True)
        vec_ref[3:4, :] += jnp.sum(mg.astype(bf16).astype(f32), axis=0, keepdims=True)
    out_ref[...] = dot(picks_out(kc[0]), acc_scr[...].astype(bf16)).astype(bf16)


def back_kernel(
    kc, xc_ref, nrm_ref, qkv_ref, e_ref, linv_ref, att_ref, mg_ref, w_ref, wo_ref, g1,
    out_ref, dw_ref, dwo_ref, db_ref, vec_ref, flat_ref,
    ag_scr, dop_scr, doT_scr, qT_scr, in_scr, x_scr, ds_scr, pg_scr, dvT_scr, dkT_scr, table_scr,
    seg_scr, wide_scr, grad_scr,
):
    w = pl.program_id(0)
    last = pl.num_programs(0) - 1

    @pl.when(w == 0)
    def _():
        dw_ref[...] = jnp.zeros_like(dw_ref)
        dwo_ref[...] = jnp.zeros_like(dwo_ref)
        db_ref[...] = jnp.zeros_like(db_ref)
        vec_ref[...] = jnp.zeros_like(vec_ref)
        table_scr[...] = jnp.zeros_like(table_scr)

    ag_scr[...] = mg_ref[...].astype(bf16)
    dwo_ref[...] += dot(ag_scr[...].T, att_ref[...])
    scaled = dot(ag_scr[...], wo_ref[...]).astype(bf16).astype(f32) * linv_ref[...]
    dop_scr[...] = scaled.astype(bf16)
    in_scr[...] = dop_scr[...].astype(f32) * att_ref[...].astype(f32)
    doT_scr[...] = dop_scr[...].T
    qT_scr[...] = qkv_ref[:, 0:D].T

    def group(g, carry):
        off = pl.multiple_of(g * (GRP * HD), GRP * HD)
        kg = qkv_ref[:, pl.ds(D + off, GRP * HD)]
        vg = qkv_ref[:, pl.ds(2 * D + off, GRP * HD)]
        dg = dop_scr[:, pl.ds(off, GRP * HD)]
        ig = in_scr[:, pl.ds(off, GRP * HD)]
        total = None
        for hh in range(GRP):
            h = g * GRP + hh
            lanes = head_lanes(hh)
            slot = x_scr.at[hh % 2]
            dslot = ds_scr.at[hh % 2]
            slot[...] = dot(dg * lanes, vg, NT)
            inner = jnp.sum(jnp.where(iota((WIN, GRP * HD), 1) // HD == hh, ig, 0.0), axis=1, keepdims=True)
            for at, size in ROW_CHUNKS:
                rows = slice(at, at + size)
                ds = (e_ref[0, h, rows, :].astype(f32) * (slot[rows, :] - inner[rows, :])).astype(bf16)
                dslot[rows, :] = ds
                table_scr[h, rows, :] += ds.astype(f32)
            hrow = pl.ds(pl.multiple_of(off + hh * HD, HD), HD)
            dvT_scr[hrow, :] = dot(doT_scr[hrow, :], e_ref[0, h]).astype(bf16)
            dkT_scr[hrow, :] = (dot(qT_scr[hrow, :], dslot[...]) * SCALE).astype(bf16)
            part = dot(dslot[...], kg * lanes)
            total = part if total is None else total + part
        pg_scr[:, pl.ds(off, GRP * HD)] = (total * SCALE).astype(bf16)
        return carry

    lax.fori_loop(0, HEADS // GRP, group, 0)
    pg_scr[:, D : 2 * D] = dkT_scr[...].T
    pg_scr[:, 2 * D :] = dvT_scr[...].T
    nT = nrm_ref[...].T
    for part in range(3):
        cols = slice(part * D, (part + 1) * D)
        dw_ref[:, cols] += dot(nT, pg_scr[:, cols])
        db_ref[:, cols] += jnp.sum(pg_scr[:, cols].astype(f32), axis=0, keepdims=True)
    grad_scr[...] = dot(pg_scr[...], w_ref[...], NT)
    for at, size in ROW_CHUNKS:
        rows = slice(at, at + size)
        back = grad_scr[rows, :]
        centered, rstd = moments(xc_ref[rows, :].astype(f32))
        xhat = centered * rstd
        g = back * g1[...]
        vec_ref[0:1, :] += jnp.sum(back * xhat, axis=0, keepdims=True)
        vec_ref[1:2, :] += jnp.sum(back, axis=0, keepdims=True)
        ag_scr[rows, :] = (
            mg_ref[rows, :]
            + rstd * (g - jnp.mean(g, axis=-1, keepdims=True) - xhat * jnp.mean(g * xhat, axis=-1, keepdims=True))
        ).astype(bf16)
    out_ref[...] = dot(picks_out(kc[0]), ag_scr[...]).astype(bf16)

    @pl.when(w == last)
    def _():
        spread = one_hot_flat()
        seg_scr[...] = jnp.zeros_like(seg_scr)
        flat_ref[...] = jnp.zeros_like(flat_ref)
        for wi in range(WW):
            total = None
            for hi in range(WH):
                at = (hi * WW + wi) * WT
                off = (WH - 1 - hi) * WW * WT
                seg_scr[:, 0:WIN] = table_scr[:, at : at + WT, :].reshape(HEADS * WT, WIN)
                moved = seg_scr[...]
                if off:
                    moved = pltpu.roll(moved, off, 1)
                total = moved if total is None else total + moved
            top = total.astype(bf16)
            low = (total - top.astype(f32)).astype(bf16)
            flat = dot(top, spread, NT) + dot(low, spread, NT)
            shift = (WW - 1 - wi) * WT
            flat_ref[...] += pltpu.roll(flat, shift, 1) if shift else flat


def whole(shape):
    return pl.BlockSpec(shape, lambda w: (0,) * len(shape))


def kept(shape):
    return pl.BlockSpec(shape, lambda w: (0,) * len(shape), pipeline_mode=pl.Buffered(1))


def per(shape):
    rest = (0,) * (len(shape) - 1)
    return pl.BlockSpec(shape, lambda w: (w,) + rest)


def shape_of(shape, dtype):
    return jax.ShapeDtypeStruct(shape, dtype)


PARAMS = pltpu.CompilerParams(dimension_semantics=("arbitrary",), vmem_limit_bytes=VMEM_LIMIT)


def run_attend(nw, kr, kc, rr, rc, x, w, wb, bias, wo, bo, g1, s1, g2, s2):
    rows = nw * WIN
    tok = per((WIN, D))
    return pl.pallas_call(
        attend_kernel,
        grid=(nw,),
        in_specs=[
            per((1, 1, WIN)), per((1, WIN, 1)), per((1, 1, WIN)), per((1, WIN, 1)), tok,
            kept((D, 3 * D)), kept((1, 3 * D)), kept((HEADS, WIN, WIN)), kept((D, D)),
            kept((1, D)), kept((1, D)), kept((1, D)), kept((1, D)), kept((1, D)),
        ],
        out_specs=[
            tok, tok, per((WIN, 3 * D)), per((1, HEADS, WIN, WIN)), tok, tok, tok, tok,
            whole((HEADS, 8, WIN)),
        ],
        out_shape=[
            shape_of((rows, D), bf16),
            shape_of((rows, D), bf16),
            shape_of((rows, 3 * D), bf16),
            shape_of((nw, HEADS, WIN, WIN), bf16),
            shape_of((rows, D), f32),
            shape_of((rows, D), bf16),
            shape_of((rows, D), f32),
            shape_of((rows, D), bf16),
            shape_of((HEADS, 8, WIN), f32),
        ],
        scratch_shapes=[pltpu.VMEM((2, WIN, WIN), f32), pltpu.VMEM((WIN, WIN), f32)],
        compiler_params=PARAMS,
        name="attend",
    )(kr, kc, rr, rc, x, w, wb, bias, wo, bo, g1, s1, g2, s2)


def run_feed(nw, kr, kc, mid, n2, cot, we, be, wr, br, g2):
    rows = nw * WIN
    tok = per((WIN, D))
    return pl.pallas_call(
        feed_kernel,
        grid=(nw,),
        in_specs=[
            per((1, 1, WIN)), per((1, WIN, 1)), tok, tok, tok,
            kept((D, FF)), kept((1, FF)), kept((D, FF)), kept((1, D)), kept((1, D)),
        ],
        out_specs=[tok, tok, whole((D, FF)), whole((D, FF)), whole((1, FF)), whole((8, D))],
        out_shape=[
            shape_of((rows, D), bf16),
            shape_of((rows, D), f32),
            shape_of((D, FF), f32),
            shape_of((D, FF), f32),
            shape_of((1, FF), f32),
            shape_of((8, D), f32),
        ],
        scratch_shapes=[
            pltpu.VMEM((WIN, D), bf16),
            pltpu.VMEM((D, WIN), bf16),
            pltpu.VMEM((D, WIN), bf16),
            pltpu.VMEM((WIN, D), f32),
            pltpu.VMEM((WIN, D), f32),
        ],
        compiler_params=PARAMS,
        name="feed",
    )(kr, kc, mid, n2, cot, we, be, wr, br, g2)


def run_back(nw, kc, xc, nrm, qkv, e, linv, att, mg, w, wo, g1):
    rows = nw * WIN
    tok = per((WIN, D))
    return pl.pallas_call(
        back_kernel,
        grid=(nw,),
        in_specs=[
            per((1, WIN, 1)), tok, tok, per((WIN, 3 * D)), per((1, HEADS, WIN, WIN)), tok, tok, tok,
            kept((D, 3 * D)), kept((D, D)), kept((1, D)),
        ],
        out_specs=[
            tok, whole((D, 3 * D)), whole((D, D)), whole((1, 3 * D)), whole((8, D)),
            whole((HEADS * WT, FLAT_PAD)),
        ],
        out_shape=[
            shape_of((rows, D), bf16),
            shape_of((D, 3 * D), f32),
            shape_of((D, D), f32),
            shape_of((1, 3 * D), f32),
            shape_of((8, D), f32),
            shape_of((HEADS * WT, FLAT_PAD), f32),
        ],
        scratch_shapes=[
            pltpu.VMEM((WIN, D), bf16),
            pltpu.VMEM((WIN, D), bf16),
            pltpu.VMEM((D, WIN), bf16),
            pltpu.VMEM((D, WIN), bf16),
            pltpu.VMEM((WIN, D), f32),
            pltpu.VMEM((2, WIN, WIN), f32),
            pltpu.VMEM((2, WIN, WIN), bf16),
            pltpu.VMEM((WIN, 3 * D), bf16),
            pltpu.VMEM((D, WIN), bf16),
            pltpu.VMEM((D, WIN), bf16),
            pltpu.VMEM((HEADS, WIN, WIN), f32),
            pltpu.VMEM((HEADS * WT, WIDE_PAD), f32),
            pltpu.VMEM((8, 128), f32),
            pltpu.VMEM((WIN, D), f32),
        ],
        compiler_params=PARAMS,
        name="attend_back",
    )(kc, xc, nrm, qkv, e, linv, att, mg, w, wo, g1)


BOTH = ("wide", "tensor")


def body(
    inputs, cotangent, window_order, region_ids, clip_threshold, norm1_gain, norm1_shift,
    qkv_weight, qv_bias, rel_table, out_weight, out_bias, norm2_gain, norm2_shift,
    expand_weight, expand_bias, reduce_weight, reduce_bias,
):
    parts = lax.axis_size("tensor")
    groups = lax.axis_size("wide")
    mine = lax.axis_index("tensor")
    own = HEADS // parts
    nw = inputs.shape[0] // WIN
    strip = D // groups

    order = lax.dynamic_slice_in_dim(window_order, mine * nw, nw, 0)
    place = order % SP * WT + order // SP
    regions = lax.dynamic_slice_in_dim(region_ids, mine * nw * WIN, nw * WIN, 0)
    regions = regions.reshape(nw, WIN).astype(f32)
    kr, kc = place[:, None, :], place[:, :, None]
    rr, rc = regions[:, None, :], regions[:, :, None]

    def row(v):
        return v.astype(f32)[None]

    qkv_strip = qkv_weight.reshape(strip, own, 3, HD).transpose(0, 2, 1, 3).reshape(strip, 3 * own * HD)
    shard = jnp.concatenate([qkv_strip, out_weight.T, expand_weight, reduce_weight.T], axis=1)
    full = lax.all_gather(shard, BOTH, axis=0)
    full = full.reshape(groups, parts, strip, shard.shape[1]).transpose(0, 2, 1, 3)
    full = full.reshape(D, parts, shard.shape[1])
    oc, fc = D // parts, FF // parts
    wqkv = full[:, :, : 3 * oc].reshape(D, parts, 3, oc).transpose(0, 2, 1, 3).reshape(D, 3 * D)
    wo = full[:, :, 3 * oc : 4 * oc].reshape(D, D)
    we = full[:, :, 4 * oc : 4 * oc + fc].reshape(D, FF)
    wr = full[:, :, 4 * oc + fc :].reshape(D, FF)
    small = jnp.concatenate([qv_bias.reshape(-1), expand_bias, rel_table.reshape(-1)])
    small = lax.all_gather(small, "tensor", axis=0)
    qv = small[:, : 2 * oc].reshape(parts, 2, oc).transpose(1, 0, 2).reshape(2, D).astype(f32)
    be = small[:, 2 * oc : 2 * oc + fc].reshape(1, FF).astype(f32)
    table = small[:, 2 * oc + fc :].reshape(HEADS, RT)
    wb = jnp.concatenate([qv[0:1], jnp.zeros((1, D), f32), qv[1:2]], axis=1)

    bias = table_bias(table)
    xc, nrm, qkv, e, linv, att, mid, n2, hm = run_attend(
        nw, kr, kc, rr, rc, inputs, wqkv, wb, bias, wo, row(out_bias),
        row(norm1_gain), row(norm1_shift), row(norm2_gain), row(norm2_shift),
    )
    layer_out, mg, dwe, dwr, dbe, vec2 = run_feed(
        nw, kr, kc, mid, n2, cotangent, we, be, wr, row(reduce_bias), row(norm2_gain)
    )
    input_grad, dw, dwo, db, vec1, flat = run_back(
        nw, kc, xc, nrm, qkv, e, linv, att, mg, wqkv, wo, row(norm1_gain)
    )

    grads = jnp.concatenate(
        [
            dw.reshape(D, 3, parts, oc).transpose(2, 0, 1, 3).reshape(parts, D, 3 * oc),
            dwo.reshape(D, parts, oc).transpose(1, 0, 2),
            dwe.reshape(D, parts, fc).transpose(1, 0, 2),
            dwr.reshape(D, parts, fc).transpose(1, 0, 2),
        ],
        axis=2,
    )
    grads = grads.reshape(parts, groups, strip, shard.shape[1]).transpose(1, 0, 2, 3)
    grads = grads.reshape(groups * parts * strip, shard.shape[1])
    mine_grad = lax.psum_scatter(grads, BOTH, scatter_dimension=0, tiled=True)
    qkv_out = (
        mine_grad[:, : 3 * oc].reshape(strip, 3, own, HD).transpose(0, 2, 1, 3).reshape(strip, 3 * oc)
    )
    out_out = mine_grad[:, 3 * oc : 4 * oc].T
    expand_out = mine_grad[:, 4 * oc : 4 * oc + fc]
    reduce_out = mine_grad[:, 4 * oc + fc :].T

    table_grad = table_back(flat)
    bias_grad = jnp.concatenate([db[:, :D], db[:, 2 * D :]], axis=0)
    sums = lax.psum((vec1[:2], vec2[:4], dbe, bias_grad, table_grad), BOTH)
    v1, v2, dbe_all, bias_all, table_all = sums
    peak = lax.pmax(jnp.max(hm, axis=(1, 2)) * SCALE, BOTH)
    start = mine * own
    peak_own = lax.dynamic_slice_in_dim(peak, start, own, 0)
    factor = jnp.sqrt(clip_threshold / jnp.maximum(peak_own, clip_threshold))
    column_factor = jnp.stack([factor, factor, jnp.ones_like(factor)], axis=1)
    clipped_qkv = (
        qkv_weight.astype(f32).reshape(strip, own, 3, HD) * column_factor[None, :, :, None]
    ).reshape(qkv_weight.shape)
    bias_scale = jnp.stack([jnp.repeat(factor, HD), jnp.ones((own * HD,), f32)], axis=0)
    clipped_bias = qv_bias.astype(f32) * bias_scale
    return (
        layer_out,
        input_grad,
        v1[0],
        v1[1],
        qkv_out,
        lax.dynamic_slice_in_dim(bias_all, start * HD, oc, 1),
        lax.dynamic_slice_in_dim(table_all, start, own, 0),
        out_out,
        v2[3],
        v2[0],
        v2[1],
        expand_out,
        lax.dynamic_slice_in_dim(dbe_all[0], mine * fc, fc, 0),
        reduce_out,
        v2[2],
        peak_own,
        clipped_qkv,
        clipped_bias,
    )


def solution(mesh):
    tokens = P(BOTH, None)
    in_specs = (
        tokens, tokens, P("wide", None), P("wide"), P(), P(), P(), P("wide", "tensor"),
        P(None, "tensor"), P("tensor", None), P("tensor", "wide"), P(), P(), P(),
        P("wide", "tensor"), P("tensor"), P("tensor", "wide"), P(),
    )
    out_specs = (
        tokens, tokens, P(), P(), P("wide", "tensor"), P(None, "tensor"), P("tensor", None),
        P("tensor", "wide"), P(), P(), P(), P("wide", "tensor"), P("tensor"),
        P("tensor", "wide"), P(), P("tensor"), P("wide", "tensor"), P(None, "tensor"),
    )
    return jax.shard_map(body, mesh=mesh, in_specs=in_specs, out_specs=out_specs, check_vma=False)
```

```python
import functools
import math

import jax
import jax.numpy as jnp
from jax import lax
from jax.experimental import pallas as pl
from jax.experimental.pallas import tpu as pltpu
from jax.sharding import PartitionSpec as P

D = 512
HEADS = 16
HD = 32
FF = 2048
WT = 8
WH = 7
WW = 7
SP = WH * WW
WIN = 392
RT = 2535
ROWS = 13 * 13
GRP = 4

epsilon = 1e-05
masked = -100.0
lowest = -1e30
LOG2E = 1.4426950408889634
SCALE = HD ** (-0.5)
WIDE_SEG = 13 * WW * WT
WIDE_PAD = 768
PITCH = 176
FLAT_PAD = 1408
UP = 256
HALF = D // 2
QW = 3 * HALF
VW = QW + FF // 2

f32 = jnp.float32
bf16 = jnp.bfloat16
NN = (((1,), (0,)), ((), ()))
NT = (((1,), (1,)), ((), ()))
TN = (((0,), (0,)), ((), ()))

VMEM_LIMIT = 60 * 2**20


def dot(a, b, dims=NN):
    return lax.dot_general(a, b, dims, preferred_element_type=f32)


def chunks(total, size):
    starts = list(range(0, total - size + 1, size))
    sizes = [size] * len(starts)
    rest = total - size * len(starts)
    if rest:
        if rest < size // 2:
            sizes[-1] += rest
        else:
            starts.append(size * len(starts))
            sizes.append(rest)
    return list(zip(starts, sizes))


ROW_CHUNKS = chunks(WIN, 64)


def iota(shape, axis):
    return lax.broadcasted_iota(jnp.int32, shape, axis)


def group_at(g):
    return pl.multiple_of(g // 2 * QW + g % 2 * (GRP * HD), GRP * HD)


def head_lanes(hh):
    return (iota((1, GRP * HD), 1) // HD == hh).astype(f32).astype(bf16)


def picks_of(order_ref, w):
    order = order_ref[pl.ds(w, 1), :]
    return iota((WIN, WIN), 0) == order % SP * WT + order // SP


def one_hot(hit):
    return hit.astype(f32).astype(bf16)


def column_moves():
    new = iota((1, QW), 1)
    old = new % HALF // HD * (3 * HD) + new // HALF * HD + new % HD
    return one_hot(iota((QW, QW), 0) == old)


def moments(rows):
    mean = jnp.mean(rows, axis=-1, keepdims=True)
    centered = rows - mean
    spread = jnp.mean(centered * centered, axis=-1, keepdims=True)
    return centered, lax.rsqrt(spread + epsilon)


def one_hot_spread():
    column = iota((1, WIDE_PAD), 1)
    dh, rest = column // (WW * WT), column % (WW * WT)
    target = rest % WT * PITCH + (12 - dh) * 13 + 6 - rest // WT
    target = jnp.where(column < WIDE_SEG, target, -1)
    return (iota((FLAT_PAD, WIDE_PAD), 0) == target).astype(f32).astype(bf16)


def flatten_table(table_ref, flat_ref):
    total = None
    rest = jnp.zeros((HEADS * WT, FLAT_PAD - UP), f32)
    for tj in range(WT):
        rows = table_ref[:, WT - 1 - tj : 2 * WT - 1 - tj, :].reshape(HEADS * WT, UP)
        part = jnp.concatenate([rows, rest], axis=1)
        if tj:
            part = pltpu.roll(part, tj * PITCH, 1)
        total = part if total is None else total + part
    flat_ref[...] = total


def turn_table(flat_ref, wide_ref, out_ref):
    flat = flat_ref[...]
    for wi in range(WW):
        wide_ref[wi] = (pltpu.roll(flat, FLAT_PAD - wi, 1) if wi else flat).astype(bf16)
    out_ref[...] = dot(wide_ref[...].reshape(WW * HEADS * WT, FLAT_PAD), one_hot_spread()) * LOG2E


def spread_table(turned_ref, bias_ref):
    for wi in range(WW):
        for hi in range(WH):
            at = (hi * WW + wi) * WT
            off = (WH - 1 - hi) * WW * WT
            rows = turned_ref[wi * HEADS * WT : (wi + 1) * HEADS * WT, off : off + WIN]
            bias_ref[:, at : at + WT, :] = rows.reshape(HEADS, WT, WIN)


def table_kernel(table_ref, bias_ref, flat_ref, wide_ref, turned_ref):
    flatten_table(table_ref, flat_ref)
    turn_table(flat_ref, wide_ref, turned_ref)
    spread_table(turned_ref, bias_ref)


TABLE_SCRATCH = [
    pltpu.VMEM((HEADS * WT, FLAT_PAD), f32),
    pltpu.VMEM((WW, HEADS * WT, FLAT_PAD), bf16),
    pltpu.VMEM((WW * HEADS * WT, WIDE_PAD), f32),
]


def padded_table(table):
    parts = table.astype(f32).reshape(-1, 2 * WT - 1, ROWS)
    return jnp.pad(parts, ((0, 0), (0, 1), (0, UP - ROWS)))


def table_bias(table):
    return pl.pallas_call(
        table_kernel,
        out_shape=jax.ShapeDtypeStruct((HEADS, WIN, WIN), f32),
        scratch_shapes=TABLE_SCRATCH,
        compiler_params=pltpu.CompilerParams(vmem_limit_bytes=VMEM_LIMIT),
        name="table_bias",
    )(padded_table(table))


def fold_table(table_scr, seg_scr, wide_scr, out_ref):
    seg_scr[...] = jnp.zeros_like(seg_scr)
    for wi in range(WW):
        total = None
        for hi in range(WH):
            at = (hi * WW + wi) * WT
            off = (WH - 1 - hi) * WW * WT
            seg_scr[:, 0:WIN] = table_scr[:, at : at + WT, :].reshape(HEADS * WT, WIN)
            moved = seg_scr[...]
            if off:
                moved = pltpu.roll(moved, off, 1)
            total = moved if total is None else total + moved
        wide_scr[wi] = total.astype(bf16)
    flat = dot(wide_scr[...].reshape(WW * HEADS * WT, WIDE_PAD), one_hot_spread(), NT)
    total = None
    for wi in range(WW):
        part = flat[wi * HEADS * WT : (wi + 1) * HEADS * WT, :]
        part = pltpu.roll(part, wi, 1) if wi else part
        total = part if total is None else total + part
    out_ref[...] = jnp.zeros_like(out_ref)
    for tj in range(WT):
        rows = pltpu.roll(total, FLAT_PAD - tj * PITCH, 1) if tj else total
        out_ref[:, WT - 1 - tj : 2 * WT - 1 - tj, :] += rows[:, :UP].reshape(HEADS, WT, UP)


def attend_kernel(nb, order_ref, region_ref, x_ref, *rest):
    if nb:
        (params_ref, table_ref, own_ref), shards, rest = rest[:3], rest[3:6], rest[6:]
    else:
        (vecs_ref, w_ref, bias_ref), rest = rest[:3], rest[3:]
    (xc_ref, nrm_ref, qkv_ref, e_ref, linv_ref, att_ref, peak_ref), rest = rest[:7], rest[7:]
    if nb:
        (vecs_out, w_out), bufs, rest = rest[:2], rest[2:5], rest[5:]
    (x_scr, mask_scr, hm_ref), rest = rest[:3], rest[3:]
    w, g = pl.program_id(0), pl.program_id(1)
    at_step = w * (HEADS // GRP) + g
    opening = (w == 0) & (g == 0)
    if nb:
        (vecs_ref, w_scr, bias_ref, own_scr, tables, flat_ref, wide_ref, turned_ref), sems = rest[:8], rest[8:]
        place = Place(nb)
        first = Gather(place, [own_scr], [w_scr], *sems[:3])
        second = Gather(place, shards, bufs, *sems[3:])
        base = Gather.copies(nb, 1)
        mine = pl.ds(pl.multiple_of(place.t * (HEADS // 2), HEADS // 2), HEADS // 2)
        near = [
            remote(part, part, sems[0].at[base + i], sems[1].at[base + i], place.sibling())
            for i, part in enumerate((tables.at[mine], vecs_ref.at[place.t]))
        ]

    def prepare():
        pick = picks_of(order_ref, w)
        region = region_ref[pl.ds(w, 1), :]
        row_at = jnp.sum(jnp.where(pick, region, 0.0), axis=1, keepdims=True)
        pick = one_hot(pick)
        column_at = dot(jnp.broadcast_to(region, (8, WIN)).astype(bf16), pick, NT)[0:1, :]
        mask_scr[...] = jnp.where(row_at == column_at, 0.0, masked * LOG2E)
        xc_ref[...] = dot(pick, x_ref[...]).astype(bf16)
        for at, size in ROW_CHUNKS:
            centered, rstd = moments(xc_ref[at : at + size, :].astype(f32))
            nrm_ref[at : at + size, :] = (centered * rstd * vecs_ref[0, 1:2, 0:D] + vecs_ref[0, 2:3, 0:D]).astype(bf16)

    def project():
        weight = w_scr[...].reshape(D, 3 * D) if nb else w_ref
        for v in range(2):
            cols = slice(v * QW, (v + 1) * QW)
            qkv_ref[:, cols] = (dot(nrm_ref[...], weight[:, cols]) + vecs_ref[v, 0:1, 0:QW]).astype(bf16)

    def group():
        off = pl.multiple_of(g * (GRP * HD), GRP * HD)
        qoff = group_at(g)
        qg = qkv_ref[:, pl.ds(qoff, GRP * HD)]
        kg = qkv_ref[:, pl.ds(qoff + HALF, GRP * HD)]
        vg = qkv_ref[:, pl.ds(qoff + 2 * HALF, GRP * HD)]
        vx = jnp.concatenate([vg, jnp.ones((WIN, GRP * HD), bf16)], axis=1)

        def score(hh):
            x_scr[hh % 2] = dot(qg * head_lanes(hh), kg, NT)

        def soften(hh):
            h = g * GRP + hh
            top = hm_ref[h]
            for at, size in ROW_CHUNKS:
                xx = x_scr[hh % 2, at : at + size, :]
                top = jnp.maximum(top, jnp.max(xx.reshape(size // 8, 8, WIN), axis=0))
                s = xx * (SCALE * LOG2E) + bias_ref[h, at : at + size, :] + mask_scr[at : at + size, :]
                e_ref[0, hh, at : at + size, :] = jnp.exp2(s - jnp.max(s, axis=1, keepdims=True)).astype(bf16)
            hm_ref[h] = top

        def weigh(hh, total, scale):
            out = dot(e_ref[0, hh], vx)
            inv = 1.0 / out[:, GRP * HD :]
            out = out[:, : GRP * HD] * inv
            if hh == 0:
                return out, inv
            here = iota((WIN, GRP * HD), 1) // HD == hh
            return jnp.where(here, out, total), jnp.where(here, inv, scale)

        total = scale = None
        score(0)
        for hh in range(GRP):
            if hh + 1 < GRP:
                score(hh + 1)
            soften(hh)
            if hh:
                total, scale = weigh(hh - 1, total, scale)
        total, scale = weigh(GRP - 1, total, scale)
        att_ref[:, pl.ds(off, GRP * HD)] = total.astype(bf16)
        linv_ref[:, pl.ds(off, GRP * HD)] = scale

    @pl.when(opening)
    def _():
        hm_ref[...] = jnp.full(hm_ref.shape, lowest, f32)
        if nb:
            place.greet()
            own_scr[...] = dot(own_ref[...], column_moves()).astype(bf16)
            first.step(0)
            tables[mine] = table_ref[...]
            vecs_ref[place.t] = params_ref[...]
            for copy in near:
                copy.start()
            for copy in near:
                copy.wait()
            flatten_table(tables, flat_ref)
            first.step(1)

    @pl.when(g == 0)
    def _():
        prepare()

    if nb:

        @pl.when(opening)
        def _():
            first.step(2)
            turn_table(flat_ref, wide_ref, turned_ref)
            first.step(3)
            second.step(0)
            spread_table(turned_ref, bias_ref)
            for p in range(4, first.steps()):
                first.step(p)
            w_out[...] = w_scr[...].reshape(D, 3 * D)
            vecs_out[...] = vecs_ref[...]

        run_beside(second, at_step, GATHER_TIMES)

    @pl.when(g == 0)
    def _():
        project()

    group()

    @pl.when(at_step == pl.num_programs(0) * pl.num_programs(1) - 1)
    def _():
        lane = iota((1, D), 1)
        peaks = jnp.full((1, D), lowest, f32)
        for h in range(HEADS):
            top = jnp.max(jnp.max(hm_ref[h], axis=0, keepdims=True), axis=1, keepdims=True)
            peaks = jnp.where(lane == h, top * SCALE, peaks)
        peak_ref[...] = jnp.broadcast_to(peaks, peak_ref.shape)


def gelu_both(hidden):
    z = jnp.abs(hidden) * (0.5**0.5)
    base = 1.0 + 0.3275911 * z
    t = pl.reciprocal(base, approx=True)
    t = t * (2.0 - base * t)
    poly = 1.061405429
    for coefficient in (-1.453152027, 1.421413741, -0.284496736, 0.254829592):
        poly = poly * t + coefficient
    bell = jnp.exp2(hidden * hidden * (-0.5 * LOG2E))
    tail = 0.5 * poly * t * bell
    cdf = jnp.where(hidden >= 0.0, 1.0 - tail, tail)
    return hidden * cdf, cdf + hidden * bell * (1.0 / math.sqrt(2.0 * math.pi))


FC = 256
FEED_CHUNKS = chunks(WIN, 32)


def feed_kernel(
    order_ref, vecs_ref, xc_ref, att_ref, cot_ref, wo_ref, we_ref, wr_ref,
    out_ref, mgrad_ref, gwe_ref, gwr_ref, gwo_ref, vec_ref,
    mid_ref, n2_ref, cc_scr, cT_scr, nT_scr, acc_scr, ng_scr, dwe_ref, dwr_ref, dwo_ref,
    hid_scr, ag_scr, act_scr, hg_scr,
):
    w = pl.program_id(0)

    @pl.when(w == 0)
    def _():
        dwe_ref[...] = jnp.zeros_like(dwe_ref)
        dwr_ref[...] = jnp.zeros_like(dwr_ref)
        dwo_ref[...] = jnp.zeros_like(dwo_ref)
        vec_ref[...] = jnp.zeros_like(vec_ref)

    g2, s2, bo, br = (vecs_ref[0, i : i + 1, 0:D] for i in (3, 4, 5, 6))
    pick = one_hot(picks_of(order_ref, w))
    mid_ref[...] = xc_ref[...].astype(f32) + (dot(att_ref[...], wo_ref[...], NT) + bo)
    for at, size in ROW_CHUNKS:
        centered, rstd = moments(mid_ref[at : at + size, :])
        n2_ref[at : at + size, :] = (centered * rstd * g2 + s2).astype(bf16)
    canon = dot(pick, cot_ref[...])
    cc_scr[...] = canon.astype(bf16)
    cT_scr[...] = cc_scr[...].T
    nT_scr[...] = n2_ref[...].T

    blocks = [slice(c * FC, (c + 1) * FC) for c in range(FF // FC)]

    def widen(c):
        hid_scr[c % 2] = dot(n2_ref[...], we_ref[:, blocks[c]])
        ag_scr[c % 2] = dot(cc_scr[...], wr_ref[:, blocks[c]])

    def bend(c):
        half, off = divmod(c * FC, FF // 2)
        shift = vecs_ref[half, 0:1, QW + off : QW + off + FC]
        total = jnp.zeros((8, FC), f32)
        for at, size in FEED_CHUNKS:
            rows = slice(at, at + size)
            act, slope = gelu_both(hid_scr[c % 2, rows, :] + shift)
            act_scr[rows, blocks[c]] = act.astype(bf16)
            hg = (ag_scr[c % 2, rows, :] * slope).astype(bf16)
            hg_scr[rows, blocks[c]] = hg
            total += jnp.sum(hg.astype(f32).reshape(size // 8, 8, FC), axis=0)
        line, off = divmod(c * FC, D)
        vec_ref[4 + line : 5 + line, off : off + FC] += jnp.sum(total, axis=0, keepdims=True)

    def gather_up(c):
        dwr_ref[:, blocks[c]] += dot(cT_scr[...], act_scr[:, blocks[c]])
        dwe_ref[:, blocks[c]] += dot(nT_scr[...], hg_scr[:, blocks[c]])

    widen(0)
    for c in range(FF // FC):
        if c + 1 < FF // FC:
            widen(c + 1)
        bend(c)
        if c:
            gather_up(c - 1)
    gather_up(FF // FC - 1)
    acc_scr[...] = dot(act_scr[...], wr_ref[...], NT)
    ng_scr[...] = dot(hg_scr[...], we_ref[...], NT)
    for at, size in ROW_CHUNKS:
        rows = slice(at, at + size)
        mid = mid_ref[rows, :]
        cot = cc_scr[rows, :].astype(f32)
        acc_scr[rows, :] = mid + (acc_scr[rows, :] + br)
        back = ng_scr[rows, :]
        centered, rstd = moments(mid)
        xhat = centered * rstd
        g = back * g2
        mg = cot + rstd * (
            g - jnp.mean(g, axis=-1, keepdims=True) - xhat * jnp.mean(g * xhat, axis=-1, keepdims=True)
        )
        mgrad_ref[rows, :] = mg
        vec_ref[0:1, :] += jnp.sum(back * xhat, axis=0, keepdims=True)
        vec_ref[1:2, :] += jnp.sum(back, axis=0, keepdims=True)
        vec_ref[2:3, :] += jnp.sum(cot, axis=0, keepdims=True)
        vec_ref[3:4, :] += jnp.sum(mg.astype(bf16).astype(f32), axis=0, keepdims=True)
    out_ref[...] = dot(pick, acc_scr[...].astype(bf16), TN).astype(bf16)
    cT_scr[...] = mgrad_ref[...].astype(bf16).T
    dwo_ref[...] += dot(cT_scr[...], att_ref[...])

    @pl.when(w == pl.num_programs(0) - 1)
    def _():
        for grad, acc, width in ((gwe_ref, dwe_ref, FF // 2), (gwr_ref, dwr_ref, FF // 2), (gwo_ref, dwo_ref, HALF)):
            for v in range(2):
                for at in range(0, D, 64):
                    grad[v, at : at + 64, :] = acc[at : at + 64, v * width : (v + 1) * width].astype(bf16)


def back_kernel(
    nb, plans, order_ref, vecs_ref, xc_ref, nrm_ref, qkv_ref, e_ref, linv_ref, att_ref, mg_ref, w_ref, wo_ref,
    feed_ref, peak_ref, *rest
):
    if nb:
        matrices, rest = rest[:3], rest[3:]
        (out_ref, sums_out, table_out, qkv_out), outs, rest = rest[:4], rest[4:7], rest[7:]
    else:
        (out_ref, acc, table_out, gw_ref), rest = rest[:4], rest[4:]
    (
        dw_ref, wide_scr, ag_scr, dop_scr, doT_scr, qT_scr, in_scr, x_scr, ds_scr, pg_scr, dvT_scr, dkT_scr,
        table_scr, seg_scr, grad_scr,
    ), rest = rest[:15], rest[15:]
    w, g = pl.program_id(0), pl.program_id(1)
    end = HEADS // GRP - 1
    at_step = w * (HEADS // GRP) + g
    closing = at_step == pl.num_programs(0) * pl.num_programs(1) - 1
    if nb:
        (gw_ref, fold_scr, own_out, vec, vec_in, table, table_in), rest = rest[:7], rest[7:]
        acc = vec.at[0]
        place = Place(nb)
        count = [len(plan) * (nb + 2) for plan in plans]
        early, rest = rest[: count[0]], rest[count[0] :]
        late, sems = rest[: count[1]], rest[count[1] :]
        first = Scatter(place, build_streams(plans[0], matrices, early, outs, nb), *sems[:3])
        second = Scatter(place, build_streams(plans[1], [gw_ref], late, [own_out], nb), *sems[3:])
        sums = Sums(place, vec, vec_in, table, table_in, sems[3], sems[4], len(plans[1]) * (nb + 1))

    def prepare():
        ag_scr[...] = mg_ref[...].astype(bf16)
        scaled = dot(ag_scr[...], wo_ref[...]).astype(bf16).astype(f32) * linv_ref[...]
        dop_scr[...] = scaled.astype(bf16)
        in_scr[...] = (dop_scr[...].astype(f32) * -att_ref[...].astype(f32)).astype(bf16)
        doT_scr[...] = dop_scr[...].T
        for v in range(2):
            qT_scr[v * HALF : (v + 1) * HALF, :] = qkv_ref[:, v * QW : v * QW + HALF].T

    def group():
        off = pl.multiple_of(g * (GRP * HD), GRP * HD)
        qoff = group_at(g)
        kg = qkv_ref[:, pl.ds(qoff + HALF, GRP * HD)]
        vg = qkv_ref[:, pl.ds(qoff + 2 * HALF, GRP * HD)]
        vx = jnp.concatenate([vg, jnp.ones((WIN, GRP * HD), bf16)], axis=1)
        dx = jnp.concatenate([dop_scr[:, pl.ds(off, GRP * HD)], in_scr[:, pl.ds(off, GRP * HD)]], axis=1)

        def score(hh):
            lanes = head_lanes(hh)
            x_scr[hh % 2] = dot(dx * jnp.concatenate([lanes, lanes], axis=1), vx, NT)

        def differ(hh):
            h = g * GRP + hh
            for at, size in ROW_CHUNKS:
                rows = slice(at, at + size)
                ds = (e_ref[0, hh, rows, :].astype(f32) * x_scr[hh % 2, rows, :]).astype(bf16)
                ds_scr[hh % 2, rows, :] = ds
                table_scr[h, rows, :] += ds.astype(f32)

        def spread(hh, total):
            hrow = pl.ds(pl.multiple_of(off + hh * HD, HD), HD)
            ds = ds_scr[hh % 2]
            dvT_scr[hrow, :] = dot(doT_scr[hrow, :], e_ref[0, hh]).astype(bf16)
            dkT_scr[hrow, :] = (dot(qT_scr[hrow, :], ds) * SCALE).astype(bf16)
            part = dot(ds, kg * head_lanes(hh))
            return part if total is None else total + part

        total = None
        score(0)
        for hh in range(GRP):
            if hh + 1 < GRP:
                score(hh + 1)
            differ(hh)
            if hh:
                total = spread(hh - 1, total)
        total = spread(GRP - 1, total)
        pg_scr[:, pl.ds(qoff, GRP * HD)] = (total * SCALE).astype(bf16)

    def collect():
        for v in range(2):
            heads = slice(v * HALF, (v + 1) * HALF)
            pg_scr[:, v * QW + HALF : v * QW + 2 * HALF] = dkT_scr[heads, :].T
            pg_scr[:, v * QW + 2 * HALF : (v + 1) * QW] = dvT_scr[heads, :].T
        nT = nrm_ref[...].T
        for part in range(3):
            cols = slice(part * D, (part + 1) * D)
            dw_ref[:, cols] += dot(nT, pg_scr[:, cols])
            acc[10 + part : 11 + part, :] += jnp.sum(pg_scr[:, cols].astype(f32), axis=0, keepdims=True)

    def finish():
        grad_scr[...] = dot(pg_scr[...], w_ref[...], NT)
        for at, size in ROW_CHUNKS:
            rows = slice(at, at + size)
            back = grad_scr[rows, :]
            centered, rstd = moments(xc_ref[rows, :].astype(f32))
            xhat = centered * rstd
            g = back * vecs_ref[0, 1:2, 0:D]
            acc[0:1, :] += jnp.sum(back * xhat, axis=0, keepdims=True)
            acc[1:2, :] += jnp.sum(back, axis=0, keepdims=True)
            ag_scr[rows, :] = (
                mg_ref[rows, :]
                + rstd * (g - jnp.mean(g, axis=-1, keepdims=True) - xhat * jnp.mean(g * xhat, axis=-1, keepdims=True))
            ).astype(bf16)
        out_ref[...] = dot(one_hot(picks_of(order_ref, w)), ag_scr[...], TN).astype(bf16)

    @pl.when(at_step == 0)
    def _():
        dw_ref[...] = jnp.zeros_like(dw_ref)
        acc[...] = jnp.zeros((VEC_ROWS, D), f32)
        table_scr[...] = jnp.zeros_like(table_scr)
        if nb:
            place.greet()
            first.step(0)

    if nb:
        run_beside(first, at_step, SCATTER_TIMES)

    @pl.when(g == 0)
    def _():
        prepare()

    group()

    @pl.when(g == end)
    def _():
        collect()

    @pl.when(closing)
    def _():
        strip = D >> nb if nb else D
        for v in range(2):
            for at in range(0, D, 64):
                part = dw_ref[at : at + 64, v * QW : (v + 1) * QW].astype(bf16)
                if nb:
                    for i in range(64 // strip):
                        bits = tuple((at // strip + i) // (1 << k) % 2 for k in reversed(range(nb)))
                        gw_ref[(v, *bits)] = part[i * strip : (i + 1) * strip, :]
                else:
                    gw_ref[v, at : at + 64, :] = part
        if nb:
            second.step(0)

    @pl.when(g == end)
    def _():
        finish()

    @pl.when(closing)
    def _():
        acc[2:10, :] = feed_ref[...]
        acc[SUM_ROWS:VEC_ROWS, :] = peak_ref[...]
        if not nb:
            fold_table(table_scr, seg_scr, wide_scr, table_out)
            return
        second.step(1)
        for p in range(1, first.steps()):
            if SCATTER_TIMES[min(p, len(SCATTER_TIMES) - 1)] >= 1.0:
                first.step(p)
        fold_table(table_scr, seg_scr, wide_scr, fold_scr)
        half = HEADS // 2
        for v in range(2):
            table[v] = fold_scr[v * half : (v + 1) * half].astype(bf16)
        for p in range(second.steps()):
            sums.step(p, sums_out, table_out)
            if p + 2 < second.steps():
                second.step(p + 2)
        top = own_out[...].astype(bf16)
        low = (own_out[...] - top.astype(f32)).astype(bf16)
        moves = column_moves()
        qkv_out[...] = dot(top, moves, NT) + dot(low, moves, NT)


def whole(shape):
    return pl.BlockSpec(shape, lambda *at: (0,) * len(shape))


def kept(shape):
    return pl.BlockSpec(shape, lambda *at: (0,) * len(shape), pipeline_mode=pl.Buffered(1))


def per(shape):
    rest = (0,) * (len(shape) - 1)
    return pl.BlockSpec(shape, lambda w, *at: (w,) + rest)


EXPS = pl.BlockSpec((1, GRP, WIN, WIN), lambda w, g: (w, g, 0, 0))


def shape_of(shape, dtype):
    return jax.ShapeDtypeStruct(shape, dtype)


PARAMS = pltpu.CompilerParams(vmem_limit_bytes=VMEM_LIMIT)
ANY = pl.BlockSpec(memory_space=pl.ANY)
SUM_ROWS = 16
VEC_ROWS = 24


def dma(*counts):
    return [pltpu.SemaphoreType.DMA((n,)) for n in counts]


def run_attend(nw, nb, order, region, x, weights, shards):
    rows = nw * WIN
    tok = per((WIN, D))
    out_specs = [tok, tok, per((WIN, 3 * D)), EXPS, tok, tok, whole((8, D))]
    out_shape = [
        shape_of((rows, D), bf16),
        shape_of((rows, D), bf16),
        shape_of((rows, 3 * D), bf16),
        shape_of((nw, HEADS, WIN, WIN), bf16),
        shape_of((rows, D), f32),
        shape_of((rows, D), bf16),
        shape_of((8, D), f32),
    ]
    scratch = [pltpu.VMEM((2, WIN, WIN), f32), pltpu.VMEM((WIN, WIN), f32), pltpu.VMEM((HEADS, 8, WIN), f32)]
    if nb:
        strip = D >> nb
        copies, more = Gather.copies(nb, 1) + 2, Gather.copies(nb, len(shards))
        out_specs += [whole((2, 8, VW)), whole((D, 3 * D)), *[ANY] * len(shards)]
        out_shape += [shape_of((2, 8, VW), f32), shape_of((D, 3 * D), bf16)]
        out_shape += [shape_of((2,) * nb + (strip, 2 * v.shape[1]), bf16) for v in shards]
        scratch += [
            pltpu.VMEM((2, 8, VW), f32),
            pltpu.VMEM((2,) * nb + (strip, 3 * D), bf16),
            pltpu.VMEM((HEADS, WIN, WIN), f32),
            pltpu.VMEM((strip, QW), bf16),
            pltpu.VMEM((HEADS, 2 * WT, UP), f32),
            *TABLE_SCRATCH,
            *dma(copies, copies, 1, more, more, len(shards)),
        ]
    out = pl.pallas_call(
        functools.partial(attend_kernel, nb),
        grid=(nw, HEADS // GRP),
        in_specs=[
            kept((nw, WIN)), kept((nw, WIN)), tok, *(kept(v.shape) for v in weights), *[ANY] * len(shards),
        ],
        out_specs=out_specs,
        out_shape=out_shape,
        scratch_shapes=scratch,
        compiler_params=comm_params(2) if nb else PARAMS,
        name="attend",
    )(order, region, x, *weights, *shards)
    if nb:
        return out[:9], [v.reshape(D, v.shape[-1]) for v in out[9:]]
    return (*out, weights[0], weights[1]), []


def run_feed(nw, order, vecs, xc, att, cot, wo, we, wr):
    rows = nw * WIN
    tok = per((WIN, D))
    return pl.pallas_call(
        feed_kernel,
        grid=(nw,),
        in_specs=[
            kept((nw, WIN)), kept((2, 8, VW)), tok, tok, tok, kept((D, D)), kept((D, FF)), kept((D, FF)),
        ],
        out_specs=[
            tok, tok, whole((2, D, FF // 2)), whole((2, D, FF // 2)), whole((2, D, HALF)), whole((8, D)),
        ],
        out_shape=[
            shape_of((rows, D), bf16),
            shape_of((rows, D), f32),
            shape_of((2, D, FF // 2), bf16),
            shape_of((2, D, FF // 2), bf16),
            shape_of((2, D, HALF), bf16),
            shape_of((8, D), f32),
        ],
        scratch_shapes=[
            pltpu.VMEM((WIN, D), f32),
            pltpu.VMEM((WIN, D), bf16),
            pltpu.VMEM((WIN, D), bf16),
            pltpu.VMEM((D, WIN), bf16),
            pltpu.VMEM((D, WIN), bf16),
            pltpu.VMEM((WIN, D), f32),
            pltpu.VMEM((WIN, D), f32),
            pltpu.VMEM((D, FF), f32),
            pltpu.VMEM((D, FF), f32),
            pltpu.VMEM((D, D), f32),
            pltpu.VMEM((2, WIN, FC), f32),
            pltpu.VMEM((2, WIN, FC), f32),
            pltpu.VMEM((WIN, FF), bf16),
            pltpu.VMEM((WIN, FF), bf16),
        ],
        compiler_params=PARAMS,
        name="feed",
    )(order, vecs, xc, att, cot, wo, we, wr)


def run_back(nw, nb, order, vecs, xc, nrm, qkv, e, linv, att, mg, w, wo, feed, peak, grads):
    rows = nw * WIN
    tok = per((WIN, D))
    folded = (HEADS, 2 * WT, UP)
    half = (HEADS // 2, 2 * WT, UP)
    scratch = [
        pltpu.VMEM((D, 3 * D), f32),
        pltpu.VMEM((WW, HEADS * WT, WIDE_PAD), bf16),
        pltpu.VMEM((WIN, D), bf16),
        pltpu.VMEM((WIN, D), bf16),
        pltpu.VMEM((D, WIN), bf16),
        pltpu.VMEM((D, WIN), bf16),
        pltpu.VMEM((WIN, D), bf16),
        pltpu.VMEM((2, WIN, WIN), f32),
        pltpu.VMEM((2, WIN, WIN), bf16),
        pltpu.VMEM((WIN, 3 * D), bf16),
        pltpu.VMEM((D, WIN), bf16),
        pltpu.VMEM((D, WIN), bf16),
        pltpu.VMEM((HEADS, WIN, WIN), f32),
        pltpu.VMEM((HEADS * WT, WIDE_PAD), f32),
        pltpu.VMEM((WIN, D), f32),
    ]
    out_specs = [tok, whole((VEC_ROWS, D))]
    out_shape = [shape_of((rows, D), bf16), shape_of((VEC_ROWS, D), f32)]
    plans = []
    if nb:
        strip = D >> nb
        widths = [v.shape[2] for v in grads]
        plans = [stream_plan(nb, widths, strip), stream_plan(nb, [QW], strip)]
        copies = [len(plan) * (nb + 1) for plan in plans]
        more = copies[1] + 2 * (nb + 1)
        out_specs += [whole(half), whole((strip, QW)), *(whole((strip, width)) for width in widths)]
        out_shape += [shape_of(half, f32), shape_of((strip, QW), f32)]
        out_shape += [shape_of((strip, width), f32) for width in widths]
        scratch += [
            pltpu.VMEM((2,) * (nb + 1) + (strip, QW), bf16),
            pltpu.VMEM(folded, f32),
            pltpu.VMEM((strip, QW), f32),
            pltpu.VMEM((nb + 1, VEC_ROWS, D), f32),
            pltpu.VMEM((nb + 1, VEC_ROWS, D), f32),
            pltpu.VMEM((nb + 2, *half), bf16),
            pltpu.VMEM((nb + 1, *half), bf16),
        ]
        for plan, among in zip(plans, (widths, [QW])):
            for m, first, size, order_of in plan:
                scratch += Scatter.arrivals(nb, size, among[m])
        scratch += dma(copies[0], copies[0], len(plans[0]), more, more, len(plans[1]))
        grads = [v.reshape((2,) * (nb + 1) + (strip, v.shape[2])) for v in grads]
    else:
        grads = []
        out_specs += [whole(folded), whole((2, D, QW))]
        out_shape += [shape_of(folded, f32), shape_of((2, D, QW), bf16)]
    return pl.pallas_call(
        functools.partial(back_kernel, nb, plans),
        grid=(nw, HEADS // GRP),
        in_specs=[
            kept((nw, WIN)), kept((2, 8, VW)), tok, tok, per((WIN, 3 * D)), EXPS, tok, tok, tok,
            kept((D, 3 * D)), kept((D, D)), kept((8, D)), kept((8, D)), *[ANY] * len(grads),
        ],
        out_specs=out_specs,
        out_shape=out_shape,
        scratch_shapes=scratch,
        compiler_params=comm_params(3) if nb else PARAMS,
        name="attend_back",
    )(order, vecs, xc, nrm, qkv, e, linv, att, mg, w, wo, feed, peak, *grads)


BOTH = ("wide", "tensor")
MESH = pl.DeviceIdType.MESH


def bits_of(groups):
    return groups.bit_length() - 1


def orders_of(nb):
    down = tuple(reversed(range(nb)))
    return (down, down[:-2] + (down[-1], down[-2])) if nb > 1 else (down, down)


class Place:
    def __init__(self, nb):
        self.nb = nb
        self.w = lax.axis_index("wide")
        self.t = lax.axis_index("tensor")
        self.bit = [self.w // (1 << k) % 2 for k in range(nb)]

    def across(self, k):
        return (self.w + (1 - 2 * self.bit[k]) * (1 << k), self.t)

    def sibling(self):
        return (self.w, 1 - self.t)

    def greet(self):
        barrier = pltpu.get_barrier_semaphore()
        partners = [self.across(k) for k in range(self.nb)] + [self.sibling()]
        for partner in partners:
            pl.semaphore_signal(barrier, inc=1, device_id=partner, device_id_type=MESH)
        pl.semaphore_wait(barrier, len(partners))

    def index(self, chosen):
        return tuple(chosen.get(k, slice(None)) for k in reversed(range(self.nb)))


def remote(src, dst, send, recv, to):
    return pltpu.make_async_remote_copy(
        src_ref=src, dst_ref=dst, send_sem=send, recv_sem=recv, device_id=to, device_id_type=MESH
    )


class Gather:
    def __init__(self, place, owns, bufs, send, recv, near):
        self.place, self.owns, self.bufs = place, owns, bufs
        self.send, self.recv, self.near = send, recv, near
        nb = place.nb
        self.streams = []
        for own, buf in zip(owns, bufs):
            strip = own.shape[0]
            for half, order in enumerate(orders_of(nb)):
                self.streams.append((own, buf, pl.ds(half * strip // 2, strip // 2), order))

    @staticmethod
    def copies(nb, count):
        return count * (2 * nb + 1)

    def lanes(self, own):
        width = own.shape[1]
        return pl.ds(pl.multiple_of(self.place.t * width, 128), width)

    def local(self, b):
        own, buf = self.owns[b], self.bufs[b]
        mine = self.place.index(dict(enumerate(self.place.bit)))
        return pltpu.make_async_copy(own, buf.at[(*mine, slice(None), self.lanes(own))], self.near.at[b])

    def wide(self, s, p):
        own, buf, rows, order = self.streams[s]
        place = self.place
        chosen = {k: place.bit[k] for k in order[p:]}
        region = buf.at[(*place.index(chosen), rows, self.lanes(own))]
        src = region if p else own.at[rows, :]
        at = s * place.nb + p
        return remote(src, region, self.send.at[at], self.recv.at[at], place.across(order[p]))

    def core(self, b):
        own, buf = self.owns[b], self.bufs[b]
        region = buf.at[(*self.place.index({}), slice(None), self.lanes(own))]
        at = len(self.streams) * self.place.nb + b
        return remote(region, region, self.send.at[at], self.recv.at[at], self.place.sibling())

    def step(self, p):
        nb = self.place.nb
        streams, count = range(len(self.streams)), range(len(self.bufs))
        if p == 0:
            for b in count:
                self.local(b).start()
        elif p == 1:
            for b in count:
                self.local(b).wait()
        if 0 < p <= nb:
            for s in streams:
                self.wide(s, p - 1).wait_recv()
        if p < nb:
            for s in streams:
                self.wide(s, p).start()
        elif p == nb:
            for b in count:
                self.core(b).start()
        else:
            for s in streams:
                for q in range(nb):
                    self.wide(s, q).wait_send()
            for b in count:
                self.core(b).wait()

    def steps(self):
        return self.place.nb + 2


class Scatter:
    def __init__(self, place, streams, send, recv, near):
        self.place, self.streams = place, streams
        self.send, self.recv, self.near = send, recv, near

    @staticmethod
    def arrivals(nb, rows, width):
        return [pltpu.VMEM((2,) * (nb - max(p, 0)) + (rows, width), bf16) for p in range(-1, nb + 1)]

    def local(self, s):
        matrix, first, size, order, (own, *arrive), out = self.streams[s]
        src = matrix.at[(self.place.t, *self.place.index({}), pl.ds(first, size), slice(None))]
        return pltpu.make_async_copy(src, own, self.near.at[s])

    def left(self, order, p):
        return [k for k in reversed(range(self.place.nb)) if k not in order[:p]]

    def copy(self, s, p):
        matrix, first, size, order, (own, *arrive), out = self.streams[s]
        place = self.place
        if p == 0:
            src, to = matrix.at[(1 - place.t, *place.index({}), pl.ds(first, size), slice(None))], place.sibling()
        else:
            k = order[p - 1]
            src = arrive[p - 1].at[self.part(order, p, 1 - place.bit[k])]
            to = place.across(k)
        at = s * (place.nb + 1) + p
        return remote(src, arrive[p], self.send.at[at], self.recv.at[at], to)

    def part(self, order, p, value):
        return tuple(value if k == order[p - 1] else slice(None) for k in self.left(order, p - 1))

    def add(self, s, p):
        matrix, first, size, order, (own, *arrive), out = self.streams[s]
        place = self.place
        left = self.left(order, p)

        def one(i, carry):
            picked = {k: i // (1 << j) % 2 for j, k in enumerate(left)}
            there = (*(picked[k] for k in left), slice(None), slice(None))
            if p == 0:
                here = own[there]
            else:
                picked[order[p - 1]] = place.bit[order[p - 1]]
                before = tuple(picked[k] for k in self.left(order, p - 1))
                here = arrive[p - 1][(*before, slice(None), slice(None))]
            total = here.astype(f32) + arrive[p][there].astype(f32)
            if left:
                arrive[p][there] = total.astype(bf16)
            else:
                out[first : first + size, :] = total
            return carry

        if left:
            lax.fori_loop(0, 1 << len(left), one, 0)
        else:
            one(0, 0)

    def step(self, p):
        nb = self.place.nb
        for s in range(len(self.streams)):
            if p == 0:
                self.local(s).start()
            if p == 1:
                self.local(s).wait()
            if p:
                self.copy(s, p - 1).wait_recv()
                self.add(s, p - 1)
            if p <= nb:
                self.copy(s, p).start()
        if p == nb + 1:
            for s in range(len(self.streams)):
                for q in range(nb + 1):
                    self.copy(s, q).wait_send()

    def steps(self):
        return self.place.nb + 2


GATHER_TIMES = (0.0, 0.07, 0.25, 0.44, 0.75, 0.94)
SCATTER_TIMES = (0.0, 0.13, 0.5, 0.7, 0.88, 1.0)


def run_beside(transfer, at_step, times):
    total = pl.num_programs(0) * pl.num_programs(1)
    for p in range(1, transfer.steps()):
        when = times[min(p, len(times) - 1)]
        if when < 1.0:

            @pl.when(at_step == int(when * 64) * total // 64)
            def _():
                transfer.step(p)


def comm_params(collective_id, **more):
    return pltpu.CompilerParams(
        vmem_limit_bytes=VMEM_LIMIT, collective_id=collective_id, has_side_effects=True, **more
    )


def stream_plan(nb, widths, strip):
    first, second = (tuple(reversed(order)) for order in orders_of(nb))
    plan = []
    for m in range(len(widths)):
        plan.append((m, 0, strip // 2, first))
        plan.append((m, strip // 2, strip // 2, second))
    return plan


def build_streams(plan, matrices, arrive, outs, nb):
    streams = []
    for i, (m, first, size, order) in enumerate(plan):
        streams.append((matrices[m], first, size, order, arrive[i * (nb + 2) : (i + 1) * (nb + 2)], outs[m]))
    return streams


class Sums:
    def __init__(self, place, vec, vec_in, table, table_in, send, recv, base):
        self.place, self.base = place, base
        self.vec, self.vec_in, self.table, self.table_in = vec, vec_in, table, table_in
        self.send, self.recv = send, recv

    def pair(self, p):
        place = self.place
        to = place.across(p - 1) if p else place.sibling()
        at = self.base + 2 * p
        table = self.table.at[1 - place.t] if p == 0 else self.table.at[p + 1]
        return (
            remote(self.vec.at[p], self.vec_in.at[p], self.send.at[at], self.recv.at[at], to),
            remote(table, self.table_in.at[p], self.send.at[at + 1], self.recv.at[at + 1], to),
        )

    def step(self, p, vec_out, table_out):
        nb = self.place.nb
        if p:
            vec, table = self.pair(p - 1)
            vec.wait_recv()
            table.wait_recv()
            mine, theirs = self.vec[p - 1], self.vec_in[p - 1]
            summed = iota(mine.shape, 0) < SUM_ROWS
            total = jnp.where(summed, mine + theirs, jnp.maximum(mine, theirs))
            mine = self.table[self.place.t] if p == 1 else self.table[p]
            table_total = mine.astype(f32) + self.table_in[p - 1].astype(f32)
            if p <= nb:
                self.vec[p] = total
                self.table[p + 1] = table_total.astype(bf16)
            else:
                vec_out[...] = total
                table_out[...] = table_total
        if p <= nb:
            for copy in self.pair(p):
                copy.start()
        else:
            for q in range(nb + 1):
                for copy in self.pair(q):
                    copy.wait_send()


def body(
    inputs, cotangent, window_order, region_ids, clip_threshold, norm1_gain, norm1_shift,
    qkv_weight, qv_bias, rel_table, out_weight, out_bias, norm2_gain, norm2_shift,
    expand_weight, expand_bias, reduce_weight, reduce_bias,
):
    parts = lax.axis_size("tensor")
    groups = lax.axis_size("wide")
    mine = lax.axis_index("tensor")
    own = HEADS // parts
    oc, fc = D // parts, FF // parts
    nw = inputs.shape[0] // WIN
    strip = D // groups
    nb = bits_of(groups)
    paired = parts == 2 and groups == 1 << nb and nb > 0 and strip % 32 == 0

    order = lax.dynamic_slice_in_dim(window_order, mine * nw, nw, 0)
    region = lax.dynamic_slice_in_dim(region_ids, mine * nw * WIN, nw * WIN, 0)
    region = region.reshape(nw, WIN).astype(f32)

    def params(first):
        rows = [norm1_gain, norm1_shift, norm2_gain, norm2_shift, out_bias, reduce_bias]
        rows = jnp.pad(jnp.stack(rows + [jnp.zeros((D,), bf16)]), ((0, 0), (0, VW - D)))
        return jnp.concatenate([first[None], rows], axis=0).astype(f32)

    if paired:
        first = jnp.concatenate([qv_bias[0], jnp.zeros((oc,), bf16), qv_bias[1], expand_bias])
        weights = [params(first), padded_table(rel_table), qkv_weight]
        shards = [out_weight.T, expand_weight, reduce_weight.T]
    else:
        qkv_strip = qkv_weight.reshape(strip, own, 3, HD).transpose(0, 2, 1, 3).reshape(strip, 3 * oc)
        shard = jnp.concatenate([qkv_strip, out_weight.T, expand_weight, reduce_weight.T], axis=1)
        full = lax.all_gather(shard, BOTH, axis=0)
        full = full.reshape(groups, parts, strip, shard.shape[1]).transpose(0, 2, 1, 3)
        full = full.reshape(D, parts, shard.shape[1])
        wqkv = full[:, :, : 3 * oc].reshape(D, parts, 3, oc).transpose(0, 2, 1, 3)
        wqkv = wqkv.reshape(D, 3, 2, HALF).transpose(0, 2, 1, 3).reshape(D, 3 * D)
        wo = full[:, :, 3 * oc : 4 * oc].reshape(D, D)
        we = full[:, :, 4 * oc : 4 * oc + fc].reshape(D, FF)
        wr = full[:, :, 4 * oc + fc :].reshape(D, FF)
        small = jnp.concatenate([qv_bias.reshape(-1), expand_bias, rel_table.reshape(-1)])
        small = lax.all_gather(small, "tensor", axis=0)
        qv = small[:, : 2 * oc].reshape(parts, 2, oc).transpose(1, 0, 2).reshape(2, 2, HALF)
        be = small[:, 2 * oc : 2 * oc + fc].reshape(2, FF // 2)
        zero = jnp.zeros((HALF,), bf16)
        vecs = jnp.stack([params(jnp.concatenate([qv[0, v], zero, qv[1, v], be[v]])) for v in range(2)])
        weights = [vecs, wqkv, table_bias(small[:, 2 * oc + fc :].reshape(HEADS, RT))]
        shards = []
        nb = 0

    (xc, nrm, qkv, e, linv, att, peak, vecs, wqkv), gathered = run_attend(
        nw, nb, order, region, inputs, weights, shards
    )
    if paired:
        wo, we, wr = gathered
    layer_out, mg, gwe, gwr, gwo, feed = run_feed(nw, order, vecs, xc, att, cotangent, wo, we, wr)
    input_grad, sums, table, qkv_own, *summed = run_back(
        nw, nb, order, vecs, xc, nrm, qkv, e, linv, att, mg, wqkv, wo, feed, peak, [gwo, gwe, gwr]
    )
    if paired:
        out_own, expand_own, reduce_own = summed
        qkv_out = qkv_own
    else:
        gw = qkv_own

        def cut(grad, width):
            return grad.transpose(1, 0, 2).reshape(D, parts, width).astype(f32)

        gw = gw.reshape(2, D, 3, HALF).transpose(1, 2, 0, 3).reshape(D, 3, parts, oc)
        gw = gw.transpose(0, 2, 1, 3).reshape(D, parts, 3 * oc).astype(f32)
        grads = jnp.concatenate([gw, cut(gwo, oc), cut(gwe, fc), cut(gwr, fc)], axis=2)
        grads = grads.reshape(groups, strip, parts, 4 * oc + 2 * fc).transpose(0, 2, 1, 3)
        grads = grads.reshape(groups * parts * strip, 4 * oc + 2 * fc)
        grads = lax.psum_scatter(grads, BOTH, scatter_dimension=0, tiled=True)
        qkv_out = grads[:, : 3 * oc].reshape(strip, 3, own, HD).transpose(0, 2, 1, 3).reshape(strip, 3 * oc)
        out_own = grads[:, 3 * oc : 4 * oc]
        expand_own, reduce_own = grads[:, 4 * oc : 4 * oc + fc], grads[:, 4 * oc + fc :]
        table = lax.dynamic_slice_in_dim(lax.psum(table, BOTH), mine * own, own, 0)
        sums = jnp.concatenate(
            [lax.psum(sums[:SUM_ROWS], BOTH), lax.pmax(sums[SUM_ROWS:], BOTH)], axis=0
        )

    table_own = table[:, : 2 * WT - 1, :ROWS].reshape(own, RT)
    dbe_own = lax.dynamic_slice_in_dim(sums[6:10].reshape(FF), mine * fc, fc, 0)
    heads_grad = sums[10:13].reshape(2, 3, HALF)
    bias_grad = jnp.stack([heads_grad[:, 0].reshape(D), heads_grad[:, 2].reshape(D)], axis=0)
    bias_own = lax.dynamic_slice_in_dim(bias_grad, mine * oc, oc, 1)
    peak_own = lax.dynamic_slice_in_dim(sums[SUM_ROWS], mine * own, own, 0)
    factor = jnp.sqrt(clip_threshold / jnp.maximum(peak_own, clip_threshold))
    column_factor = jnp.stack([factor, factor, jnp.ones_like(factor)], axis=1)
    clipped_qkv = (
        qkv_weight.astype(f32).reshape(strip, own, 3, HD) * column_factor[None, :, :, None]
    ).reshape(qkv_weight.shape)
    bias_scale = jnp.stack([jnp.repeat(factor, HD), jnp.ones((own * HD,), f32)], axis=0)
    clipped_bias = qv_bias.astype(f32) * bias_scale
    return (
        layer_out,
        input_grad,
        sums[0],
        sums[1],
        qkv_out,
        bias_own,
        table_own,
        out_own.T,
        sums[5],
        sums[2],
        sums[3],
        expand_own,
        dbe_own,
        reduce_own.T,
        sums[4],
        peak_own,
        clipped_qkv,
        clipped_bias,
    )


def solution(mesh):
    tokens = P(BOTH, None)
    in_specs = (
        tokens, tokens, P("wide", None), P("wide"), P(), P(), P(), P("wide", "tensor"),
        P(None, "tensor"), P("tensor", None), P("tensor", "wide"), P(), P(), P(),
        P("wide", "tensor"), P("tensor"), P("tensor", "wide"), P(),
    )
    out_specs = (
        tokens, tokens, P(), P(), P("wide", "tensor"), P(None, "tensor"), P("tensor", None),
        P("tensor", "wide"), P(), P(), P(), P("wide", "tensor"), P("tensor"),
        P("tensor", "wide"), P(), P("tensor"), P("wide", "tensor"), P(None, "tensor"),
    )
    return jax.shard_map(body, mesh=mesh, in_specs=in_specs, out_specs=out_specs, check_vma=False)
```

```python
import functools
import math

import jax
import jax.numpy as jnp
import numpy as np
from jax import lax
from jax.experimental import pallas as pl
from jax.experimental.pallas import tpu as pltpu
from jax.sharding import PartitionSpec as P

D = 512
HEADS = 16
HD = 32
FF = 2048
WT = 8
WH = 7
WW = 7
SP = WH * WW
WIN = 392
RT = 2535
ROWS = 13 * 13
GRP = 4

epsilon = 1e-05
masked = -100.0
lowest = -1e30
LOG2E = 1.4426950408889634
SCALE = HD ** (-0.5)
WIDE_SEG = 13 * WW * WT
WIDE_PAD = 768
PITCH = 176
FLAT_PAD = 1408
UP = 256
HALF = D // 2
QW = 3 * HALF
VW = QW + FF // 2

f32 = jnp.float32
bf16 = jnp.bfloat16
NN = (((1,), (0,)), ((), ()))
NT = (((1,), (1,)), ((), ()))
TN = (((0,), (0,)), ((), ()))

VMEM_LIMIT = 62 * 2**20


def dot(a, b, dims=NN):
    return lax.dot_general(a, b, dims, preferred_element_type=f32)


def chunks(total, size):
    starts = list(range(0, total - size + 1, size))
    sizes = [size] * len(starts)
    rest = total - size * len(starts)
    if rest:
        if rest < size // 2:
            sizes[-1] += rest
        else:
            starts.append(size * len(starts))
            sizes.append(rest)
    return list(zip(starts, sizes))


ROW_CHUNKS = chunks(WIN, 64)


def iota(shape, axis):
    return lax.broadcasted_iota(jnp.int32, shape, axis)


def group_at(g):
    return pl.multiple_of(g // 2 * QW + g % 2 * (GRP * HD), GRP * HD)


def head_lanes(hh):
    return (iota((1, GRP * HD), 1) // HD == hh).astype(f32).astype(bf16)


def picks_of(order_ref, w):
    order = order_ref[pl.ds(w, 1), :]
    return iota((WIN, WIN), 0) == order % SP * WT + order // SP


def one_hot(hit):
    return hit.astype(f32).astype(bf16)


def column_moves():
    new = iota((1, QW), 1)
    old = new % HALF // HD * (3 * HD) + new // HALF * HD + new % HD
    return one_hot(iota((QW, QW), 0) == old)


def moments(rows):
    mean = jnp.mean(rows, axis=-1, keepdims=True)
    centered = rows - mean
    spread = jnp.mean(centered * centered, axis=-1, keepdims=True)
    return centered, lax.rsqrt(spread + epsilon)


def one_hot_spread():
    column = iota((1, WIDE_PAD), 1)
    dh, rest = column // (WW * WT), column % (WW * WT)
    target = rest % WT * PITCH + (12 - dh) * 13 + 6 - rest // WT
    target = jnp.where(column < WIDE_SEG, target, -1)
    return (iota((FLAT_PAD, WIDE_PAD), 0) == target).astype(f32).astype(bf16)


def spread_constant():
    column = np.arange(WIDE_PAD)
    rest = column % (WW * WT)
    target = rest % WT * PITCH + (12 - column // (WW * WT)) * 13 + 6 - rest // WT
    target = np.where(column < WIDE_SEG, target, -1)
    return jnp.asarray(np.arange(FLAT_PAD)[:, None] == target[None, :], bf16)


def flatten_table(table_ref, flat_ref):
    total = None
    rest = jnp.zeros((HEADS * WT, FLAT_PAD - UP), f32)
    for tj in range(WT):
        rows = table_ref[:, WT - 1 - tj : 2 * WT - 1 - tj, :].reshape(HEADS * WT, UP)
        part = jnp.concatenate([rows, rest], axis=1)
        if tj:
            part = pltpu.roll(part, tj * PITCH, 1)
        total = part if total is None else total + part
    flat_ref[...] = total


def turn_table(flat_ref, wide_ref, out_ref):
    flat = flat_ref[...]
    for wi in range(WW):
        wide_ref[wi] = (pltpu.roll(flat, FLAT_PAD - wi, 1) if wi else flat).astype(bf16)
    out_ref[...] = dot(wide_ref[...].reshape(WW * HEADS * WT, FLAT_PAD), one_hot_spread()) * LOG2E


def spread_table(turned_ref, bias_ref):
    for wi in range(WW):
        for hi in range(WH):
            at = (hi * WW + wi) * WT
            off = (WH - 1 - hi) * WW * WT
            rows = turned_ref[wi * HEADS * WT : (wi + 1) * HEADS * WT, off : off + WIN]
            bias_ref[:, at : at + WT, :] = rows.reshape(HEADS, WT, WIN)


def table_kernel(table_ref, bias_ref, flat_ref, wide_ref, turned_ref):
    flatten_table(table_ref, flat_ref)
    turn_table(flat_ref, wide_ref, turned_ref)
    spread_table(turned_ref, bias_ref)


TABLE_SCRATCH = [
    pltpu.VMEM((HEADS * WT, FLAT_PAD), f32),
    pltpu.VMEM((WW, HEADS * WT, FLAT_PAD), bf16),
    pltpu.VMEM((WW * HEADS * WT, WIDE_PAD), f32),
]


def padded_table(table):
    parts = table.astype(f32).reshape(-1, 2 * WT - 1, ROWS)
    return jnp.pad(parts, ((0, 0), (0, 1), (0, UP - ROWS)))


def table_bias(table):
    return pl.pallas_call(
        table_kernel,
        out_shape=jax.ShapeDtypeStruct((HEADS, WIN, WIN), f32),
        scratch_shapes=TABLE_SCRATCH,
        compiler_params=pltpu.CompilerParams(vmem_limit_bytes=VMEM_LIMIT),
        name="table_bias",
    )(padded_table(table))


def fold_table(table_scr, seg_scr, wide_scr, spread_ref, out_ref):
    seg_scr[...] = jnp.zeros_like(seg_scr)
    for wi in range(WW):
        total = None
        for hi in range(WH):
            at = (hi * WW + wi) * WT
            off = (WH - 1 - hi) * WW * WT
            seg_scr[:, 0:WIN] = table_scr[:, at : at + WT, :].reshape(HEADS * WT, WIN)
            moved = seg_scr[...]
            if off:
                moved = pltpu.roll(moved, off, 1)
            total = moved if total is None else total + moved
        wide_scr[wi] = total.astype(bf16)
    flat = dot(wide_scr[...].reshape(WW * HEADS * WT, WIDE_PAD), spread_ref[...], NT)
    total = None
    for wi in range(WW):
        part = flat[wi * HEADS * WT : (wi + 1) * HEADS * WT, :]
        part = pltpu.roll(part, wi, 1) if wi else part
        total = part if total is None else total + part
    out_ref[...] = jnp.zeros_like(out_ref)
    for tj in range(WT):
        rows = pltpu.roll(total, FLAT_PAD - tj * PITCH, 1) if tj else total
        out_ref[:, WT - 1 - tj : 2 * WT - 1 - tj, :] += rows[:, :UP].reshape(HEADS, WT, UP)


def attend_kernel(nw, nb, order_ref, region_ref, x_ref, *rest):
    if nb:
        (params_ref, table_ref, own_ref), shards, rest = rest[:3], rest[3:6], rest[6:]
    else:
        (vecs_ref, w_ref, bias_ref), rest = rest[:3], rest[3:]
    (xc_ref, nrm_ref, qkv_ref, e_ref, linv_ref, att_ref, peak_ref), rest = rest[:7], rest[7:]
    if nb:
        (vecs_out, w_out), bufs, rest = rest[:2], rest[2:5], rest[5:]
    (x_scr, mask_scr, hm_ref, xc_scr, nrm_scr), rest = rest[:5], rest[5:]
    w, g = pl.program_id(0), pl.program_id(1)
    at_step = w * (HEADS // GRP) + g
    opening = (w == 0) & (g == 0)
    if nb:
        (vecs_ref, w_scr, bias_ref, own_scr, tables, flat_ref, wide_ref, turned_ref), sems = rest[:8], rest[8:]
        place = Place(nb)
        first = Gather(place, [own_scr], [w_scr], *sems[:3])
        second = Gather(place, shards[:1], bufs[:1], *sems[3:6])
        third = Gather(place, shards[1:], bufs[1:], *sems[6:])
        base = Gather.copies(nb, 1)
        mine = pl.ds(pl.multiple_of(place.t * (HEADS // 2), HEADS // 2), HEADS // 2)
        near = [
            remote(part, part, sems[0].at[base + i], sems[1].at[base + i], place.sibling())
            for i, part in enumerate((tables.at[mine], vecs_ref.at[place.t]))
        ]

    def prepare(i):
        pick = picks_of(order_ref, i)
        region = region_ref[pl.ds(i, 1), :]
        row_at = jnp.sum(jnp.where(pick, region, 0.0), axis=1, keepdims=True)
        pick = one_hot(pick)
        column_at = dot(jnp.broadcast_to(region, (8, WIN)).astype(bf16), pick, NT)[0:1, :]
        mask_scr[i] = jnp.where(row_at == column_at, 0.0, masked * LOG2E)
        xc_scr[i] = dot(pick, x_ref[i]).astype(bf16)
        for at, size in ROW_CHUNKS:
            centered, rstd = moments(xc_scr[i, at : at + size, :].astype(f32))
            nrm_scr[i, at : at + size, :] = (
                centered * rstd * vecs_ref[0, 1:2, 0:D] + vecs_ref[0, 2:3, 0:D]
            ).astype(bf16)

    def project():
        xc_ref[...] = xc_scr[w]
        nrm_ref[...] = nrm_scr[w]
        weight = w_scr[...].reshape(D, 3 * D) if nb else w_ref
        for v in range(2):
            cols = slice(v * QW, (v + 1) * QW)
            qkv_ref[:, cols] = (dot(nrm_ref[...], weight[:, cols]) + vecs_ref[v, 0:1, 0:QW]).astype(bf16)

    def group():
        off = pl.multiple_of(g * (GRP * HD), GRP * HD)
        qoff = group_at(g)
        qg = qkv_ref[:, pl.ds(qoff, GRP * HD)]
        kg = qkv_ref[:, pl.ds(qoff + HALF, GRP * HD)]
        vg = qkv_ref[:, pl.ds(qoff + 2 * HALF, GRP * HD)]
        vx = jnp.concatenate([vg, jnp.ones((WIN, GRP * HD), bf16)], axis=1)

        def score(hh):
            x_scr[hh % 2] = dot(qg * head_lanes(hh), kg, NT)

        def soften(hh):
            h = g * GRP + hh
            top = hm_ref[h]
            for at, size in ROW_CHUNKS:
                xx = x_scr[hh % 2, at : at + size, :]
                top = jnp.maximum(top, jnp.max(xx.reshape(size // 8, 8, WIN), axis=0))
                s = xx * (SCALE * LOG2E) + bias_ref[h, at : at + size, :] + mask_scr[w, at : at + size, :]
                e_ref[0, hh, at : at + size, :] = jnp.exp2(s - jnp.max(s, axis=1, keepdims=True)).astype(bf16)
            hm_ref[h] = top

        def weigh(hh, total, scale):
            out = dot(e_ref[0, hh], vx)
            inv = 1.0 / out[:, GRP * HD :]
            out = out[:, : GRP * HD] * inv
            if hh == 0:
                return out, inv
            here = iota((WIN, GRP * HD), 1) // HD == hh
            return jnp.where(here, out, total), jnp.where(here, inv, scale)

        total = scale = None
        score(0)
        for hh in range(GRP):
            if hh + 1 < GRP:
                score(hh + 1)
            soften(hh)
            if hh:
                total, scale = weigh(hh - 1, total, scale)
        total, scale = weigh(GRP - 1, total, scale)
        att_ref[:, pl.ds(off, GRP * HD)] = total.astype(bf16)
        linv_ref[:, pl.ds(off, GRP * HD)] = scale

    @pl.when(opening)
    def _():
        hm_ref[...] = jnp.full(hm_ref.shape, lowest, f32)
        windows = list(range(nw))

        def some(count):
            for i in windows[:count]:
                prepare(i)
            del windows[:count]

        if nb:
            place.greet()
            own_scr[...] = dot(own_ref[...], column_moves()).astype(bf16)
            first.step(0)
            tables[mine] = table_ref[...]
            vecs_ref[place.t] = params_ref[...]
            for copy in near:
                copy.start()
            for copy in near:
                copy.wait()
            flatten_table(tables, flat_ref)
            first.step(1)
            some(1)
            first.step(2)
            second.step(0)
            turn_table(flat_ref, wide_ref, turned_ref)
            first.step(3)
            second.step(1)
            spread_table(turned_ref, bias_ref)
            some(1)
            first.step(4)
            second.step(2)
            third.step(0)
            some(nw)
            for p in range(5, first.steps()):
                first.step(p)
            w_out[...] = w_scr[...].reshape(D, 3 * D)
            vecs_out[...] = vecs_ref[...]
        some(nw)

    if nb:
        run_beside(second, at_step, GATHER_TIMES, 3)
        run_beside(third, at_step, LATER_TIMES, 1)

    @pl.when(g == 0)
    def _():
        project()

    group()

    @pl.when(at_step == pl.num_programs(0) * pl.num_programs(1) - 1)
    def _():
        lane = iota((1, D), 1)
        peaks = jnp.full((1, D), lowest, f32)
        for h in range(HEADS):
            top = jnp.max(jnp.max(hm_ref[h], axis=0, keepdims=True), axis=1, keepdims=True)
            peaks = jnp.where(lane == h, top * SCALE, peaks)
        peak_ref[...] = jnp.broadcast_to(peaks, peak_ref.shape)


def gelu_both(hidden):
    z = jnp.abs(hidden) * (0.5**0.5)
    base = 1.0 + 0.3275911 * z
    t = pl.reciprocal(base, approx=True)
    t = t * (2.0 - base * t)
    poly = 1.061405429
    for coefficient in (-1.453152027, 1.421413741, -0.284496736, 0.254829592):
        poly = poly * t + coefficient
    bell = jnp.exp2(hidden * hidden * (-0.5 * LOG2E))
    tail = 0.5 * poly * t * bell
    cdf = jnp.where(hidden >= 0.0, 1.0 - tail, tail)
    return hidden * cdf, cdf + hidden * bell * (1.0 / math.sqrt(2.0 * math.pi))


FC = 256
FEED_CHUNKS = chunks(WIN, 32)


def feed_kernel(
    order_ref, vecs_ref, xc_ref, att_ref, cot_ref, wo_ref, we_ref, wr_ref,
    out_ref, mgrad_ref, gwe_ref, gwr_ref, gwo_ref, vec_ref,
    mid_ref, n2_ref, cc_scr, cT_scr, nT_scr, acc_scr, ng_scr, dwe_ref, dwr_ref, dwo_ref,
    hid_scr, ag_scr, act_scr, hg_scr,
):
    w = pl.program_id(0)

    @pl.when(w == 0)
    def _():
        dwe_ref[...] = jnp.zeros_like(dwe_ref)
        dwr_ref[...] = jnp.zeros_like(dwr_ref)
        dwo_ref[...] = jnp.zeros_like(dwo_ref)
        vec_ref[...] = jnp.zeros_like(vec_ref)

    g2, s2, bo, br = (vecs_ref[0, i : i + 1, 0:D] for i in (3, 4, 5, 6))
    pick = one_hot(picks_of(order_ref, w))
    mid_ref[...] = xc_ref[...].astype(f32) + (dot(att_ref[...], wo_ref[...], NT) + bo)
    for at, size in ROW_CHUNKS:
        centered, rstd = moments(mid_ref[at : at + size, :])
        n2_ref[at : at + size, :] = (centered * rstd * g2 + s2).astype(bf16)
    canon = dot(pick, cot_ref[...])
    cc_scr[...] = canon.astype(bf16)
    cT_scr[...] = cc_scr[...].T
    nT_scr[...] = n2_ref[...].T

    blocks = [slice(c * FC, (c + 1) * FC) for c in range(FF // FC)]

    def widen(c):
        hid_scr[c % 2] = dot(n2_ref[...], we_ref[:, blocks[c]])
        ag_scr[c % 2] = dot(cc_scr[...], wr_ref[:, blocks[c]])

    def bend(c):
        half, off = divmod(c * FC, FF // 2)
        shift = vecs_ref[half, 0:1, QW + off : QW + off + FC]
        total = jnp.zeros((8, FC), f32)
        for at, size in FEED_CHUNKS:
            rows = slice(at, at + size)
            act, slope = gelu_both(hid_scr[c % 2, rows, :] + shift)
            act_scr[rows, blocks[c]] = act.astype(bf16)
            hg = (ag_scr[c % 2, rows, :] * slope).astype(bf16)
            hg_scr[rows, blocks[c]] = hg
            total += jnp.sum(hg.astype(f32).reshape(size // 8, 8, FC), axis=0)
        line, off = divmod(c * FC, D)
        vec_ref[4 + line : 5 + line, off : off + FC] += jnp.sum(total, axis=0, keepdims=True)

    def gather_up(c):
        dwr_ref[:, blocks[c]] += dot(cT_scr[...], act_scr[:, blocks[c]])
        dwe_ref[:, blocks[c]] += dot(nT_scr[...], hg_scr[:, blocks[c]])

    widen(0)
    for c in range(FF // FC):
        if c + 1 < FF // FC:
            widen(c + 1)
        bend(c)
        if c:
            gather_up(c - 1)
    gather_up(FF // FC - 1)
    acc_scr[...] = dot(act_scr[...], wr_ref[...], NT)
    ng_scr[...] = dot(hg_scr[...], we_ref[...], NT)
    for at, size in ROW_CHUNKS:
        rows = slice(at, at + size)
        mid = mid_ref[rows, :]
        cot = cc_scr[rows, :].astype(f32)
        acc_scr[rows, :] = mid + (acc_scr[rows, :] + br)
        back = ng_scr[rows, :]
        centered, rstd = moments(mid)
        xhat = centered * rstd
        g = back * g2
        mg = cot + rstd * (
            g - jnp.mean(g, axis=-1, keepdims=True) - xhat * jnp.mean(g * xhat, axis=-1, keepdims=True)
        )
        mgrad_ref[rows, :] = mg
        vec_ref[0:1, :] += jnp.sum(back * xhat, axis=0, keepdims=True)
        vec_ref[1:2, :] += jnp.sum(back, axis=0, keepdims=True)
        vec_ref[2:3, :] += jnp.sum(cot, axis=0, keepdims=True)
        vec_ref[3:4, :] += jnp.sum(mg.astype(bf16).astype(f32), axis=0, keepdims=True)
    out_ref[...] = dot(pick, acc_scr[...].astype(bf16), TN).astype(bf16)
    cT_scr[...] = mgrad_ref[...].astype(bf16).T
    dwo_ref[...] += dot(cT_scr[...], att_ref[...])

    @pl.when(w == pl.num_programs(0) - 1)
    def _():
        for grad, acc, width in ((gwe_ref, dwe_ref, FF // 2), (gwr_ref, dwr_ref, FF // 2), (gwo_ref, dwo_ref, HALF)):
            for v in range(2):
                for at in range(0, D, 64):
                    grad[v, at : at + 64, :] = acc[at : at + 64, v * width : (v + 1) * width].astype(bf16)


def back_kernel(
    nb, plans, order_ref, vecs_ref, xc_ref, nrm_ref, qkv_ref, e_ref, linv_ref, att_ref, mg_ref, w_ref, wo_ref,
    feed_ref, peak_ref, spread_ref, *rest
):
    if nb:
        matrices, rest = rest[:3], rest[3:]
        (out_ref, late_out, table_out, qkv_out, early_out), outs, rest = rest[:5], rest[5:8], rest[8:]
    else:
        (out_ref, acc, table_out, gw_ref), rest = rest[:4], rest[4:]
    (
        dw_ref, wide_scr, ag_scr, dop_scr, doT_scr, qT_scr, in_scr, x_scr, ds_scr, pg_scr, dvT_scr, dkT_scr,
        table_scr, seg_scr, grad_scr,
    ), rest = rest[:15], rest[15:]
    w, g = pl.program_id(0), pl.program_id(1)
    end = HEADS // GRP - 1
    at_step = w * (HEADS // GRP) + g
    closing = at_step == pl.num_programs(0) * pl.num_programs(1) - 1
    if nb:
        (gw_ref, fold_scr, own_out, vec, vec_in, table, table_in, vec0, vec0_in), rest = rest[:9], rest[9:]
        acc = vec.at[0]
        place = Place(nb)
        count = [len(plan) * (nb + 2) for plan in plans]
        early, rest = rest[: count[0]], rest[count[0] :]
        late, sems = rest[: count[1]], rest[count[1] :]
        first = Scatter(place, build_streams(plans[0], matrices, early, outs, nb), *sems[:3])
        second = Scatter(place, build_streams(plans[1], [gw_ref], late, [own_out], nb), *sems[3:])
        sums = Sums(place, vec, vec_in, table, table_in, sems[3], sems[4], len(plans[1]) * (nb + 1))
        known = Sums(place, vec0, vec0_in, None, None, sems[0], sems[1], len(plans[0]) * (nb + 1))

    def prepare():
        ag_scr[...] = mg_ref[...].astype(bf16)
        scaled = dot(ag_scr[...], wo_ref[...]).astype(bf16).astype(f32) * linv_ref[...]
        dop_scr[...] = scaled.astype(bf16)
        in_scr[...] = (dop_scr[...].astype(f32) * -att_ref[...].astype(f32)).astype(bf16)
        doT_scr[...] = dop_scr[...].T
        for v in range(2):
            qT_scr[v * HALF : (v + 1) * HALF, :] = qkv_ref[:, v * QW : v * QW + HALF].T

    def group():
        off = pl.multiple_of(g * (GRP * HD), GRP * HD)
        qoff = group_at(g)
        kg = qkv_ref[:, pl.ds(qoff + HALF, GRP * HD)]
        vg = qkv_ref[:, pl.ds(qoff + 2 * HALF, GRP * HD)]
        vx = jnp.concatenate([vg, jnp.ones((WIN, GRP * HD), bf16)], axis=1)
        dx = jnp.concatenate([dop_scr[:, pl.ds(off, GRP * HD)], in_scr[:, pl.ds(off, GRP * HD)]], axis=1)

        def score(hh):
            lanes = head_lanes(hh)
            x_scr[hh % 2] = dot(dx * jnp.concatenate([lanes, lanes], axis=1), vx, NT)

        def differ(hh):
            h = g * GRP + hh
            for at, size in ROW_CHUNKS:
                rows = slice(at, at + size)
                ds = (e_ref[0, hh, rows, :].astype(f32) * x_scr[hh % 2, rows, :]).astype(bf16)
                ds_scr[hh % 2, rows, :] = ds
                table_scr[h, rows, :] += ds.astype(f32)

        def spread(hh, total):
            hrow = pl.ds(pl.multiple_of(off + hh * HD, HD), HD)
            ds = ds_scr[hh % 2]
            dvT_scr[hrow, :] = dot(doT_scr[hrow, :], e_ref[0, hh]).astype(bf16)
            dkT_scr[hrow, :] = (dot(qT_scr[hrow, :], ds) * SCALE).astype(bf16)
            part = dot(ds, kg * head_lanes(hh))
            return part if total is None else total + part

        total = None
        score(0)
        for hh in range(GRP):
            if hh + 1 < GRP:
                score(hh + 1)
            differ(hh)
            if hh:
                total = spread(hh - 1, total)
        total = spread(GRP - 1, total)
        pg_scr[:, pl.ds(qoff, GRP * HD)] = (total * SCALE).astype(bf16)

    def collect():
        for v in range(2):
            heads = slice(v * HALF, (v + 1) * HALF)
            pg_scr[:, v * QW + HALF : v * QW + 2 * HALF] = dkT_scr[heads, :].T
            pg_scr[:, v * QW + 2 * HALF : (v + 1) * QW] = dvT_scr[heads, :].T
        nT = nrm_ref[...].T
        for part in range(3):
            cols = slice(part * D, (part + 1) * D)
            dw_ref[:, cols] += dot(nT, pg_scr[:, cols])
            acc[2 + part : 3 + part, :] += jnp.sum(pg_scr[:, cols].astype(f32), axis=0, keepdims=True)

    def finish():
        grad_scr[...] = dot(pg_scr[...], w_ref[...], NT)
        for at, size in ROW_CHUNKS:
            rows = slice(at, at + size)
            back = grad_scr[rows, :]
            centered, rstd = moments(xc_ref[rows, :].astype(f32))
            xhat = centered * rstd
            g = back * vecs_ref[0, 1:2, 0:D]
            acc[0:1, :] += jnp.sum(back * xhat, axis=0, keepdims=True)
            acc[1:2, :] += jnp.sum(back, axis=0, keepdims=True)
            ag_scr[rows, :] = (
                mg_ref[rows, :]
                + rstd * (g - jnp.mean(g, axis=-1, keepdims=True) - xhat * jnp.mean(g * xhat, axis=-1, keepdims=True))
            ).astype(bf16)
        out_ref[...] = dot(one_hot(picks_of(order_ref, w)), ag_scr[...], TN).astype(bf16)

    @pl.when(at_step == 0)
    def _():
        dw_ref[...] = jnp.zeros_like(dw_ref)
        acc[...] = jnp.zeros((8, D), f32)
        table_scr[...] = jnp.zeros_like(table_scr)
        if nb:
            place.greet()
            first.step(0)

    if nb:
        run_beside(first, at_step, SCATTER_TIMES)
        for p in range(nb + 2):

            @pl.when(at_step == pl.num_programs(0) * pl.num_programs(1) * (3 + 2 * p) // (2 * nb + 8))
            def _():
                if p == 0:
                    vec0[0, 0:8, :] = feed_ref[...]
                    vec0[0, 8:16, :] = peak_ref[...]
                known.step(p, early_out)

    @pl.when(g == 0)
    def _():
        prepare()

    group()

    @pl.when(g == end)
    def _():
        collect()

    @pl.when(closing)
    def _():
        strip = D >> nb if nb else D
        for v in range(2):
            for at in range(0, D, 64):
                part = dw_ref[at : at + 64, v * QW : (v + 1) * QW].astype(bf16)
                if nb:
                    for i in range(64 // strip):
                        bits = tuple((at // strip + i) // (1 << k) % 2 for k in reversed(range(nb)))
                        gw_ref[(v, *bits)] = part[i * strip : (i + 1) * strip, :]
                else:
                    gw_ref[v, at : at + 64, :] = part
        if nb:
            second.step(0)

    @pl.when(g == end)
    def _():
        finish()

    @pl.when(closing)
    def _():
        if not nb:
            fold_table(table_scr, seg_scr, wide_scr, spread_ref, table_out)
            return
        second.step(1)
        for p in range(1, first.steps()):
            if SCATTER_TIMES[min(p, len(SCATTER_TIMES) - 1)] >= 1.0:
                first.step(p)
        fold_table(table_scr, seg_scr, wide_scr, spread_ref, fold_scr)
        half = HEADS // 2
        for v in range(2):
            table[v] = fold_scr[v * half : (v + 1) * half].astype(bf16)
        for p in range(second.steps()):
            sums.step(p, late_out, table_out)
            if p + 2 < second.steps():
                second.step(p + 2)
        top = own_out[...].astype(bf16)
        low = (own_out[...] - top.astype(f32)).astype(bf16)
        moves = column_moves()
        qkv_out[...] = dot(top, moves, NT) + dot(low, moves, NT)


def whole(shape):
    return pl.BlockSpec(shape, lambda *at: (0,) * len(shape))


def kept(shape):
    return pl.BlockSpec(shape, lambda *at: (0,) * len(shape), pipeline_mode=pl.Buffered(1))


def per(shape):
    rest = (0,) * (len(shape) - 1)
    return pl.BlockSpec(shape, lambda w, *at: (w,) + rest)


EXPS = pl.BlockSpec((1, GRP, WIN, WIN), lambda w, g: (w, g, 0, 0))


def shape_of(shape, dtype):
    return jax.ShapeDtypeStruct(shape, dtype)


PARAMS = pltpu.CompilerParams(vmem_limit_bytes=VMEM_LIMIT)
ANY = pl.BlockSpec(memory_space=pl.ANY)


def dma(*counts):
    return [pltpu.SemaphoreType.DMA((n,)) for n in counts]


def run_attend(nw, nb, order, region, x, weights, shards):
    rows = nw * WIN
    tok = per((WIN, D))
    out_specs = [tok, tok, per((WIN, 3 * D)), EXPS, tok, tok, whole((8, D))]
    out_shape = [
        shape_of((rows, D), bf16),
        shape_of((rows, D), bf16),
        shape_of((rows, 3 * D), bf16),
        shape_of((nw, HEADS, WIN, WIN), bf16),
        shape_of((rows, D), f32),
        shape_of((rows, D), bf16),
        shape_of((8, D), f32),
    ]
    scratch = [
        pltpu.VMEM((2, WIN, WIN), f32),
        pltpu.VMEM((nw, WIN, WIN), f32),
        pltpu.VMEM((HEADS, 8, WIN), f32),
        pltpu.VMEM((nw, WIN, D), bf16),
        pltpu.VMEM((nw, WIN, D), bf16),
    ]
    if nb:
        strip = D >> nb
        copies, one, more = Gather.copies(nb, 1) + 2, Gather.copies(nb, 1), Gather.copies(nb, len(shards) - 1)
        out_specs += [whole((2, 8, VW)), whole((D, 3 * D)), *[ANY] * len(shards)]
        out_shape += [shape_of((2, 8, VW), f32), shape_of((D, 3 * D), bf16)]
        out_shape += [shape_of((2,) * nb + (strip, 2 * v.shape[1]), bf16) for v in shards]
        scratch += [
            pltpu.VMEM((2, 8, VW), f32),
            pltpu.VMEM((2,) * nb + (strip, 3 * D), bf16),
            pltpu.VMEM((HEADS, WIN, WIN), f32),
            pltpu.VMEM((strip, QW), bf16),
            pltpu.VMEM((HEADS, 2 * WT, UP), f32),
            *TABLE_SCRATCH,
            *dma(copies, copies, 1, one, one, 1, more, more, len(shards) - 1),
        ]
    out = pl.pallas_call(
        functools.partial(attend_kernel, nw, nb),
        grid=(nw, HEADS // GRP),
        in_specs=[
            kept((nw, WIN)), kept((nw, WIN)), kept((nw, WIN, D)), *(kept(v.shape) for v in weights), *[ANY] * len(shards),
        ],
        out_specs=out_specs,
        out_shape=out_shape,
        scratch_shapes=scratch,
        compiler_params=comm_params(2) if nb else PARAMS,
        name="attend",
    )(order, region, x.reshape(nw, WIN, D), *weights, *shards)
    if nb:
        return out[:9], [v.reshape(D, v.shape[-1]) for v in out[9:]]
    return (*out, weights[0], weights[1]), []


def run_feed(nw, order, vecs, xc, att, cot, wo, we, wr):
    rows = nw * WIN
    tok = per((WIN, D))
    return pl.pallas_call(
        feed_kernel,
        grid=(nw,),
        in_specs=[
            kept((nw, WIN)), kept((2, 8, VW)), tok, tok, tok, kept((D, D)), kept((D, FF)), kept((D, FF)),
        ],
        out_specs=[
            tok, tok, whole((2, D, FF // 2)), whole((2, D, FF // 2)), whole((2, D, HALF)), whole((8, D)),
        ],
        out_shape=[
            shape_of((rows, D), bf16),
            shape_of((rows, D), f32),
            shape_of((2, D, FF // 2), bf16),
            shape_of((2, D, FF // 2), bf16),
            shape_of((2, D, HALF), bf16),
            shape_of((8, D), f32),
        ],
        scratch_shapes=[
            pltpu.VMEM((WIN, D), f32),
            pltpu.VMEM((WIN, D), bf16),
            pltpu.VMEM((WIN, D), bf16),
            pltpu.VMEM((D, WIN), bf16),
            pltpu.VMEM((D, WIN), bf16),
            pltpu.VMEM((WIN, D), f32),
            pltpu.VMEM((WIN, D), f32),
            pltpu.VMEM((D, FF), f32),
            pltpu.VMEM((D, FF), f32),
            pltpu.VMEM((D, D), f32),
            pltpu.VMEM((2, WIN, FC), f32),
            pltpu.VMEM((2, WIN, FC), f32),
            pltpu.VMEM((WIN, FF), bf16),
            pltpu.VMEM((WIN, FF), bf16),
        ],
        compiler_params=PARAMS,
        name="feed",
    )(order, vecs, xc, att, cot, wo, we, wr)


def run_back(nw, nb, order, vecs, xc, nrm, qkv, e, linv, att, mg, w, wo, feed, peak, grads):
    rows = nw * WIN
    tok = per((WIN, D))
    folded = (HEADS, 2 * WT, UP)
    half = (HEADS // 2, 2 * WT, UP)
    scratch = [
        pltpu.VMEM((D, 3 * D), f32),
        pltpu.VMEM((WW, HEADS * WT, WIDE_PAD), bf16),
        pltpu.VMEM((WIN, D), bf16),
        pltpu.VMEM((WIN, D), bf16),
        pltpu.VMEM((D, WIN), bf16),
        pltpu.VMEM((D, WIN), bf16),
        pltpu.VMEM((WIN, D), bf16),
        pltpu.VMEM((2, WIN, WIN), f32),
        pltpu.VMEM((2, WIN, WIN), bf16),
        pltpu.VMEM((WIN, 3 * D), bf16),
        pltpu.VMEM((D, WIN), bf16),
        pltpu.VMEM((D, WIN), bf16),
        pltpu.VMEM((HEADS, WIN, WIN), f32),
        pltpu.VMEM((HEADS * WT, WIDE_PAD), f32),
        pltpu.VMEM((WIN, D), f32),
    ]
    out_specs = [tok, whole((8, D))]
    out_shape = [shape_of((rows, D), bf16), shape_of((8, D), f32)]
    plans = []
    if nb:
        strip = D >> nb
        widths = [v.shape[2] for v in grads]
        plans = [stream_plan(nb, widths), stream_plan(nb, [QW])]
        copies = [len(plan) * (nb + 1) for plan in plans]
        more = copies[1] + 2 * (nb + 1)
        out_specs += [whole(half), whole((strip, QW)), whole((16, D))]
        out_specs += [whole((strip, width)) for width in widths]
        out_shape += [shape_of(half, f32), shape_of((strip, QW), f32), shape_of((16, D), f32)]
        out_shape += [shape_of((strip, width), f32) for width in widths]
        scratch += [
            pltpu.VMEM((2,) * (nb + 1) + (strip, QW), bf16),
            pltpu.VMEM(folded, f32),
            pltpu.VMEM((strip, QW), f32),
            pltpu.VMEM((nb + 1, 8, D), f32),
            pltpu.VMEM((nb + 1, 8, D), f32),
            pltpu.VMEM((nb + 2, *half), bf16),
            pltpu.VMEM((nb + 1, *half), bf16),
            *[pltpu.VMEM((nb + 1, 16, D), f32)] * 2,
        ]
        for plan in plans:
            for _, _, size, _ in plan:
                scratch += Scatter.arrivals(nb, strip, size)
        some = copies[0] + 2 * (nb + 1)
        scratch += dma(some, some, len(plans[0]), more, more, len(plans[1]))
        grads = [v.reshape((2,) * (nb + 1) + (strip, v.shape[2])) for v in grads]
    else:
        grads = []
        out_specs += [whole(folded), whole((2, D, QW))]
        out_shape += [shape_of(folded, f32), shape_of((2, D, QW), bf16)]
    return pl.pallas_call(
        functools.partial(back_kernel, nb, plans),
        grid=(nw, HEADS // GRP),
        in_specs=[
            kept((nw, WIN)), kept((2, 8, VW)), tok, tok, per((WIN, 3 * D)), EXPS, tok, tok, tok,
            kept((D, 3 * D)), kept((D, D)), kept((8, D)), kept((8, D)), kept((FLAT_PAD, WIDE_PAD)),
            *[ANY] * len(grads),
        ],
        out_specs=out_specs,
        out_shape=out_shape,
        scratch_shapes=scratch,
        compiler_params=comm_params(3) if nb else PARAMS,
        name="attend_back",
    )(order, vecs, xc, nrm, qkv, e, linv, att, mg, w, wo, feed, peak, spread_constant(), *grads)


BOTH = ("wide", "tensor")
MESH = pl.DeviceIdType.MESH


def bits_of(groups):
    return groups.bit_length() - 1


def orders_of(nb):
    down = tuple(reversed(range(nb)))
    if nb < 2:
        return (down,)
    half = nb // 2
    swapped = down[:-2] + (down[-1], down[-2])
    return (down, swapped, tuple(range(half)) + tuple(reversed(range(half, nb))))


def cuts_of(width, count):
    tiles = width // 128
    sizes = [(tiles + count - 1 - i) // count for i in range(count)]
    cuts, at = [], 0
    for size in sizes:
        if size:
            cuts.append((at * 128, size * 128))
            at += size
    return cuts


class Place:
    def __init__(self, nb):
        self.nb = nb
        self.w = lax.axis_index("wide")
        self.t = lax.axis_index("tensor")
        self.bit = [self.w // (1 << k) % 2 for k in range(nb)]

    def across(self, k):
        return (self.w + (1 - 2 * self.bit[k]) * (1 << k), self.t)

    def sibling(self):
        return (self.w, 1 - self.t)

    def greet(self):
        barrier = pltpu.get_barrier_semaphore()
        partners = [self.across(k) for k in range(self.nb)] + [self.sibling()]
        for partner in partners:
            pl.semaphore_signal(barrier, inc=1, device_id=partner, device_id_type=MESH)
        pl.semaphore_wait(barrier, len(partners))

    def index(self, chosen):
        return tuple(chosen.get(k, slice(None)) for k in reversed(range(self.nb)))


def remote(src, dst, send, recv, to):
    return pltpu.make_async_remote_copy(
        src_ref=src, dst_ref=dst, send_sem=send, recv_sem=recv, device_id=to, device_id_type=MESH
    )


class Gather:
    def __init__(self, place, owns, bufs, send, recv, near):
        self.place, self.owns, self.bufs = place, owns, bufs
        self.send, self.recv, self.near = send, recv, near
        nb = place.nb
        self.streams = []
        orders = orders_of(nb)
        for own, buf in zip(owns, bufs):
            for (first, size), order in zip(cuts_of(own.shape[1], len(orders)), orders):
                self.streams.append((own, buf, first, size, order))

    @staticmethod
    def copies(nb, count):
        return count * (len(orders_of(nb)) * nb + 1)

    def lanes(self, own):
        width = own.shape[1]
        return pl.ds(pl.multiple_of(self.place.t * width, 128), width)

    def local(self, b):
        own, buf = self.owns[b], self.bufs[b]
        mine = self.place.index(dict(enumerate(self.place.bit)))
        return pltpu.make_async_copy(own, buf.at[(*mine, slice(None), self.lanes(own))], self.near.at[b])

    def wide(self, s, p):
        own, buf, first, size, order = self.streams[s]
        place = self.place
        chosen = {k: place.bit[k] for k in order[p:]}
        lanes = pl.ds(pl.multiple_of(place.t * own.shape[1] + first, 128), size)
        region = buf.at[(*place.index(chosen), slice(None), lanes)]
        src = region if p else own.at[:, pl.ds(first, size)]
        at = s * place.nb + p
        return remote(src, region, self.send.at[at], self.recv.at[at], place.across(order[p]))

    def core(self, b):
        own, buf = self.owns[b], self.bufs[b]
        region = buf.at[(*self.place.index({}), slice(None), self.lanes(own))]
        at = len(self.streams) * self.place.nb + b
        return remote(region, region, self.send.at[at], self.recv.at[at], self.place.sibling())

    def step(self, p):
        nb = self.place.nb
        streams, count = range(len(self.streams)), range(len(self.bufs))
        if p == 0:
            for b in count:
                self.local(b).start()
        elif p == 1:
            for b in count:
                self.local(b).wait()
        if 0 < p <= nb:
            for s in streams:
                self.wide(s, p - 1).wait_recv()
        if p < nb:
            for s in streams:
                self.wide(s, p).start()
        elif p == nb:
            for b in count:
                self.core(b).start()
        else:
            for s in streams:
                for q in range(nb):
                    self.wide(s, q).wait_send()
            for b in count:
                self.core(b).wait()

    def steps(self):
        return self.place.nb + 2


class Scatter:
    def __init__(self, place, streams, send, recv, near):
        self.place, self.streams = place, streams
        self.send, self.recv, self.near = send, recv, near

    @staticmethod
    def arrivals(nb, rows, width):
        return [pltpu.VMEM((2,) * (nb - max(p, 0)) + (rows, width), bf16) for p in range(-1, nb + 1)]

    def local(self, s):
        matrix, first, size, order, (own, *arrive), out = self.streams[s]
        src = matrix.at[(self.place.t, *self.place.index({}), slice(None), pl.ds(first, size))]
        return pltpu.make_async_copy(src, own, self.near.at[s])

    def left(self, order, p):
        return [k for k in reversed(range(self.place.nb)) if k not in order[:p]]

    def copy(self, s, p):
        matrix, first, size, order, (own, *arrive), out = self.streams[s]
        place = self.place
        if p == 0:
            src, to = matrix.at[(1 - place.t, *place.index({}), slice(None), pl.ds(first, size))], place.sibling()
        else:
            k = order[p - 1]
            src = arrive[p - 1].at[self.part(order, p, 1 - place.bit[k])]
            to = place.across(k)
        at = s * (place.nb + 1) + p
        return remote(src, arrive[p], self.send.at[at], self.recv.at[at], to)

    def part(self, order, p, value):
        return tuple(value if k == order[p - 1] else slice(None) for k in self.left(order, p - 1))

    def add(self, s, p):
        matrix, first, size, order, (own, *arrive), out = self.streams[s]
        place = self.place
        left = self.left(order, p)

        def one(i, carry):
            picked = {k: i // (1 << j) % 2 for j, k in enumerate(left)}
            there = (*(picked[k] for k in left), slice(None), slice(None))
            if p == 0:
                here = own[there]
            else:
                picked[order[p - 1]] = place.bit[order[p - 1]]
                before = tuple(picked[k] for k in self.left(order, p - 1))
                here = arrive[p - 1][(*before, slice(None), slice(None))]
            total = here.astype(f32) + arrive[p][there].astype(f32)
            if left:
                arrive[p][there] = total.astype(bf16)
            else:
                out[:, first : first + size] = total
            return carry

        if left:
            lax.fori_loop(0, 1 << len(left), one, 0)
        else:
            one(0, 0)

    def step(self, p):
        nb = self.place.nb
        for s in range(len(self.streams)):
            if p == 0:
                self.local(s).start()
            if p == 1:
                self.local(s).wait()
            if p:
                self.copy(s, p - 1).wait_recv()
                self.add(s, p - 1)
            if p <= nb:
                self.copy(s, p).start()
        if p == nb + 1:
            for s in range(len(self.streams)):
                for q in range(nb + 1):
                    self.copy(s, q).wait_send()

    def steps(self):
        return self.place.nb + 2


GATHER_TIMES = (0.0, 0.0, 0.0, 0.2, 0.5, 0.94)
LATER_TIMES = (0.0, 0.2, 0.38, 0.57, 0.82, 0.94)
SCATTER_TIMES = (0.0, 0.13, 0.44, 0.63, 0.82, 1.0)


def run_beside(transfer, at_step, times, start=1):
    total = pl.num_programs(0) * pl.num_programs(1)
    for p in range(start, transfer.steps()):
        when = times[min(p, len(times) - 1)]
        if when < 1.0:

            @pl.when(at_step == int(when * 64) * total // 64)
            def _():
                transfer.step(p)


def comm_params(collective_id, **more):
    return pltpu.CompilerParams(
        vmem_limit_bytes=VMEM_LIMIT, collective_id=collective_id, has_side_effects=True, **more
    )


def stream_plan(nb, widths):
    orders = [tuple(reversed(order)) for order in orders_of(nb)]
    plan = []
    for m, width in enumerate(widths):
        for (first, size), order in zip(cuts_of(width, len(orders)), orders):
            plan.append((m, first, size, order))
    return plan


def build_streams(plan, matrices, arrive, outs, nb):
    streams = []
    for i, (m, first, size, order) in enumerate(plan):
        streams.append((matrices[m], first, size, order, arrive[i * (nb + 2) : (i + 1) * (nb + 2)], outs[m]))
    return streams


class Sums:
    def __init__(self, place, vec, vec_in, table, table_in, send, recv, base):
        self.place, self.base = place, base
        self.vec, self.vec_in, self.table, self.table_in = vec, vec_in, table, table_in
        self.send, self.recv = send, recv

    def pair(self, p):
        place = self.place
        to = place.across(p - 1) if p else place.sibling()
        at = self.base + 2 * p
        vec = remote(self.vec.at[p], self.vec_in.at[p], self.send.at[at], self.recv.at[at], to)
        if self.table is None:
            return [vec]
        table = self.table.at[1 - place.t] if p == 0 else self.table.at[p + 1]
        return [vec, remote(table, self.table_in.at[p], self.send.at[at + 1], self.recv.at[at + 1], to)]

    def step(self, p, vec_out, table_out=None):
        nb = self.place.nb
        if p:
            for copy in self.pair(p - 1):
                copy.wait_recv()
            mine, theirs = self.vec[p - 1], self.vec_in[p - 1]
            total = jnp.where(iota(mine.shape, 0) < 8, mine + theirs, jnp.maximum(mine, theirs))
            if p <= nb:
                self.vec[p] = total
            else:
                vec_out[...] = total
            if self.table is not None:
                mine = self.table[self.place.t] if p == 1 else self.table[p]
                total = mine.astype(f32) + self.table_in[p - 1].astype(f32)
                if p <= nb:
                    self.table[p + 1] = total.astype(bf16)
                else:
                    table_out[...] = total
        if p <= nb:
            for copy in self.pair(p):
                copy.start()
        else:
            for q in range(nb + 1):
                for copy in self.pair(q):
                    copy.wait_send()


def body(
    inputs, cotangent, window_order, region_ids, clip_threshold, norm1_gain, norm1_shift,
    qkv_weight, qv_bias, rel_table, out_weight, out_bias, norm2_gain, norm2_shift,
    expand_weight, expand_bias, reduce_weight, reduce_bias,
):
    parts = lax.axis_size("tensor")
    groups = lax.axis_size("wide")
    mine = lax.axis_index("tensor")
    own = HEADS // parts
    oc, fc = D // parts, FF // parts
    nw = inputs.shape[0] // WIN
    strip = D // groups
    nb = bits_of(groups)
    paired = parts == 2 and groups == 1 << nb and nb > 0 and strip % 32 == 0

    order = lax.dynamic_slice_in_dim(window_order, mine * nw, nw, 0)
    region = lax.dynamic_slice_in_dim(region_ids, mine * nw * WIN, nw * WIN, 0)
    region = region.reshape(nw, WIN).astype(f32)

    def params(first):
        rows = [norm1_gain, norm1_shift, norm2_gain, norm2_shift, out_bias, reduce_bias]
        rows = jnp.pad(jnp.stack(rows + [jnp.zeros((D,), bf16)]), ((0, 0), (0, VW - D)))
        return jnp.concatenate([first[None], rows], axis=0).astype(f32)

    if paired:
        first = jnp.concatenate([qv_bias[0], jnp.zeros((oc,), bf16), qv_bias[1], expand_bias])
        weights = [params(first), padded_table(rel_table), qkv_weight]
        shards = [expand_weight, reduce_weight.T, out_weight.T]
    else:
        qkv_strip = qkv_weight.reshape(strip, own, 3, HD).transpose(0, 2, 1, 3).reshape(strip, 3 * oc)
        shard = jnp.concatenate([qkv_strip, out_weight.T, expand_weight, reduce_weight.T], axis=1)
        full = lax.all_gather(shard, BOTH, axis=0)
        full = full.reshape(groups, parts, strip, shard.shape[1]).transpose(0, 2, 1, 3)
        full = full.reshape(D, parts, shard.shape[1])
        wqkv = full[:, :, : 3 * oc].reshape(D, parts, 3, oc).transpose(0, 2, 1, 3)
        wqkv = wqkv.reshape(D, 3, 2, HALF).transpose(0, 2, 1, 3).reshape(D, 3 * D)
        wo = full[:, :, 3 * oc : 4 * oc].reshape(D, D)
        we = full[:, :, 4 * oc : 4 * oc + fc].reshape(D, FF)
        wr = full[:, :, 4 * oc + fc :].reshape(D, FF)
        small = jnp.concatenate([qv_bias.reshape(-1), expand_bias, rel_table.reshape(-1)])
        small = lax.all_gather(small, "tensor", axis=0)
        qv = small[:, : 2 * oc].reshape(parts, 2, oc).transpose(1, 0, 2).reshape(2, 2, HALF)
        be = small[:, 2 * oc : 2 * oc + fc].reshape(2, FF // 2)
        zero = jnp.zeros((HALF,), bf16)
        vecs = jnp.stack([params(jnp.concatenate([qv[0, v], zero, qv[1, v], be[v]])) for v in range(2)])
        weights = [vecs, wqkv, table_bias(small[:, 2 * oc + fc :].reshape(HEADS, RT))]
        shards = []
        nb = 0

    (xc, nrm, qkv, e, linv, att, peak, vecs, wqkv), gathered = run_attend(
        nw, nb, order, region, inputs, weights, shards
    )
    if paired:
        we, wr, wo = gathered
    layer_out, mg, gwe, gwr, gwo, feed = run_feed(nw, order, vecs, xc, att, cotangent, wo, we, wr)
    input_grad, late, table, *more = run_back(
        nw, nb, order, vecs, xc, nrm, qkv, e, linv, att, mg, wqkv, wo, feed, peak, [gwo, gwe, gwr]
    )
    if paired:
        qkv_out, early, out_own, expand_own, reduce_own = more
    else:
        gw = more[0]

        def cut(grad, width):
            return grad.transpose(1, 0, 2).reshape(D, parts, width).astype(f32)

        gw = gw.reshape(2, D, 3, HALF).transpose(1, 2, 0, 3).reshape(D, 3, parts, oc)
        gw = gw.transpose(0, 2, 1, 3).reshape(D, parts, 3 * oc).astype(f32)
        grads = jnp.concatenate([gw, cut(gwo, oc), cut(gwe, fc), cut(gwr, fc)], axis=2)
        grads = grads.reshape(groups, strip, parts, 4 * oc + 2 * fc).transpose(0, 2, 1, 3)
        grads = grads.reshape(groups * parts * strip, 4 * oc + 2 * fc)
        grads = lax.psum_scatter(grads, BOTH, scatter_dimension=0, tiled=True)
        qkv_out = grads[:, : 3 * oc].reshape(strip, 3, own, HD).transpose(0, 2, 1, 3).reshape(strip, 3 * oc)
        out_own = grads[:, 3 * oc : 4 * oc]
        expand_own, reduce_own = grads[:, 4 * oc : 4 * oc + fc], grads[:, 4 * oc + fc :]
        table = lax.dynamic_slice_in_dim(lax.psum(table, BOTH), mine * own, own, 0)
        late = lax.psum(late, BOTH)
        early = jnp.concatenate([lax.psum(feed, BOTH), lax.pmax(peak, BOTH)], axis=0)

    table_own = table[:, : 2 * WT - 1, :ROWS].reshape(own, RT)
    dbe_own = lax.dynamic_slice_in_dim(early[4:8].reshape(FF), mine * fc, fc, 0)
    heads_grad = late[2:5].reshape(2, 3, HALF)
    bias_grad = jnp.stack([heads_grad[:, 0].reshape(D), heads_grad[:, 2].reshape(D)], axis=0)
    bias_own = lax.dynamic_slice_in_dim(bias_grad, mine * oc, oc, 1)
    peak_own = lax.dynamic_slice_in_dim(early[8], mine * own, own, 0)
    factor = jnp.sqrt(clip_threshold / jnp.maximum(peak_own, clip_threshold))
    column_factor = jnp.stack([factor, factor, jnp.ones_like(factor)], axis=1)
    clipped_qkv = (
        qkv_weight.astype(f32).reshape(strip, own, 3, HD) * column_factor[None, :, :, None]
    ).reshape(qkv_weight.shape)
    bias_scale = jnp.stack([jnp.repeat(factor, HD), jnp.ones((own * HD,), f32)], axis=0)
    clipped_bias = qv_bias.astype(f32) * bias_scale
    return (
        layer_out,
        input_grad,
        late[0],
        late[1],
        qkv_out,
        bias_own,
        table_own,
        out_own.T,
        early[3],
        early[0],
        early[1],
        expand_own,
        dbe_own,
        reduce_own.T,
        early[2],
        peak_own,
        clipped_qkv,
        clipped_bias,
    )


def solution(mesh):
    tokens = P(BOTH, None)
    in_specs = (
        tokens, tokens, P("wide", None), P("wide"), P(), P(), P(), P("wide", "tensor"),
        P(None, "tensor"), P("tensor", None), P("tensor", "wide"), P(), P(), P(),
        P("wide", "tensor"), P("tensor"), P("tensor", "wide"), P(),
    )
    out_specs = (
        tokens, tokens, P(), P(), P("wide", "tensor"), P(None, "tensor"), P("tensor", None),
        P("tensor", "wide"), P(), P(), P(), P("wide", "tensor"), P("tensor"),
        P("tensor", "wide"), P(), P("tensor"), P("wide", "tensor"), P(None, "tensor"),
    )
    return jax.shard_map(body, mesh=mesh, in_specs=in_specs, out_specs=out_specs, check_vma=False)
```

```python
import functools
import math

import jax
import jax.numpy as jnp
from jax import lax
from jax.experimental import pallas as pl
from jax.experimental.pallas import tpu as pltpu
from jax.sharding import PartitionSpec as P

D = 512
HEADS = 16
HD = 32
FF = 2048
WT = 8
WH = 7
WW = 7
SP = WH * WW
WIN = 392
RT = 2535
ROWS = 13 * 13
GRP = 4

epsilon = 1e-05
masked = -100.0
lowest = -1e30
LOG2E = 1.4426950408889634
SCALE = HD ** (-0.5)
WIDE_SEG = 13 * WW * WT
WIDE_PAD = 768
PITCH = 176
FLAT_PAD = 1408
UP = 256
HALF = D // 2
QW = 3 * HALF
VW = QW + FF // 2

f32 = jnp.float32
bf16 = jnp.bfloat16
NN = (((1,), (0,)), ((), ()))
NT = (((1,), (1,)), ((), ()))
TN = (((0,), (0,)), ((), ()))

VMEM_LIMIT = 60 * 2**20


def dot(a, b, dims=NN):
    return lax.dot_general(a, b, dims, preferred_element_type=f32)


def chunks(total, size):
    starts = list(range(0, total - size + 1, size))
    sizes = [size] * len(starts)
    rest = total - size * len(starts)
    if rest:
        if rest < size // 2:
            sizes[-1] += rest
        else:
            starts.append(size * len(starts))
            sizes.append(rest)
    return list(zip(starts, sizes))


ROW_CHUNKS = chunks(WIN, 64)


def iota(shape, axis):
    return lax.broadcasted_iota(jnp.int32, shape, axis)


def group_at(g):
    return pl.multiple_of(g // 2 * QW + g % 2 * (GRP * HD), GRP * HD)


def head_lanes(hh):
    return (iota((1, GRP * HD), 1) // HD == hh).astype(f32).astype(bf16)


def picks_of(order_ref, w):
    order = order_ref[pl.ds(w, 1), :]
    return iota((WIN, WIN), 0) == order % SP * WT + order // SP


def one_hot(hit):
    return hit.astype(f32).astype(bf16)


def column_moves():
    new = iota((1, QW), 1)
    old = new % HALF // HD * (3 * HD) + new // HALF * HD + new % HD
    return one_hot(iota((QW, QW), 0) == old)


def moments(rows):
    mean = jnp.mean(rows, axis=-1, keepdims=True)
    centered = rows - mean
    spread = jnp.mean(centered * centered, axis=-1, keepdims=True)
    return centered, lax.rsqrt(spread + epsilon)


def one_hot_spread():
    column = iota((1, WIDE_PAD), 1)
    dh, rest = column // (WW * WT), column % (WW * WT)
    target = rest % WT * PITCH + (12 - dh) * 13 + 6 - rest // WT
    target = jnp.where(column < WIDE_SEG, target, -1)
    return (iota((FLAT_PAD, WIDE_PAD), 0) == target).astype(f32).astype(bf16)


def flatten_table(table_ref, flat_ref):
    total = None
    rest = jnp.zeros((HEADS * WT, FLAT_PAD - UP), f32)
    for tj in range(WT):
        rows = table_ref[:, WT - 1 - tj : 2 * WT - 1 - tj, :].reshape(HEADS * WT, UP)
        part = jnp.concatenate([rows, rest], axis=1)
        if tj:
            part = pltpu.roll(part, tj * PITCH, 1)
        total = part if total is None else total + part
    flat_ref[...] = total


def turn_table(flat_ref, wide_ref, out_ref):
    flat = flat_ref[...]
    for wi in range(WW):
        wide_ref[wi] = (pltpu.roll(flat, FLAT_PAD - wi, 1) if wi else flat).astype(bf16)
    out_ref[...] = dot(wide_ref[...].reshape(WW * HEADS * WT, FLAT_PAD), one_hot_spread()) * LOG2E


def spread_table(turned_ref, bias_ref):
    for wi in range(WW):
        for hi in range(WH):
            at = (hi * WW + wi) * WT
            off = (WH - 1 - hi) * WW * WT
            rows = turned_ref[wi * HEADS * WT : (wi + 1) * HEADS * WT, off : off + WIN]
            bias_ref[:, at : at + WT, :] = rows.reshape(HEADS, WT, WIN)


def table_kernel(table_ref, bias_ref, flat_ref, wide_ref, turned_ref):
    flatten_table(table_ref, flat_ref)
    turn_table(flat_ref, wide_ref, turned_ref)
    spread_table(turned_ref, bias_ref)


TABLE_SCRATCH = [
    pltpu.VMEM((HEADS * WT, FLAT_PAD), f32),
    pltpu.VMEM((WW, HEADS * WT, FLAT_PAD), bf16),
    pltpu.VMEM((WW * HEADS * WT, WIDE_PAD), f32),
]


def padded_table(table):
    parts = table.astype(f32).reshape(-1, 2 * WT - 1, ROWS)
    return jnp.pad(parts, ((0, 0), (0, 1), (0, UP - ROWS)))


def table_bias(table):
    return pl.pallas_call(
        table_kernel,
        out_shape=jax.ShapeDtypeStruct((HEADS, WIN, WIN), f32),
        scratch_shapes=TABLE_SCRATCH,
        compiler_params=pltpu.CompilerParams(vmem_limit_bytes=VMEM_LIMIT),
        name="table_bias",
    )(padded_table(table))


def fold_table(table_scr, seg_scr, wide_scr, out_ref):
    seg_scr[...] = jnp.zeros_like(seg_scr)
    for wi in range(WW):
        total = None
        for hi in range(WH):
            at = (hi * WW + wi) * WT
            off = (WH - 1 - hi) * WW * WT
            seg_scr[:, 0:WIN] = table_scr[:, at : at + WT, :].reshape(HEADS * WT, WIN)
            moved = seg_scr[...]
            if off:
                moved = pltpu.roll(moved, off, 1)
            total = moved if total is None else total + moved
        wide_scr[wi] = total.astype(bf16)
    flat = dot(wide_scr[...].reshape(WW * HEADS * WT, WIDE_PAD), one_hot_spread(), NT)
    total = None
    for wi in range(WW):
        part = flat[wi * HEADS * WT : (wi + 1) * HEADS * WT, :]
        part = pltpu.roll(part, wi, 1) if wi else part
        total = part if total is None else total + part
    out_ref[...] = jnp.zeros_like(out_ref)
    for tj in range(WT):
        rows = pltpu.roll(total, FLAT_PAD - tj * PITCH, 1) if tj else total
        out_ref[:, WT - 1 - tj : 2 * WT - 1 - tj, :] += rows[:, :UP].reshape(HEADS, WT, UP)


def attend_kernel(nb, order_ref, region_ref, x_ref, *rest):
    if nb:
        (params_ref, table_ref, own_ref), shards, rest = rest[:3], rest[3:6], rest[6:]
    else:
        (vecs_ref, w_ref, bias_ref), rest = rest[:3], rest[3:]
    (xc_ref, nrm_ref, qkv_ref, e_ref, linv_ref, att_ref, peak_ref), rest = rest[:7], rest[7:]
    if nb:
        (vecs_out, w_out), bufs, rest = rest[:2], rest[2:5], rest[5:]
    (x_scr, mask_scr, hm_ref), rest = rest[:3], rest[3:]
    w, g = pl.program_id(0), pl.program_id(1)
    at_step = w * (HEADS // GRP) + g
    opening = (w == 0) & (g == 0)
    if nb:
        (vecs_ref, w_scr, bias_ref, own_scr, tables, flat_ref, wide_ref, turned_ref), sems = rest[:8], rest[8:]
        place = Place(nb)
        first = Gather(place, [own_scr], [w_scr], *sems[:3])
        second = Gather(place, shards, bufs, *sems[3:])
        base = Gather.copies(nb, 1)
        mine = pl.ds(pl.multiple_of(place.t * (HEADS // 2), HEADS // 2), HEADS // 2)
        near = [
            remote(part, part, sems[0].at[base + i], sems[1].at[base + i], place.sibling())
            for i, part in enumerate((tables.at[mine], vecs_ref.at[place.t]))
        ]

    def prepare():
        pick = picks_of(order_ref, w)
        region = region_ref[pl.ds(w, 1), :]
        row_at = jnp.sum(jnp.where(pick, region, 0.0), axis=1, keepdims=True)
        pick = one_hot(pick)
        column_at = dot(jnp.broadcast_to(region, (8, WIN)).astype(bf16), pick, NT)[0:1, :]
        mask_scr[...] = jnp.where(row_at == column_at, 0.0, masked * LOG2E)
        xc_ref[...] = dot(pick, x_ref[...]).astype(bf16)
        for at, size in ROW_CHUNKS:
            centered, rstd = moments(xc_ref[at : at + size, :].astype(f32))
            nrm_ref[at : at + size, :] = (centered * rstd * vecs_ref[0, 1:2, 0:D] + vecs_ref[0, 2:3, 0:D]).astype(bf16)

    def project():
        weight = w_scr[...].reshape(D, 3 * D) if nb else w_ref
        for v in range(2):
            cols = slice(v * QW, (v + 1) * QW)
            qkv_ref[:, cols] = (dot(nrm_ref[...], weight[:, cols]) + vecs_ref[v, 0:1, 0:QW]).astype(bf16)

    def group():
        off = pl.multiple_of(g * (GRP * HD), GRP * HD)
        qoff = group_at(g)
        qg = qkv_ref[:, pl.ds(qoff, GRP * HD)]
        kg = qkv_ref[:, pl.ds(qoff + HALF, GRP * HD)]
        vg = qkv_ref[:, pl.ds(qoff + 2 * HALF, GRP * HD)]
        vx = jnp.concatenate([vg, jnp.ones((WIN, GRP * HD), bf16)], axis=1)

        def score(hh):
            x_scr[hh % 2] = dot(qg * head_lanes(hh), kg, NT)

        def soften(hh):
            h = g * GRP + hh
            top = hm_ref[h]
            for at, size in ROW_CHUNKS:
                xx = x_scr[hh % 2, at : at + size, :]
                top = jnp.maximum(top, jnp.max(xx.reshape(size // 8, 8, WIN), axis=0))
                s = xx * (SCALE * LOG2E) + bias_ref[h, at : at + size, :] + mask_scr[at : at + size, :]
                e_ref[0, hh, at : at + size, :] = jnp.exp2(s - jnp.max(s, axis=1, keepdims=True)).astype(bf16)
            hm_ref[h] = top

        def weigh(hh, total, scale):
            out = dot(e_ref[0, hh], vx)
            inv = 1.0 / out[:, GRP * HD :]
            out = out[:, : GRP * HD] * inv
            if hh == 0:
                return out, inv
            here = iota((WIN, GRP * HD), 1) // HD == hh
            return jnp.where(here, out, total), jnp.where(here, inv, scale)

        total = scale = None
        score(0)
        for hh in range(GRP):
            if hh + 1 < GRP:
                score(hh + 1)
            soften(hh)
            if hh:
                total, scale = weigh(hh - 1, total, scale)
        total, scale = weigh(GRP - 1, total, scale)
        att_ref[:, pl.ds(off, GRP * HD)] = total.astype(bf16)
        linv_ref[:, pl.ds(off, GRP * HD)] = scale

    @pl.when(opening)
    def _():
        hm_ref[...] = jnp.full(hm_ref.shape, lowest, f32)
        if nb:
            place.greet()
            own_scr[...] = dot(own_ref[...], column_moves()).astype(bf16)
            first.step(0)
            tables[mine] = table_ref[...]
            vecs_ref[place.t] = params_ref[...]
            for copy in near:
                copy.start()
            for copy in near:
                copy.wait()
            flatten_table(tables, flat_ref)
            first.step(1)

    @pl.when(g == 0)
    def _():
        prepare()

    if nb:

        @pl.when(opening)
        def _():
            first.step(2)
            turn_table(flat_ref, wide_ref, turned_ref)
            first.step(3)
            second.step(0)
            spread_table(turned_ref, bias_ref)
            for p in range(4, first.steps()):
                first.step(p)
            w_out[...] = w_scr[...].reshape(D, 3 * D)
            vecs_out[...] = vecs_ref[...]

        run_beside(second, at_step, GATHER_TIMES)

    @pl.when(g == 0)
    def _():
        project()

    group()

    @pl.when(at_step == pl.num_programs(0) * pl.num_programs(1) - 1)
    def _():
        lane = iota((1, D), 1)
        peaks = jnp.full((1, D), lowest, f32)
        for h in range(HEADS):
            top = jnp.max(jnp.max(hm_ref[h], axis=0, keepdims=True), axis=1, keepdims=True)
            peaks = jnp.where(lane == h, top * SCALE, peaks)
        peak_ref[...] = jnp.broadcast_to(peaks, peak_ref.shape)


def gelu_both(hidden):
    z = jnp.abs(hidden) * (0.5**0.5)
    base = 1.0 + 0.3275911 * z
    t = pl.reciprocal(base, approx=True)
    t = t * (2.0 - base * t)
    poly = 1.061405429
    for coefficient in (-1.453152027, 1.421413741, -0.284496736, 0.254829592):
        poly = poly * t + coefficient
    bell = jnp.exp2(hidden * hidden * (-0.5 * LOG2E))
    tail = 0.5 * poly * t * bell
    cdf = jnp.where(hidden >= 0.0, 1.0 - tail, tail)
    return hidden * cdf, cdf + hidden * bell * (1.0 / math.sqrt(2.0 * math.pi))


FC = 256
FEED_CHUNKS = chunks(WIN, 32)


def feed_kernel(
    order_ref, vecs_ref, xc_ref, att_ref, cot_ref, wo_ref, we_ref, wr_ref,
    out_ref, mgrad_ref, gwe_ref, gwr_ref, gwo_ref, vec_ref,
    mid_ref, n2_ref, cc_scr, cT_scr, nT_scr, acc_scr, ng_scr, dwe_ref, dwr_ref, dwo_ref,
    hid_scr, ag_scr, act_scr, hg_scr,
):
    w = pl.program_id(0)

    @pl.when(w == 0)
    def _():
        dwe_ref[...] = jnp.zeros_like(dwe_ref)
        dwr_ref[...] = jnp.zeros_like(dwr_ref)
        dwo_ref[...] = jnp.zeros_like(dwo_ref)
        vec_ref[...] = jnp.zeros_like(vec_ref)

    g2, s2, bo, br = (vecs_ref[0, i : i + 1, 0:D] for i in (3, 4, 5, 6))
    pick = one_hot(picks_of(order_ref, w))
    mid_ref[...] = xc_ref[...].astype(f32) + (dot(att_ref[...], wo_ref[...], NT) + bo)
    for at, size in ROW_CHUNKS:
        centered, rstd = moments(mid_ref[at : at + size, :])
        n2_ref[at : at + size, :] = (centered * rstd * g2 + s2).astype(bf16)
    canon = dot(pick, cot_ref[...])
    cc_scr[...] = canon.astype(bf16)
    cT_scr[...] = cc_scr[...].T
    nT_scr[...] = n2_ref[...].T

    blocks = [slice(c * FC, (c + 1) * FC) for c in range(FF // FC)]

    def widen(c):
        hid_scr[c % 2] = dot(n2_ref[...], we_ref[:, blocks[c]])
        ag_scr[c % 2] = dot(cc_scr[...], wr_ref[:, blocks[c]])

    def bend(c):
        half, off = divmod(c * FC, FF // 2)
        shift = vecs_ref[half, 0:1, QW + off : QW + off + FC]
        total = jnp.zeros((8, FC), f32)
        for at, size in FEED_CHUNKS:
            rows = slice(at, at + size)
            act, slope = gelu_both(hid_scr[c % 2, rows, :] + shift)
            act_scr[rows, blocks[c]] = act.astype(bf16)
            hg = (ag_scr[c % 2, rows, :] * slope).astype(bf16)
            hg_scr[rows, blocks[c]] = hg
            total += jnp.sum(hg.astype(f32).reshape(size // 8, 8, FC), axis=0)
        line, off = divmod(c * FC, D)
        vec_ref[4 + line : 5 + line, off : off + FC] += jnp.sum(total, axis=0, keepdims=True)

    def gather_up(c):
        dwr_ref[:, blocks[c]] += dot(cT_scr[...], act_scr[:, blocks[c]])
        dwe_ref[:, blocks[c]] += dot(nT_scr[...], hg_scr[:, blocks[c]])

    widen(0)
    for c in range(FF // FC):
        if c + 1 < FF // FC:
            widen(c + 1)
        bend(c)
        if c:
            gather_up(c - 1)
    gather_up(FF // FC - 1)
    acc_scr[...] = dot(act_scr[...], wr_ref[...], NT)
    ng_scr[...] = dot(hg_scr[...], we_ref[...], NT)
    for at, size in ROW_CHUNKS:
        rows = slice(at, at + size)
        mid = mid_ref[rows, :]
        cot = cc_scr[rows, :].astype(f32)
        acc_scr[rows, :] = mid + (acc_scr[rows, :] + br)
        back = ng_scr[rows, :]
        centered, rstd = moments(mid)
        xhat = centered * rstd
        g = back * g2
        mg = cot + rstd * (
            g - jnp.mean(g, axis=-1, keepdims=True) - xhat * jnp.mean(g * xhat, axis=-1, keepdims=True)
        )
        mgrad_ref[rows, :] = mg
        vec_ref[0:1, :] += jnp.sum(back * xhat, axis=0, keepdims=True)
        vec_ref[1:2, :] += jnp.sum(back, axis=0, keepdims=True)
        vec_ref[2:3, :] += jnp.sum(cot, axis=0, keepdims=True)
        vec_ref[3:4, :] += jnp.sum(mg.astype(bf16).astype(f32), axis=0, keepdims=True)
    out_ref[...] = dot(pick, acc_scr[...].astype(bf16), TN).astype(bf16)
    cT_scr[...] = mgrad_ref[...].astype(bf16).T
    dwo_ref[...] += dot(cT_scr[...], att_ref[...])

    @pl.when(w == pl.num_programs(0) - 1)
    def _():
        for grad, acc, width in ((gwe_ref, dwe_ref, FF // 2), (gwr_ref, dwr_ref, FF // 2), (gwo_ref, dwo_ref, HALF)):
            for v in range(2):
                for at in range(0, D, 64):
                    grad[v, at : at + 64, :] = acc[at : at + 64, v * width : (v + 1) * width].astype(bf16)


def back_kernel(
    nb, plans, order_ref, vecs_ref, xc_ref, nrm_ref, qkv_ref, e_ref, linv_ref, att_ref, mg_ref, w_ref, wo_ref,
    feed_ref, peak_ref, *rest
):
    if nb:
        matrices, rest = rest[:3], rest[3:]
        (out_ref, sums_out, table_out, qkv_out), outs, rest = rest[:4], rest[4:7], rest[7:]
    else:
        (out_ref, acc, table_out, gw_ref), rest = rest[:4], rest[4:]
    (
        dw_ref, wide_scr, ag_scr, dop_scr, doT_scr, qT_scr, in_scr, x_scr, ds_scr, pg_scr, dvT_scr, dkT_scr,
        table_scr, seg_scr, grad_scr,
    ), rest = rest[:15], rest[15:]
    w, g = pl.program_id(0), pl.program_id(1)
    end = HEADS // GRP - 1
    at_step = w * (HEADS // GRP) + g
    closing = at_step == pl.num_programs(0) * pl.num_programs(1) - 1
    if nb:
        (gw_ref, fold_scr, own_out, vec, vec_in, table, table_in), rest = rest[:7], rest[7:]
        acc = vec.at[0]
        place = Place(nb)
        count = [len(plan) * (nb + 2) for plan in plans]
        early, rest = rest[: count[0]], rest[count[0] :]
        late, sems = rest[: count[1]], rest[count[1] :]
        first = Scatter(place, build_streams(plans[0], matrices, early, outs, nb), *sems[:3])
        second = Scatter(place, build_streams(plans[1], [gw_ref], late, [own_out], nb), *sems[3:])
        sums = Sums(place, vec, vec_in, table, table_in, sems[3], sems[4], len(plans[1]) * (nb + 1))

    def prepare():
        ag_scr[...] = mg_ref[...].astype(bf16)
        scaled = dot(ag_scr[...], wo_ref[...]).astype(bf16).astype(f32) * linv_ref[...]
        dop_scr[...] = scaled.astype(bf16)
        in_scr[...] = (dop_scr[...].astype(f32) * -att_ref[...].astype(f32)).astype(bf16)
        doT_scr[...] = dop_scr[...].T
        for v in range(2):
            qT_scr[v * HALF : (v + 1) * HALF, :] = qkv_ref[:, v * QW : v * QW + HALF].T

    def group():
        off = pl.multiple_of(g * (GRP * HD), GRP * HD)
        qoff = group_at(g)
        kg = qkv_ref[:, pl.ds(qoff + HALF, GRP * HD)]
        vg = qkv_ref[:, pl.ds(qoff + 2 * HALF, GRP * HD)]
        vx = jnp.concatenate([vg, jnp.ones((WIN, GRP * HD), bf16)], axis=1)
        dx = jnp.concatenate([dop_scr[:, pl.ds(off, GRP * HD)], in_scr[:, pl.ds(off, GRP * HD)]], axis=1)

        def score(hh):
            lanes = head_lanes(hh)
            x_scr[hh % 2] = dot(dx * jnp.concatenate([lanes, lanes], axis=1), vx, NT)

        def differ(hh):
            h = g * GRP + hh
            for at, size in ROW_CHUNKS:
                rows = slice(at, at + size)
                ds = (e_ref[0, hh, rows, :].astype(f32) * x_scr[hh % 2, rows, :]).astype(bf16)
                ds_scr[hh % 2, rows, :] = ds
                table_scr[h, rows, :] += ds.astype(f32)

        def spread(hh, total):
            hrow = pl.ds(pl.multiple_of(off + hh * HD, HD), HD)
            ds = ds_scr[hh % 2]
            dvT_scr[hrow, :] = dot(doT_scr[hrow, :], e_ref[0, hh]).astype(bf16)
            dkT_scr[hrow, :] = (dot(qT_scr[hrow, :], ds) * SCALE).astype(bf16)
            part = dot(ds, kg * head_lanes(hh))
            return part if total is None else total + part

        total = None
        score(0)
        for hh in range(GRP):
            if hh + 1 < GRP:
                score(hh + 1)
            differ(hh)
            if hh:
                total = spread(hh - 1, total)
        total = spread(GRP - 1, total)
        pg_scr[:, pl.ds(qoff, GRP * HD)] = (total * SCALE).astype(bf16)

    def collect():
        for v in range(2):
            heads = slice(v * HALF, (v + 1) * HALF)
            pg_scr[:, v * QW + HALF : v * QW + 2 * HALF] = dkT_scr[heads, :].T
            pg_scr[:, v * QW + 2 * HALF : (v + 1) * QW] = dvT_scr[heads, :].T
        nT = nrm_ref[...].T
        for part in range(3):
            cols = slice(part * D, (part + 1) * D)
            dw_ref[:, cols] += dot(nT, pg_scr[:, cols])
            acc[10 + part : 11 + part, :] += jnp.sum(pg_scr[:, cols].astype(f32), axis=0, keepdims=True)

    def finish():
        grad_scr[...] = dot(pg_scr[...], w_ref[...], NT)
        for at, size in ROW_CHUNKS:
            rows = slice(at, at + size)
            back = grad_scr[rows, :]
            centered, rstd = moments(xc_ref[rows, :].astype(f32))
            xhat = centered * rstd
            g = back * vecs_ref[0, 1:2, 0:D]
            acc[0:1, :] += jnp.sum(back * xhat, axis=0, keepdims=True)
            acc[1:2, :] += jnp.sum(back, axis=0, keepdims=True)
            ag_scr[rows, :] = (
                mg_ref[rows, :]
                + rstd * (g - jnp.mean(g, axis=-1, keepdims=True) - xhat * jnp.mean(g * xhat, axis=-1, keepdims=True))
            ).astype(bf16)
        out_ref[...] = dot(one_hot(picks_of(order_ref, w)), ag_scr[...], TN).astype(bf16)

    @pl.when(at_step == 0)
    def _():
        dw_ref[...] = jnp.zeros_like(dw_ref)
        acc[...] = jnp.zeros((VEC_ROWS, D), f32)
        table_scr[...] = jnp.zeros_like(table_scr)
        if nb:
            place.greet()
            first.step(0)

    if nb:
        run_beside(first, at_step, SCATTER_TIMES)

    @pl.when(g == 0)
    def _():
        prepare()

    group()

    @pl.when(g == end)
    def _():
        collect()

    @pl.when(closing)
    def _():
        strip = D >> nb if nb else D
        for v in range(2):
            for at in range(0, D, 64):
                part = dw_ref[at : at + 64, v * QW : (v + 1) * QW].astype(bf16)
                if nb:
                    for i in range(64 // strip):
                        bits = tuple((at // strip + i) // (1 << k) % 2 for k in reversed(range(nb)))
                        gw_ref[(v, *bits)] = part[i * strip : (i + 1) * strip, :]
                else:
                    gw_ref[v, at : at + 64, :] = part
        if nb:
            second.step(0)

    @pl.when(g == end)
    def _():
        finish()

    @pl.when(closing)
    def _():
        acc[2:10, :] = feed_ref[...]
        acc[SUM_ROWS:VEC_ROWS, :] = peak_ref[...]
        if not nb:
            fold_table(table_scr, seg_scr, wide_scr, table_out)
            return
        second.step(1)
        for p in range(1, first.steps()):
            if SCATTER_TIMES[min(p, len(SCATTER_TIMES) - 1)] >= 1.0:
                first.step(p)
        fold_table(table_scr, seg_scr, wide_scr, fold_scr)
        half = HEADS // 2
        for v in range(2):
            table[v] = fold_scr[v * half : (v + 1) * half].astype(bf16)
        for p in range(second.steps()):
            sums.step(p, sums_out, table_out)
            if p + 2 < second.steps():
                second.step(p + 2)
        top = own_out[...].astype(bf16)
        low = (own_out[...] - top.astype(f32)).astype(bf16)
        moves = column_moves()
        qkv_out[...] = dot(top, moves, NT) + dot(low, moves, NT)


def whole(shape):
    return pl.BlockSpec(shape, lambda *at: (0,) * len(shape))


def kept(shape):
    return pl.BlockSpec(shape, lambda *at: (0,) * len(shape), pipeline_mode=pl.Buffered(1))


def per(shape):
    rest = (0,) * (len(shape) - 1)
    return pl.BlockSpec(shape, lambda w, *at: (w,) + rest)


EXPS = pl.BlockSpec((1, GRP, WIN, WIN), lambda w, g: (w, g, 0, 0))


def shape_of(shape, dtype):
    return jax.ShapeDtypeStruct(shape, dtype)


PARAMS = pltpu.CompilerParams(vmem_limit_bytes=VMEM_LIMIT)
ANY = pl.BlockSpec(memory_space=pl.ANY)
SUM_ROWS = 16
VEC_ROWS = 24


def dma(*counts):
    return [pltpu.SemaphoreType.DMA((n,)) for n in counts]


def run_attend(nw, nb, order, region, x, weights, shards):
    rows = nw * WIN
    tok = per((WIN, D))
    out_specs = [tok, tok, per((WIN, 3 * D)), EXPS, tok, tok, whole((8, D))]
    out_shape = [
        shape_of((rows, D), bf16),
        shape_of((rows, D), bf16),
        shape_of((rows, 3 * D), bf16),
        shape_of((nw, HEADS, WIN, WIN), bf16),
        shape_of((rows, D), f32),
        shape_of((rows, D), bf16),
        shape_of((8, D), f32),
    ]
    scratch = [pltpu.VMEM((2, WIN, WIN), f32), pltpu.VMEM((WIN, WIN), f32), pltpu.VMEM((HEADS, 8, WIN), f32)]
    if nb:
        strip = D >> nb
        copies, more = Gather.copies(nb, 1) + 2, Gather.copies(nb, len(shards))
        out_specs += [whole((2, 8, VW)), whole((D, 3 * D)), *[ANY] * len(shards)]
        out_shape += [shape_of((2, 8, VW), f32), shape_of((D, 3 * D), bf16)]
        out_shape += [shape_of((2,) * nb + (strip, 2 * v.shape[1]), bf16) for v in shards]
        scratch += [
            pltpu.VMEM((2, 8, VW), f32),
            pltpu.VMEM((2,) * nb + (strip, 3 * D), bf16),
            pltpu.VMEM((HEADS, WIN, WIN), f32),
            pltpu.VMEM((strip, QW), bf16),
            pltpu.VMEM((HEADS, 2 * WT, UP), f32),
            *TABLE_SCRATCH,
            *dma(copies, copies, 1, more, more, len(shards)),
        ]
    out = pl.pallas_call(
        functools.partial(attend_kernel, nb),
        grid=(nw, HEADS // GRP),
        in_specs=[
            kept((nw, WIN)), kept((nw, WIN)), tok, *(kept(v.shape) for v in weights), *[ANY] * len(shards),
        ],
        out_specs=out_specs,
        out_shape=out_shape,
        scratch_shapes=scratch,
        compiler_params=comm_params(2) if nb else PARAMS,
        name="attend",
    )(order, region, x, *weights, *shards)
    if nb:
        return out[:9], [v.reshape(D, v.shape[-1]) for v in out[9:]]
    return (*out, weights[0], weights[1]), []


def run_feed(nw, order, vecs, xc, att, cot, wo, we, wr):
    rows = nw * WIN
    tok = per((WIN, D))
    return pl.pallas_call(
        feed_kernel,
        grid=(nw,),
        in_specs=[
            kept((nw, WIN)), kept((2, 8, VW)), tok, tok, tok, kept((D, D)), kept((D, FF)), kept((D, FF)),
        ],
        out_specs=[
            tok, tok, whole((2, D, FF // 2)), whole((2, D, FF // 2)), whole((2, D, HALF)), whole((8, D)),
        ],
        out_shape=[
            shape_of((rows, D), bf16),
            shape_of((rows, D), f32),
            shape_of((2, D, FF // 2), bf16),
            shape_of((2, D, FF // 2), bf16),
            shape_of((2, D, HALF), bf16),
            shape_of((8, D), f32),
        ],
        scratch_shapes=[
            pltpu.VMEM((WIN, D), f32),
            pltpu.VMEM((WIN, D), bf16),
            pltpu.VMEM((WIN, D), bf16),
            pltpu.VMEM((D, WIN), bf16),
            pltpu.VMEM((D, WIN), bf16),
            pltpu.VMEM((WIN, D), f32),
            pltpu.VMEM((WIN, D), f32),
            pltpu.VMEM((D, FF), f32),
            pltpu.VMEM((D, FF), f32),
            pltpu.VMEM((D, D), f32),
            pltpu.VMEM((2, WIN, FC), f32),
            pltpu.VMEM((2, WIN, FC), f32),
            pltpu.VMEM((WIN, FF), bf16),
            pltpu.VMEM((WIN, FF), bf16),
        ],
        compiler_params=PARAMS,
        name="feed",
    )(order, vecs, xc, att, cot, wo, we, wr)


def run_back(nw, nb, order, vecs, xc, nrm, qkv, e, linv, att, mg, w, wo, feed, peak, grads):
    rows = nw * WIN
    tok = per((WIN, D))
    folded = (HEADS, 2 * WT, UP)
    half = (HEADS // 2, 2 * WT, UP)
    scratch = [
        pltpu.VMEM((D, 3 * D), f32),
        pltpu.VMEM((WW, HEADS * WT, WIDE_PAD), bf16),
        pltpu.VMEM((WIN, D), bf16),
        pltpu.VMEM((WIN, D), bf16),
        pltpu.VMEM((D, WIN), bf16),
        pltpu.VMEM((D, WIN), bf16),
        pltpu.VMEM((WIN, D), bf16),
        pltpu.VMEM((2, WIN, WIN), f32),
        pltpu.VMEM((2, WIN, WIN), bf16),
        pltpu.VMEM((WIN, 3 * D), bf16),
        pltpu.VMEM((D, WIN), bf16),
        pltpu.VMEM((D, WIN), bf16),
        pltpu.VMEM((HEADS, WIN, WIN), f32),
        pltpu.VMEM((HEADS * WT, WIDE_PAD), f32),
        pltpu.VMEM((WIN, D), f32),
    ]
    out_specs = [tok, whole((VEC_ROWS, D))]
    out_shape = [shape_of((rows, D), bf16), shape_of((VEC_ROWS, D), f32)]
    plans = []
    if nb:
        strip = D >> nb
        widths = [v.shape[2] for v in grads]
        plans = [stream_plan(nb, widths, strip), stream_plan(nb, [QW], strip)]
        copies = [len(plan) * (nb + 1) for plan in plans]
        more = copies[1] + 2 * (nb + 1)
        out_specs += [whole(half), whole((strip, QW)), *(whole((strip, width)) for width in widths)]
        out_shape += [shape_of(half, f32), shape_of((strip, QW), f32)]
        out_shape += [shape_of((strip, width), f32) for width in widths]
        scratch += [
            pltpu.VMEM((2,) * (nb + 1) + (strip, QW), bf16),
            pltpu.VMEM(folded, f32),
            pltpu.VMEM((strip, QW), f32),
            pltpu.VMEM((nb + 1, VEC_ROWS, D), f32),
            pltpu.VMEM((nb + 1, VEC_ROWS, D), f32),
            pltpu.VMEM((nb + 2, *half), bf16),
            pltpu.VMEM((nb + 1, *half), bf16),
        ]
        for plan, among in zip(plans, (widths, [QW])):
            for m, first, size, order_of in plan:
                scratch += Scatter.arrivals(nb, size, among[m])
        scratch += dma(copies[0], copies[0], len(plans[0]), more, more, len(plans[1]))
        grads = [v.reshape((2,) * (nb + 1) + (strip, v.shape[2])) for v in grads]
    else:
        grads = []
        out_specs += [whole(folded), whole((2, D, QW))]
        out_shape += [shape_of(folded, f32), shape_of((2, D, QW), bf16)]
    return pl.pallas_call(
        functools.partial(back_kernel, nb, plans),
        grid=(nw, HEADS // GRP),
        in_specs=[
            kept((nw, WIN)), kept((2, 8, VW)), tok, tok, per((WIN, 3 * D)), EXPS, tok, tok, tok,
            kept((D, 3 * D)), kept((D, D)), kept((8, D)), kept((8, D)), *[ANY] * len(grads),
        ],
        out_specs=out_specs,
        out_shape=out_shape,
        scratch_shapes=scratch,
        compiler_params=comm_params(3) if nb else PARAMS,
        name="attend_back",
    )(order, vecs, xc, nrm, qkv, e, linv, att, mg, w, wo, feed, peak, *grads)


BOTH = ("wide", "tensor")
MESH = pl.DeviceIdType.MESH


def bits_of(groups):
    return groups.bit_length() - 1


def orders_of(nb):
    down = tuple(reversed(range(nb)))
    if nb < 2:
        return (down,)
    half = nb // 2
    swapped = down[:-2] + (down[-1], down[-2])
    return (down, swapped, tuple(range(half)) + tuple(reversed(range(half, nb))))


def cuts_of(width, count):
    tiles = width // 128
    sizes = [(tiles + count - 1 - i) // count for i in range(count)]
    cuts, at = [], 0
    for size in sizes:
        if size:
            cuts.append((at * 128, size * 128))
            at += size
    return cuts


class Place:
    def __init__(self, nb):
        self.nb = nb
        self.w = lax.axis_index("wide")
        self.t = lax.axis_index("tensor")
        self.bit = [self.w // (1 << k) % 2 for k in range(nb)]

    def across(self, k):
        return (self.w + (1 - 2 * self.bit[k]) * (1 << k), self.t)

    def sibling(self):
        return (self.w, 1 - self.t)

    def greet(self):
        barrier = pltpu.get_barrier_semaphore()
        partners = [self.across(k) for k in range(self.nb)] + [self.sibling()]
        for partner in partners:
            pl.semaphore_signal(barrier, inc=1, device_id=partner, device_id_type=MESH)
        pl.semaphore_wait(barrier, len(partners))

    def index(self, chosen):
        return tuple(chosen.get(k, slice(None)) for k in reversed(range(self.nb)))


def remote(src, dst, send, recv, to):
    return pltpu.make_async_remote_copy(
        src_ref=src, dst_ref=dst, send_sem=send, recv_sem=recv, device_id=to, device_id_type=MESH
    )


class Gather:
    def __init__(self, place, owns, bufs, send, recv, near):
        self.place, self.owns, self.bufs = place, owns, bufs
        self.send, self.recv, self.near = send, recv, near
        nb = place.nb
        self.streams = []
        orders = orders_of(nb)
        for own, buf in zip(owns, bufs):
            for (first, size), order in zip(cuts_of(own.shape[1], len(orders)), orders):
                self.streams.append((own, buf, first, size, order))

    @staticmethod
    def copies(nb, count):
        return count * (len(orders_of(nb)) * nb + 1)

    def lanes(self, own):
        width = own.shape[1]
        return pl.ds(pl.multiple_of(self.place.t * width, 128), width)

    def local(self, b):
        own, buf = self.owns[b], self.bufs[b]
        mine = self.place.index(dict(enumerate(self.place.bit)))
        return pltpu.make_async_copy(own, buf.at[(*mine, slice(None), self.lanes(own))], self.near.at[b])

    def wide(self, s, p):
        own, buf, first, size, order = self.streams[s]
        place = self.place
        chosen = {k: place.bit[k] for k in order[p:]}
        lanes = pl.ds(pl.multiple_of(place.t * own.shape[1] + first, 128), size)
        region = buf.at[(*place.index(chosen), slice(None), lanes)]
        src = region if p else own.at[:, pl.ds(first, size)]
        at = s * place.nb + p
        return remote(src, region, self.send.at[at], self.recv.at[at], place.across(order[p]))

    def core(self, b):
        own, buf = self.owns[b], self.bufs[b]
        region = buf.at[(*self.place.index({}), slice(None), self.lanes(own))]
        at = len(self.streams) * self.place.nb + b
        return remote(region, region, self.send.at[at], self.recv.at[at], self.place.sibling())

    def step(self, p):
        nb = self.place.nb
        streams, count = range(len(self.streams)), range(len(self.bufs))
        if p == 0:
            for b in count:
                self.local(b).start()
        elif p == 1:
            for b in count:
                self.local(b).wait()
        if 0 < p <= nb:
            for s in streams:
                self.wide(s, p - 1).wait_recv()
        if p < nb:
            for s in streams:
                self.wide(s, p).start()
        elif p == nb:
            for b in count:
                self.core(b).start()
        else:
            for s in streams:
                for q in range(nb):
                    self.wide(s, q).wait_send()
            for b in count:
                self.core(b).wait()

    def steps(self):
        return self.place.nb + 2


class Scatter:
    def __init__(self, place, streams, send, recv, near):
        self.place, self.streams = place, streams
        self.send, self.recv, self.near = send, recv, near

    @staticmethod
    def arrivals(nb, rows, width):
        return [pltpu.VMEM((2,) * (nb - max(p, 0)) + (rows, width), bf16) for p in range(-1, nb + 1)]

    def local(self, s):
        matrix, first, size, order, (own, *arrive), out = self.streams[s]
        src = matrix.at[(self.place.t, *self.place.index({}), pl.ds(first, size), slice(None))]
        return pltpu.make_async_copy(src, own, self.near.at[s])

    def left(self, order, p):
        return [k for k in reversed(range(self.place.nb)) if k not in order[:p]]

    def copy(self, s, p):
        matrix, first, size, order, (own, *arrive), out = self.streams[s]
        place = self.place
        if p == 0:
            src, to = matrix.at[(1 - place.t, *place.index({}), pl.ds(first, size), slice(None))], place.sibling()
        else:
            k = order[p - 1]
            src = arrive[p - 1].at[self.part(order, p, 1 - place.bit[k])]
            to = place.across(k)
        at = s * (place.nb + 1) + p
        return remote(src, arrive[p], self.send.at[at], self.recv.at[at], to)

    def part(self, order, p, value):
        return tuple(value if k == order[p - 1] else slice(None) for k in self.left(order, p - 1))

    def add(self, s, p):
        matrix, first, size, order, (own, *arrive), out = self.streams[s]
        place = self.place
        left = self.left(order, p)

        def one(i, carry):
            picked = {k: i // (1 << j) % 2 for j, k in enumerate(left)}
            there = (*(picked[k] for k in left), slice(None), slice(None))
            if p == 0:
                here = own[there]
            else:
                picked[order[p - 1]] = place.bit[order[p - 1]]
                before = tuple(picked[k] for k in self.left(order, p - 1))
                here = arrive[p - 1][(*before, slice(None), slice(None))]
            total = here.astype(f32) + arrive[p][there].astype(f32)
            if left:
                arrive[p][there] = total.astype(bf16)
            else:
                out[first : first + size, :] = total
            return carry

        if left:
            lax.fori_loop(0, 1 << len(left), one, 0)
        else:
            one(0, 0)

    def step(self, p):
        nb = self.place.nb
        for s in range(len(self.streams)):
            if p == 0:
                self.local(s).start()
            if p == 1:
                self.local(s).wait()
            if p:
                self.copy(s, p - 1).wait_recv()
                self.add(s, p - 1)
            if p <= nb:
                self.copy(s, p).start()
        if p == nb + 1:
            for s in range(len(self.streams)):
                for q in range(nb + 1):
                    self.copy(s, q).wait_send()

    def steps(self):
        return self.place.nb + 2


GATHER_TIMES = (0.0, 0.07, 0.25, 0.44, 0.75, 0.94)
SCATTER_TIMES = (0.0, 0.13, 0.5, 0.7, 0.88, 1.0)


def run_beside(transfer, at_step, times):
    total = pl.num_programs(0) * pl.num_programs(1)
    for p in range(1, transfer.steps()):
        when = times[min(p, len(times) - 1)]
        if when < 1.0:

            @pl.when(at_step == int(when * 64) * total // 64)
            def _():
                transfer.step(p)


def comm_params(collective_id, **more):
    return pltpu.CompilerParams(
        vmem_limit_bytes=VMEM_LIMIT, collective_id=collective_id, has_side_effects=True, **more
    )


def stream_plan(nb, widths, strip):
    first, second = (tuple(reversed(orders_of(nb)[i])) for i in (0, -1 if nb < 2 else 1))
    plan = []
    for m in range(len(widths)):
        plan.append((m, 0, strip // 2, first))
        plan.append((m, strip // 2, strip // 2, second))
    return plan


def build_streams(plan, matrices, arrive, outs, nb):
    streams = []
    for i, (m, first, size, order) in enumerate(plan):
        streams.append((matrices[m], first, size, order, arrive[i * (nb + 2) : (i + 1) * (nb + 2)], outs[m]))
    return streams


class Sums:
    def __init__(self, place, vec, vec_in, table, table_in, send, recv, base):
        self.place, self.base = place, base
        self.vec, self.vec_in, self.table, self.table_in = vec, vec_in, table, table_in
        self.send, self.recv = send, recv

    def pair(self, p):
        place = self.place
        to = place.across(p - 1) if p else place.sibling()
        at = self.base + 2 * p
        table = self.table.at[1 - place.t] if p == 0 else self.table.at[p + 1]
        return (
            remote(self.vec.at[p], self.vec_in.at[p], self.send.at[at], self.recv.at[at], to),
            remote(table, self.table_in.at[p], self.send.at[at + 1], self.recv.at[at + 1], to),
        )

    def step(self, p, vec_out, table_out):
        nb = self.place.nb
        if p:
            vec, table = self.pair(p - 1)
            vec.wait_recv()
            table.wait_recv()
            mine, theirs = self.vec[p - 1], self.vec_in[p - 1]
            summed = iota(mine.shape, 0) < SUM_ROWS
            total = jnp.where(summed, mine + theirs, jnp.maximum(mine, theirs))
            mine = self.table[self.place.t] if p == 1 else self.table[p]
            table_total = mine.astype(f32) + self.table_in[p - 1].astype(f32)
            if p <= nb:
                self.vec[p] = total
                self.table[p + 1] = table_total.astype(bf16)
            else:
                vec_out[...] = total
                table_out[...] = table_total
        if p <= nb:
            for copy in self.pair(p):
                copy.start()
        else:
            for q in range(nb + 1):
                for copy in self.pair(q):
                    copy.wait_send()


def body(
    inputs, cotangent, window_order, region_ids, clip_threshold, norm1_gain, norm1_shift,
    qkv_weight, qv_bias, rel_table, out_weight, out_bias, norm2_gain, norm2_shift,
    expand_weight, expand_bias, reduce_weight, reduce_bias,
):
    parts = lax.axis_size("tensor")
    groups = lax.axis_size("wide")
    mine = lax.axis_index("tensor")
    own = HEADS // parts
    oc, fc = D // parts, FF // parts
    nw = inputs.shape[0] // WIN
    strip = D // groups
    nb = bits_of(groups)
    paired = parts == 2 and groups == 1 << nb and nb > 0 and strip % 32 == 0

    order = lax.dynamic_slice_in_dim(window_order, mine * nw, nw, 0)
    region = lax.dynamic_slice_in_dim(region_ids, mine * nw * WIN, nw * WIN, 0)
    region = region.reshape(nw, WIN).astype(f32)

    def params(first):
        rows = [norm1_gain, norm1_shift, norm2_gain, norm2_shift, out_bias, reduce_bias]
        rows = jnp.pad(jnp.stack(rows + [jnp.zeros((D,), bf16)]), ((0, 0), (0, VW - D)))
        return jnp.concatenate([first[None], rows], axis=0).astype(f32)

    if paired:
        first = jnp.concatenate([qv_bias[0], jnp.zeros((oc,), bf16), qv_bias[1], expand_bias])
        weights = [params(first), padded_table(rel_table), qkv_weight]
        shards = [out_weight.T, expand_weight, reduce_weight.T]
    else:
        qkv_strip = qkv_weight.reshape(strip, own, 3, HD).transpose(0, 2, 1, 3).reshape(strip, 3 * oc)
        shard = jnp.concatenate([qkv_strip, out_weight.T, expand_weight, reduce_weight.T], axis=1)
        full = lax.all_gather(shard, BOTH, axis=0)
        full = full.reshape(groups, parts, strip, shard.shape[1]).transpose(0, 2, 1, 3)
        full = full.reshape(D, parts, shard.shape[1])
        wqkv = full[:, :, : 3 * oc].reshape(D, parts, 3, oc).transpose(0, 2, 1, 3)
        wqkv = wqkv.reshape(D, 3, 2, HALF).transpose(0, 2, 1, 3).reshape(D, 3 * D)
        wo = full[:, :, 3 * oc : 4 * oc].reshape(D, D)
        we = full[:, :, 4 * oc : 4 * oc + fc].reshape(D, FF)
        wr = full[:, :, 4 * oc + fc :].reshape(D, FF)
        small = jnp.concatenate([qv_bias.reshape(-1), expand_bias, rel_table.reshape(-1)])
        small = lax.all_gather(small, "tensor", axis=0)
        qv = small[:, : 2 * oc].reshape(parts, 2, oc).transpose(1, 0, 2).reshape(2, 2, HALF)
        be = small[:, 2 * oc : 2 * oc + fc].reshape(2, FF // 2)
        zero = jnp.zeros((HALF,), bf16)
        vecs = jnp.stack([params(jnp.concatenate([qv[0, v], zero, qv[1, v], be[v]])) for v in range(2)])
        weights = [vecs, wqkv, table_bias(small[:, 2 * oc + fc :].reshape(HEADS, RT))]
        shards = []
        nb = 0

    (xc, nrm, qkv, e, linv, att, peak, vecs, wqkv), gathered = run_attend(
        nw, nb, order, region, inputs, weights, shards
    )
    if paired:
        wo, we, wr = gathered
    layer_out, mg, gwe, gwr, gwo, feed = run_feed(nw, order, vecs, xc, att, cotangent, wo, we, wr)
    input_grad, sums, table, qkv_own, *summed = run_back(
        nw, nb, order, vecs, xc, nrm, qkv, e, linv, att, mg, wqkv, wo, feed, peak, [gwo, gwe, gwr]
    )
    if paired:
        out_own, expand_own, reduce_own = summed
        qkv_out = qkv_own
    else:
        gw = qkv_own

        def cut(grad, width):
            return grad.transpose(1, 0, 2).reshape(D, parts, width).astype(f32)

        gw = gw.reshape(2, D, 3, HALF).transpose(1, 2, 0, 3).reshape(D, 3, parts, oc)
        gw = gw.transpose(0, 2, 1, 3).reshape(D, parts, 3 * oc).astype(f32)
        grads = jnp.concatenate([gw, cut(gwo, oc), cut(gwe, fc), cut(gwr, fc)], axis=2)
        grads = grads.reshape(groups, strip, parts, 4 * oc + 2 * fc).transpose(0, 2, 1, 3)
        grads = grads.reshape(groups * parts * strip, 4 * oc + 2 * fc)
        grads = lax.psum_scatter(grads, BOTH, scatter_dimension=0, tiled=True)
        qkv_out = grads[:, : 3 * oc].reshape(strip, 3, own, HD).transpose(0, 2, 1, 3).reshape(strip, 3 * oc)
        out_own = grads[:, 3 * oc : 4 * oc]
        expand_own, reduce_own = grads[:, 4 * oc : 4 * oc + fc], grads[:, 4 * oc + fc :]
        table = lax.dynamic_slice_in_dim(lax.psum(table, BOTH), mine * own, own, 0)
        sums = jnp.concatenate(
            [lax.psum(sums[:SUM_ROWS], BOTH), lax.pmax(sums[SUM_ROWS:], BOTH)], axis=0
        )

    table_own = table[:, : 2 * WT - 1, :ROWS].reshape(own, RT)
    dbe_own = lax.dynamic_slice_in_dim(sums[6:10].reshape(FF), mine * fc, fc, 0)
    heads_grad = sums[10:13].reshape(2, 3, HALF)
    bias_grad = jnp.stack([heads_grad[:, 0].reshape(D), heads_grad[:, 2].reshape(D)], axis=0)
    bias_own = lax.dynamic_slice_in_dim(bias_grad, mine * oc, oc, 1)
    peak_own = lax.dynamic_slice_in_dim(sums[SUM_ROWS], mine * own, own, 0)
    factor = jnp.sqrt(clip_threshold / jnp.maximum(peak_own, clip_threshold))
    column_factor = jnp.stack([factor, factor, jnp.ones_like(factor)], axis=1)
    clipped_qkv = (
        qkv_weight.astype(f32).reshape(strip, own, 3, HD) * column_factor[None, :, :, None]
    ).reshape(qkv_weight.shape)
    bias_scale = jnp.stack([jnp.repeat(factor, HD), jnp.ones((own * HD,), f32)], axis=0)
    clipped_bias = qv_bias.astype(f32) * bias_scale
    return (
        layer_out,
        input_grad,
        sums[0],
        sums[1],
        qkv_out,
        bias_own,
        table_own,
        out_own.T,
        sums[5],
        sums[2],
        sums[3],
        expand_own,
        dbe_own,
        reduce_own.T,
        sums[4],
        peak_own,
        clipped_qkv,
        clipped_bias,
    )


def solution(mesh):
    tokens = P(BOTH, None)
    in_specs = (
        tokens, tokens, P("wide", None), P("wide"), P(), P(), P(), P("wide", "tensor"),
        P(None, "tensor"), P("tensor", None), P("tensor", "wide"), P(), P(), P(),
        P("wide", "tensor"), P("tensor"), P("tensor", "wide"), P(),
    )
    out_specs = (
        tokens, tokens, P(), P(), P("wide", "tensor"), P(None, "tensor"), P("tensor", None),
        P("tensor", "wide"), P(), P(), P(), P("wide", "tensor"), P("tensor"),
        P("tensor", "wide"), P(), P("tensor"), P("wide", "tensor"), P(None, "tensor"),
    )
    return jax.shard_map(body, mesh=mesh, in_specs=in_specs, out_specs=out_specs, check_vma=False)
```

```python
import functools
import math

import jax
import jax.numpy as jnp
from jax import lax
from jax.experimental import pallas as pl
from jax.experimental.pallas import tpu as pltpu
from jax.sharding import PartitionSpec as P

D = 512
HEADS = 16
HD = 32
FF = 2048
WT = 8
WH = 7
WW = 7
SP = WH * WW
WIN = 392
RT = 2535
ROWS = 13 * 13
GRP = 4

epsilon = 1e-05
masked = -100.0
lowest = -1e30
LOG2E = 1.4426950408889634
SCALE = HD ** (-0.5)
WIDE_SEG = 13 * WW * WT
WIDE_PAD = 768
PITCH = 176
FLAT_PAD = 1408
UP = 256
HALF = D // 2
QW = 3 * HALF
VW = QW + FF // 2

f32 = jnp.float32
bf16 = jnp.bfloat16
NN = (((1,), (0,)), ((), ()))
NT = (((1,), (1,)), ((), ()))
TN = (((0,), (0,)), ((), ()))

VMEM_LIMIT = 60 * 2**20


def dot(a, b, dims=NN):
    return lax.dot_general(a, b, dims, preferred_element_type=f32)


def chunks(total, size):
    starts = list(range(0, total - size + 1, size))
    sizes = [size] * len(starts)
    rest = total - size * len(starts)
    if rest:
        if rest < size // 2:
            sizes[-1] += rest
        else:
            starts.append(size * len(starts))
            sizes.append(rest)
    return list(zip(starts, sizes))


ROW_CHUNKS = chunks(WIN, 64)


def iota(shape, axis):
    return lax.broadcasted_iota(jnp.int32, shape, axis)


def group_at(g):
    return pl.multiple_of(g // 2 * QW + g % 2 * (GRP * HD), GRP * HD)


def head_lanes(hh):
    return (iota((1, GRP * HD), 1) // HD == hh).astype(f32).astype(bf16)


def picks_of(order_ref, w):
    order = order_ref[pl.ds(w, 1), :]
    return iota((WIN, WIN), 0) == order % SP * WT + order // SP


def one_hot(hit):
    return hit.astype(f32).astype(bf16)


def column_moves():
    new = iota((1, QW), 1)
    old = new % HALF // HD * (3 * HD) + new // HALF * HD + new % HD
    return one_hot(iota((QW, QW), 0) == old)


def moments(rows):
    mean = jnp.mean(rows, axis=-1, keepdims=True)
    centered = rows - mean
    spread = jnp.mean(centered * centered, axis=-1, keepdims=True)
    return centered, lax.rsqrt(spread + epsilon)


def one_hot_spread():
    column = iota((1, WIDE_PAD), 1)
    dh, rest = column // (WW * WT), column % (WW * WT)
    target = rest % WT * PITCH + (12 - dh) * 13 + 6 - rest // WT
    target = jnp.where(column < WIDE_SEG, target, -1)
    return (iota((FLAT_PAD, WIDE_PAD), 0) == target).astype(f32).astype(bf16)


def flatten_table(table_ref, flat_ref):
    total = None
    rest = jnp.zeros((HEADS * WT, FLAT_PAD - UP), f32)
    for tj in range(WT):
        rows = table_ref[:, WT - 1 - tj : 2 * WT - 1 - tj, :].reshape(HEADS * WT, UP)
        part = jnp.concatenate([rows, rest], axis=1)
        if tj:
            part = pltpu.roll(part, tj * PITCH, 1)
        total = part if total is None else total + part
    flat_ref[...] = total


def turn_table(flat_ref, wide_ref, out_ref):
    flat = flat_ref[...]
    for wi in range(WW):
        wide_ref[wi] = (pltpu.roll(flat, FLAT_PAD - wi, 1) if wi else flat).astype(bf16)
    out_ref[...] = dot(wide_ref[...].reshape(WW * HEADS * WT, FLAT_PAD), one_hot_spread()) * LOG2E


def spread_table(turned_ref, bias_ref):
    for wi in range(WW):
        for hi in range(WH):
            at = (hi * WW + wi) * WT
            off = (WH - 1 - hi) * WW * WT
            rows = turned_ref[wi * HEADS * WT : (wi + 1) * HEADS * WT, off : off + WIN]
            bias_ref[:, at : at + WT, :] = rows.reshape(HEADS, WT, WIN)


def table_kernel(table_ref, bias_ref, flat_ref, wide_ref, turned_ref):
    flatten_table(table_ref, flat_ref)
    turn_table(flat_ref, wide_ref, turned_ref)
    spread_table(turned_ref, bias_ref)


TABLE_SCRATCH = [
    pltpu.VMEM((HEADS * WT, FLAT_PAD), f32),
    pltpu.VMEM((WW, HEADS * WT, FLAT_PAD), bf16),
    pltpu.VMEM((WW * HEADS * WT, WIDE_PAD), f32),
]


def padded_table(table):
    parts = table.astype(f32).reshape(-1, 2 * WT - 1, ROWS)
    return jnp.pad(parts, ((0, 0), (0, 1), (0, UP - ROWS)))


def table_bias(table):
    return pl.pallas_call(
        table_kernel,
        out_shape=jax.ShapeDtypeStruct((HEADS, WIN, WIN), f32),
        scratch_shapes=TABLE_SCRATCH,
        compiler_params=pltpu.CompilerParams(vmem_limit_bytes=VMEM_LIMIT),
        name="table_bias",
    )(padded_table(table))


def fold_table(table_scr, seg_scr, wide_scr, out_ref):
    seg_scr[...] = jnp.zeros_like(seg_scr)
    for wi in range(WW):
        total = None
        for hi in range(WH):
            at = (hi * WW + wi) * WT
            off = (WH - 1 - hi) * WW * WT
            seg_scr[:, 0:WIN] = table_scr[:, at : at + WT, :].reshape(HEADS * WT, WIN)
            moved = seg_scr[...]
            if off:
                moved = pltpu.roll(moved, off, 1)
            total = moved if total is None else total + moved
        wide_scr[wi] = total.astype(bf16)
    flat = dot(wide_scr[...].reshape(WW * HEADS * WT, WIDE_PAD), one_hot_spread(), NT)
    total = None
    for wi in range(WW):
        part = flat[wi * HEADS * WT : (wi + 1) * HEADS * WT, :]
        part = pltpu.roll(part, wi, 1) if wi else part
        total = part if total is None else total + part
    out_ref[...] = jnp.zeros_like(out_ref)
    for tj in range(WT):
        rows = pltpu.roll(total, FLAT_PAD - tj * PITCH, 1) if tj else total
        out_ref[:, WT - 1 - tj : 2 * WT - 1 - tj, :] += rows[:, :UP].reshape(HEADS, WT, UP)


def attend_kernel(nb, order_ref, region_ref, x_ref, *rest):
    if nb:
        (params_ref, table_ref, own_ref), shards, rest = rest[:3], rest[3:6], rest[6:]
    else:
        (vecs_ref, w_ref, bias_ref), rest = rest[:3], rest[3:]
    (xc_ref, nrm_ref, qkv_ref, e_ref, linv_ref, att_ref, peak_ref), rest = rest[:7], rest[7:]
    if nb:
        (vecs_out, w_out), bufs, rest = rest[:2], rest[2:5], rest[5:]
    (x_scr, mask_scr, hm_ref), rest = rest[:3], rest[3:]
    w, g = pl.program_id(0), pl.program_id(1)
    at_step = w * (HEADS // GRP) + g
    opening = (w == 0) & (g == 0)
    if nb:
        (vecs_ref, w_scr, bias_ref, own_scr, tables, flat_ref, wide_ref, turned_ref), sems = rest[:8], rest[8:]
        place = Place(nb)
        first = Gather(place, [own_scr], [w_scr], *sems[:3])
        second = Gather(place, shards, bufs, *sems[3:])
        base = Gather.copies(nb, 1)
        mine = pl.ds(pl.multiple_of(place.t * (HEADS // 2), HEADS // 2), HEADS // 2)
        near = [
            remote(part, part, sems[0].at[base + i], sems[1].at[base + i], place.sibling())
            for i, part in enumerate((tables.at[mine], vecs_ref.at[place.t]))
        ]

    def prepare():
        pick = picks_of(order_ref, w)
        region = region_ref[pl.ds(w, 1), :]
        row_at = jnp.sum(jnp.where(pick, region, 0.0), axis=1, keepdims=True)
        pick = one_hot(pick)
        column_at = dot(jnp.broadcast_to(region, (8, WIN)).astype(bf16), pick, NT)[0:1, :]
        mask_scr[...] = jnp.where(row_at == column_at, 0.0, masked * LOG2E)
        xc_ref[...] = dot(pick, x_ref[...]).astype(bf16)
        for at, size in ROW_CHUNKS:
            centered, rstd = moments(xc_ref[at : at + size, :].astype(f32))
            nrm_ref[at : at + size, :] = (centered * rstd * vecs_ref[0, 1:2, 0:D] + vecs_ref[0, 2:3, 0:D]).astype(bf16)

    def project():
        weight = w_scr[...].reshape(D, 3 * D) if nb else w_ref
        for v in range(2):
            cols = slice(v * QW, (v + 1) * QW)
            qkv_ref[:, cols] = (dot(nrm_ref[...], weight[:, cols]) + vecs_ref[v, 0:1, 0:QW]).astype(bf16)

    def group():
        off = pl.multiple_of(g * (GRP * HD), GRP * HD)
        qoff = group_at(g)
        qg = qkv_ref[:, pl.ds(qoff, GRP * HD)]
        kg = qkv_ref[:, pl.ds(qoff + HALF, GRP * HD)]
        vg = qkv_ref[:, pl.ds(qoff + 2 * HALF, GRP * HD)]
        vx = jnp.concatenate([vg, jnp.ones((WIN, GRP * HD), bf16)], axis=1)

        def score(hh):
            x_scr[hh % 2] = dot(qg * head_lanes(hh), kg, NT)

        def soften(hh):
            h = g * GRP + hh
            top = hm_ref[h]
            for at, size in ROW_CHUNKS:
                xx = x_scr[hh % 2, at : at + size, :]
                top = jnp.maximum(top, jnp.max(xx.reshape(size // 8, 8, WIN), axis=0))
                s = xx * (SCALE * LOG2E) + bias_ref[h, at : at + size, :] + mask_scr[at : at + size, :]
                e_ref[0, hh, at : at + size, :] = jnp.exp2(s - jnp.max(s, axis=1, keepdims=True)).astype(bf16)
            hm_ref[h] = top

        def weigh(hh, total, scale):
            out = dot(e_ref[0, hh], vx)
            inv = 1.0 / out[:, GRP * HD :]
            out = out[:, : GRP * HD] * inv
            if hh == 0:
                return out, inv
            here = iota((WIN, GRP * HD), 1) // HD == hh
            return jnp.where(here, out, total), jnp.where(here, inv, scale)

        total = scale = None
        score(0)
        for hh in range(GRP):
            if hh + 1 < GRP:
                score(hh + 1)
            soften(hh)
            if hh:
                total, scale = weigh(hh - 1, total, scale)
        total, scale = weigh(GRP - 1, total, scale)
        att_ref[:, pl.ds(off, GRP * HD)] = total.astype(bf16)
        linv_ref[:, pl.ds(off, GRP * HD)] = scale

    @pl.when(opening)
    def _():
        hm_ref[...] = jnp.full(hm_ref.shape, lowest, f32)
        if nb:
            place.greet()
            own_scr[...] = dot(own_ref[...], column_moves()).astype(bf16)
            first.step(0)
            tables[mine] = table_ref[...]
            vecs_ref[place.t] = params_ref[...]
            for copy in near:
                copy.start()
            for copy in near:
                copy.wait()
            flatten_table(tables, flat_ref)
            first.step(1)

    @pl.when(g == 0)
    def _():
        prepare()

    if nb:

        @pl.when(opening)
        def _():
            first.step(2)
            turn_table(flat_ref, wide_ref, turned_ref)
            first.step(3)
            second.step(0)
            spread_table(turned_ref, bias_ref)
            for p in range(4, first.steps()):
                first.step(p)
            w_out[...] = w_scr[...].reshape(D, 3 * D)
            vecs_out[...] = vecs_ref[...]

        run_beside(second, at_step, GATHER_TIMES)

    @pl.when(g == 0)
    def _():
        project()

    group()

    @pl.when(at_step == pl.num_programs(0) * pl.num_programs(1) - 1)
    def _():
        lane = iota((1, D), 1)
        peaks = jnp.full((1, D), lowest, f32)
        for h in range(HEADS):
            top = jnp.max(jnp.max(hm_ref[h], axis=0, keepdims=True), axis=1, keepdims=True)
            peaks = jnp.where(lane == h, top * SCALE, peaks)
        peak_ref[...] = jnp.broadcast_to(peaks, peak_ref.shape)


def gelu_both(hidden):
    z = jnp.abs(hidden) * (0.5**0.5)
    base = 1.0 + 0.3275911 * z
    t = pl.reciprocal(base, approx=True)
    t = t * (2.0 - base * t)
    poly = 1.061405429
    for coefficient in (-1.453152027, 1.421413741, -0.284496736, 0.254829592):
        poly = poly * t + coefficient
    bell = jnp.exp2(hidden * hidden * (-0.5 * LOG2E))
    tail = 0.5 * poly * t * bell
    cdf = jnp.where(hidden >= 0.0, 1.0 - tail, tail)
    return hidden * cdf, cdf + hidden * bell * (1.0 / math.sqrt(2.0 * math.pi))


FC = 256
FEED_CHUNKS = chunks(WIN, 32)


def feed_kernel(
    order_ref, vecs_ref, xc_ref, att_ref, cot_ref, wo_ref, we_ref, wr_ref,
    out_ref, mgrad_ref, gwe_ref, gwr_ref, gwo_ref, vec_ref,
    mid_ref, n2_ref, cc_scr, cT_scr, nT_scr, acc_scr, ng_scr, dwe_ref, dwr_ref, dwo_ref,
    hid_scr, ag_scr, act_scr, hg_scr,
):
    w = pl.program_id(0)

    @pl.when(w == 0)
    def _():
        dwe_ref[...] = jnp.zeros_like(dwe_ref)
        dwr_ref[...] = jnp.zeros_like(dwr_ref)
        dwo_ref[...] = jnp.zeros_like(dwo_ref)
        vec_ref[...] = jnp.zeros_like(vec_ref)

    g2, s2, bo, br = (vecs_ref[0, i : i + 1, 0:D] for i in (3, 4, 5, 6))
    pick = one_hot(picks_of(order_ref, w))
    mid_ref[...] = xc_ref[...].astype(f32) + (dot(att_ref[...], wo_ref[...], NT) + bo)
    for at, size in ROW_CHUNKS:
        centered, rstd = moments(mid_ref[at : at + size, :])
        n2_ref[at : at + size, :] = (centered * rstd * g2 + s2).astype(bf16)
    canon = dot(pick, cot_ref[...])
    cc_scr[...] = canon.astype(bf16)
    cT_scr[...] = cc_scr[...].T
    nT_scr[...] = n2_ref[...].T

    blocks = [slice(c * FC, (c + 1) * FC) for c in range(FF // FC)]

    def widen(c):
        hid_scr[c % 2] = dot(n2_ref[...], we_ref[:, blocks[c]])
        ag_scr[c % 2] = dot(cc_scr[...], wr_ref[:, blocks[c]])

    def bend(c):
        half, off = divmod(c * FC, FF // 2)
        shift = vecs_ref[half, 0:1, QW + off : QW + off + FC]
        total = jnp.zeros((8, FC), f32)
        for at, size in FEED_CHUNKS:
            rows = slice(at, at + size)
            act, slope = gelu_both(hid_scr[c % 2, rows, :] + shift)
            act_scr[rows, blocks[c]] = act.astype(bf16)
            hg = (ag_scr[c % 2, rows, :] * slope).astype(bf16)
            hg_scr[rows, blocks[c]] = hg
            total += jnp.sum(hg.astype(f32).reshape(size // 8, 8, FC), axis=0)
        line, off = divmod(c * FC, D)
        vec_ref[4 + line : 5 + line, off : off + FC] += jnp.sum(total, axis=0, keepdims=True)

    def gather_up(c):
        dwr_ref[:, blocks[c]] += dot(cT_scr[...], act_scr[:, blocks[c]])
        dwe_ref[:, blocks[c]] += dot(nT_scr[...], hg_scr[:, blocks[c]])

    widen(0)
    for c in range(FF // FC):
        if c + 1 < FF // FC:
            widen(c + 1)
        bend(c)
        if c:
            gather_up(c - 1)
    gather_up(FF // FC - 1)
    acc_scr[...] = dot(act_scr[...], wr_ref[...], NT)
    ng_scr[...] = dot(hg_scr[...], we_ref[...], NT)
    for at, size in ROW_CHUNKS:
        rows = slice(at, at + size)
        mid = mid_ref[rows, :]
        cot = cc_scr[rows, :].astype(f32)
        acc_scr[rows, :] = mid + (acc_scr[rows, :] + br)
        back = ng_scr[rows, :]
        centered, rstd = moments(mid)
        xhat = centered * rstd
        g = back * g2
        mg = cot + rstd * (
            g - jnp.mean(g, axis=-1, keepdims=True) - xhat * jnp.mean(g * xhat, axis=-1, keepdims=True)
        )
        mgrad_ref[rows, :] = mg
        vec_ref[0:1, :] += jnp.sum(back * xhat, axis=0, keepdims=True)
        vec_ref[1:2, :] += jnp.sum(back, axis=0, keepdims=True)
        vec_ref[2:3, :] += jnp.sum(cot, axis=0, keepdims=True)
        vec_ref[3:4, :] += jnp.sum(mg.astype(bf16).astype(f32), axis=0, keepdims=True)
    out_ref[...] = dot(pick, acc_scr[...].astype(bf16), TN).astype(bf16)
    cT_scr[...] = mgrad_ref[...].astype(bf16).T
    dwo_ref[...] += dot(cT_scr[...], att_ref[...])

    @pl.when(w == pl.num_programs(0) - 1)
    def _():
        for grad, acc, width in ((gwe_ref, dwe_ref, FF // 2), (gwr_ref, dwr_ref, FF // 2), (gwo_ref, dwo_ref, HALF)):
            for v in range(2):
                for at in range(0, D, 64):
                    grad[v, at : at + 64, :] = acc[at : at + 64, v * width : (v + 1) * width].astype(bf16)


def back_kernel(
    nb, plans, order_ref, vecs_ref, xc_ref, nrm_ref, qkv_ref, e_ref, linv_ref, att_ref, mg_ref, w_ref, wo_ref,
    feed_ref, peak_ref, *rest
):
    if nb:
        matrices, rest = rest[:3], rest[3:]
        (out_ref, sums_out, table_out, qkv_out), outs, rest = rest[:4], rest[4:7], rest[7:]
    else:
        (out_ref, acc, table_out, gw_ref), rest = rest[:4], rest[4:]
    (
        dw_ref, wide_scr, ag_scr, dop_scr, doT_scr, qT_scr, in_scr, x_scr, ds_scr, pg_scr, dvT_scr, dkT_scr,
        table_scr, seg_scr, grad_scr,
    ), rest = rest[:15], rest[15:]
    w, g = pl.program_id(0), pl.program_id(1)
    end = HEADS // GRP - 1
    at_step = w * (HEADS // GRP) + g
    closing = at_step == pl.num_programs(0) * pl.num_programs(1) - 1
    if nb:
        (gw_ref, fold_scr, own_out, vec, vec_in, table, table_in), rest = rest[:7], rest[7:]
        acc = vec.at[0]
        place = Place(nb)
        count = [len(plan) * (nb + 2) for plan in plans]
        early, rest = rest[: count[0]], rest[count[0] :]
        late, sems = rest[: count[1]], rest[count[1] :]
        first = Scatter(place, build_streams(plans[0], matrices, early, outs, nb), *sems[:3])
        second = Scatter(place, build_streams(plans[1], [gw_ref], late, [own_out], nb), *sems[3:])
        sums = Sums(place, vec, vec_in, table, table_in, sems[3], sems[4], len(plans[1]) * (nb + 1))

    def prepare():
        ag_scr[...] = mg_ref[...].astype(bf16)
        scaled = dot(ag_scr[...], wo_ref[...]).astype(bf16).astype(f32) * linv_ref[...]
        dop_scr[...] = scaled.astype(bf16)
        in_scr[...] = (dop_scr[...].astype(f32) * -att_ref[...].astype(f32)).astype(bf16)
        doT_scr[...] = dop_scr[...].T
        for v in range(2):
            qT_scr[v * HALF : (v + 1) * HALF, :] = qkv_ref[:, v * QW : v * QW + HALF].T

    def group():
        off = pl.multiple_of(g * (GRP * HD), GRP * HD)
        qoff = group_at(g)
        kg = qkv_ref[:, pl.ds(qoff + HALF, GRP * HD)]
        vg = qkv_ref[:, pl.ds(qoff + 2 * HALF, GRP * HD)]
        vx = jnp.concatenate([vg, jnp.ones((WIN, GRP * HD), bf16)], axis=1)
        dx = jnp.concatenate([dop_scr[:, pl.ds(off, GRP * HD)], in_scr[:, pl.ds(off, GRP * HD)]], axis=1)

        def score(hh):
            lanes = head_lanes(hh)
            x_scr[hh % 2] = dot(dx * jnp.concatenate([lanes, lanes], axis=1), vx, NT)

        def differ(hh):
            h = g * GRP + hh
            for at, size in ROW_CHUNKS:
                rows = slice(at, at + size)
                ds = (e_ref[0, hh, rows, :].astype(f32) * x_scr[hh % 2, rows, :]).astype(bf16)
                ds_scr[hh % 2, rows, :] = ds
                table_scr[h, rows, :] += ds.astype(f32)

        def spread(hh, total):
            hrow = pl.ds(pl.multiple_of(off + hh * HD, HD), HD)
            ds = ds_scr[hh % 2]
            dvT_scr[hrow, :] = dot(doT_scr[hrow, :], e_ref[0, hh]).astype(bf16)
            dkT_scr[hrow, :] = (dot(qT_scr[hrow, :], ds) * SCALE).astype(bf16)
            part = dot(ds, kg * head_lanes(hh))
            return part if total is None else total + part

        total = None
        score(0)
        for hh in range(GRP):
            if hh + 1 < GRP:
                score(hh + 1)
            differ(hh)
            if hh:
                total = spread(hh - 1, total)
        total = spread(GRP - 1, total)
        pg_scr[:, pl.ds(qoff, GRP * HD)] = (total * SCALE).astype(bf16)

    def collect():
        for v in range(2):
            heads = slice(v * HALF, (v + 1) * HALF)
            pg_scr[:, v * QW + HALF : v * QW + 2 * HALF] = dkT_scr[heads, :].T
            pg_scr[:, v * QW + 2 * HALF : (v + 1) * QW] = dvT_scr[heads, :].T
        nT = nrm_ref[...].T
        for part in range(3):
            cols = slice(part * D, (part + 1) * D)
            dw_ref[:, cols] += dot(nT, pg_scr[:, cols])
            acc[10 + part : 11 + part, :] += jnp.sum(pg_scr[:, cols].astype(f32), axis=0, keepdims=True)

    def finish():
        grad_scr[...] = dot(pg_scr[...], w_ref[...], NT)
        for at, size in ROW_CHUNKS:
            rows = slice(at, at + size)
            back = grad_scr[rows, :]
            centered, rstd = moments(xc_ref[rows, :].astype(f32))
            xhat = centered * rstd
            g = back * vecs_ref[0, 1:2, 0:D]
            acc[0:1, :] += jnp.sum(back * xhat, axis=0, keepdims=True)
            acc[1:2, :] += jnp.sum(back, axis=0, keepdims=True)
            ag_scr[rows, :] = (
                mg_ref[rows, :]
                + rstd * (g - jnp.mean(g, axis=-1, keepdims=True) - xhat * jnp.mean(g * xhat, axis=-1, keepdims=True))
            ).astype(bf16)
        out_ref[...] = dot(one_hot(picks_of(order_ref, w)), ag_scr[...], TN).astype(bf16)

    @pl.when(at_step == 0)
    def _():
        dw_ref[...] = jnp.zeros_like(dw_ref)
        acc[...] = jnp.zeros((VEC_ROWS, D), f32)
        table_scr[...] = jnp.zeros_like(table_scr)
        if nb:
            place.greet()
            first.step(0)

    if nb:
        run_beside(first, at_step, SCATTER_TIMES)

    @pl.when(g == 0)
    def _():
        prepare()

    group()

    @pl.when(g == end)
    def _():
        collect()

    @pl.when(closing)
    def _():
        strip = D >> nb if nb else D
        for v in range(2):
            for at in range(0, D, 64):
                part = dw_ref[at : at + 64, v * QW : (v + 1) * QW].astype(bf16)
                if nb:
                    for i in range(64 // strip):
                        bits = tuple((at // strip + i) // (1 << k) % 2 for k in reversed(range(nb)))
                        gw_ref[(v, *bits)] = part[i * strip : (i + 1) * strip, :]
                else:
                    gw_ref[v, at : at + 64, :] = part
        if nb:
            second.step(0)

    @pl.when(g == end)
    def _():
        finish()

    @pl.when(closing)
    def _():
        acc[2:10, :] = feed_ref[...]
        acc[SUM_ROWS:VEC_ROWS, :] = peak_ref[...]
        if not nb:
            fold_table(table_scr, seg_scr, wide_scr, table_out)
            return
        second.step(1)
        for p in range(1, first.steps()):
            if SCATTER_TIMES[min(p, len(SCATTER_TIMES) - 1)] >= 1.0:
                first.step(p)
        fold_table(table_scr, seg_scr, wide_scr, fold_scr)
        half = HEADS // 2
        for v in range(2):
            table[v] = fold_scr[v * half : (v + 1) * half].astype(bf16)
        for p in range(second.steps()):
            sums.step(p, sums_out, table_out)
            if p + 2 < second.steps():
                second.step(p + 2)
        top = own_out[...].astype(bf16)
        low = (own_out[...] - top.astype(f32)).astype(bf16)
        moves = column_moves()
        qkv_out[...] = dot(top, moves, NT) + dot(low, moves, NT)


def whole(shape):
    return pl.BlockSpec(shape, lambda *at: (0,) * len(shape))


def kept(shape):
    return pl.BlockSpec(shape, lambda *at: (0,) * len(shape), pipeline_mode=pl.Buffered(1))


def per(shape):
    rest = (0,) * (len(shape) - 1)
    return pl.BlockSpec(shape, lambda w, *at: (w,) + rest)


EXPS = pl.BlockSpec((1, GRP, WIN, WIN), lambda w, g: (w, g, 0, 0))


def shape_of(shape, dtype):
    return jax.ShapeDtypeStruct(shape, dtype)


PARAMS = pltpu.CompilerParams(vmem_limit_bytes=VMEM_LIMIT)
ANY = pl.BlockSpec(memory_space=pl.ANY)
SUM_ROWS = 16
VEC_ROWS = 24


def dma(*counts):
    return [pltpu.SemaphoreType.DMA((n,)) for n in counts]


def run_attend(nw, nb, order, region, x, weights, shards):
    rows = nw * WIN
    tok = per((WIN, D))
    out_specs = [tok, tok, per((WIN, 3 * D)), EXPS, tok, tok, whole((8, D))]
    out_shape = [
        shape_of((rows, D), bf16),
        shape_of((rows, D), bf16),
        shape_of((rows, 3 * D), bf16),
        shape_of((nw, HEADS, WIN, WIN), bf16),
        shape_of((rows, D), f32),
        shape_of((rows, D), bf16),
        shape_of((8, D), f32),
    ]
    scratch = [pltpu.VMEM((2, WIN, WIN), f32), pltpu.VMEM((WIN, WIN), f32), pltpu.VMEM((HEADS, 8, WIN), f32)]
    if nb:
        strip = D >> nb
        copies, more = Gather.copies(nb, 1) + 2, Gather.copies(nb, len(shards))
        out_specs += [whole((2, 8, VW)), whole((D, 3 * D)), *[ANY] * len(shards)]
        out_shape += [shape_of((2, 8, VW), f32), shape_of((D, 3 * D), bf16)]
        out_shape += [shape_of((2,) * nb + (strip, 2 * v.shape[1]), bf16) for v in shards]
        scratch += [
            pltpu.VMEM((2, 8, VW), f32),
            pltpu.VMEM((2,) * nb + (strip, 3 * D), bf16),
            pltpu.VMEM((HEADS, WIN, WIN), f32),
            pltpu.VMEM((strip, QW), bf16),
            pltpu.VMEM((HEADS, 2 * WT, UP), f32),
            *TABLE_SCRATCH,
            *dma(copies, copies, 1, more, more, len(shards)),
        ]
    out = pl.pallas_call(
        functools.partial(attend_kernel, nb),
        grid=(nw, HEADS // GRP),
        in_specs=[
            kept((nw, WIN)), kept((nw, WIN)), tok, *(kept(v.shape) for v in weights), *[ANY] * len(shards),
        ],
        out_specs=out_specs,
        out_shape=out_shape,
        scratch_shapes=scratch,
        compiler_params=comm_params(2) if nb else PARAMS,
        name="attend",
    )(order, region, x, *weights, *shards)
    if nb:
        return out[:9], [v.reshape(D, v.shape[-1]) for v in out[9:]]
    return (*out, weights[0], weights[1]), []


def run_feed(nw, order, vecs, xc, att, cot, wo, we, wr):
    rows = nw * WIN
    tok = per((WIN, D))
    return pl.pallas_call(
        feed_kernel,
        grid=(nw,),
        in_specs=[
            kept((nw, WIN)), kept((2, 8, VW)), tok, tok, tok, kept((D, D)), kept((D, FF)), kept((D, FF)),
        ],
        out_specs=[
            tok, tok, whole((2, D, FF // 2)), whole((2, D, FF // 2)), whole((2, D, HALF)), whole((8, D)),
        ],
        out_shape=[
            shape_of((rows, D), bf16),
            shape_of((rows, D), f32),
            shape_of((2, D, FF // 2), bf16),
            shape_of((2, D, FF // 2), bf16),
            shape_of((2, D, HALF), bf16),
            shape_of((8, D), f32),
        ],
        scratch_shapes=[
            pltpu.VMEM((WIN, D), f32),
            pltpu.VMEM((WIN, D), bf16),
            pltpu.VMEM((WIN, D), bf16),
            pltpu.VMEM((D, WIN), bf16),
            pltpu.VMEM((D, WIN), bf16),
            pltpu.VMEM((WIN, D), f32),
            pltpu.VMEM((WIN, D), f32),
            pltpu.VMEM((D, FF), f32),
            pltpu.VMEM((D, FF), f32),
            pltpu.VMEM((D, D), f32),
            pltpu.VMEM((2, WIN, FC), f32),
            pltpu.VMEM((2, WIN, FC), f32),
            pltpu.VMEM((WIN, FF), bf16),
            pltpu.VMEM((WIN, FF), bf16),
        ],
        compiler_params=PARAMS,
        name="feed",
    )(order, vecs, xc, att, cot, wo, we, wr)


def run_back(nw, nb, order, vecs, xc, nrm, qkv, e, linv, att, mg, w, wo, feed, peak, grads):
    rows = nw * WIN
    tok = per((WIN, D))
    folded = (HEADS, 2 * WT, UP)
    half = (HEADS // 2, 2 * WT, UP)
    scratch = [
        pltpu.VMEM((D, 3 * D), f32),
        pltpu.VMEM((WW, HEADS * WT, WIDE_PAD), bf16),
        pltpu.VMEM((WIN, D), bf16),
        pltpu.VMEM((WIN, D), bf16),
        pltpu.VMEM((D, WIN), bf16),
        pltpu.VMEM((D, WIN), bf16),
        pltpu.VMEM((WIN, D), bf16),
        pltpu.VMEM((2, WIN, WIN), f32),
        pltpu.VMEM((2, WIN, WIN), bf16),
        pltpu.VMEM((WIN, 3 * D), bf16),
        pltpu.VMEM((D, WIN), bf16),
        pltpu.VMEM((D, WIN), bf16),
        pltpu.VMEM((HEADS, WIN, WIN), f32),
        pltpu.VMEM((HEADS * WT, WIDE_PAD), f32),
        pltpu.VMEM((WIN, D), f32),
    ]
    out_specs = [tok, whole((VEC_ROWS, D))]
    out_shape = [shape_of((rows, D), bf16), shape_of((VEC_ROWS, D), f32)]
    plans = []
    if nb:
        strip = D >> nb
        widths = [v.shape[2] for v in grads]
        plans = [stream_plan(nb, widths, strip), stream_plan(nb, [QW], strip)]
        copies = [len(plan) * (nb + 1) for plan in plans]
        more = copies[1] + 2 * (nb + 1)
        out_specs += [whole(half), whole((strip, QW)), *(whole((strip, width)) for width in widths)]
        out_shape += [shape_of(half, f32), shape_of((strip, QW), f32)]
        out_shape += [shape_of((strip, width), f32) for width in widths]
        scratch += [
            pltpu.VMEM((2,) * (nb + 1) + (strip, QW), bf16),
            pltpu.VMEM(folded, f32),
            pltpu.VMEM((strip, QW), f32),
            pltpu.VMEM((nb + 1, VEC_ROWS, D), f32),
            pltpu.VMEM((nb + 1, VEC_ROWS, D), f32),
            pltpu.VMEM((nb + 2, *half), bf16),
            pltpu.VMEM((nb + 1, *half), bf16),
        ]
        for plan, among in zip(plans, (widths, [QW])):
            for m, first, size, order_of in plan:
                scratch += Scatter.arrivals(nb, size, among[m])
        scratch += dma(copies[0], copies[0], len(plans[0]), more, more, len(plans[1]))
        grads = [v.reshape((2,) * (nb + 1) + (strip, v.shape[2])) for v in grads]
    else:
        grads = []
        out_specs += [whole(folded), whole((2, D, QW))]
        out_shape += [shape_of(folded, f32), shape_of((2, D, QW), bf16)]
    return pl.pallas_call(
        functools.partial(back_kernel, nb, plans),
        grid=(nw, HEADS // GRP),
        in_specs=[
            kept((nw, WIN)), kept((2, 8, VW)), tok, tok, per((WIN, 3 * D)), EXPS, tok, tok, tok,
            kept((D, 3 * D)), kept((D, D)), kept((8, D)), kept((8, D)), *[ANY] * len(grads),
        ],
        out_specs=out_specs,
        out_shape=out_shape,
        scratch_shapes=scratch,
        compiler_params=comm_params(3) if nb else PARAMS,
        name="attend_back",
    )(order, vecs, xc, nrm, qkv, e, linv, att, mg, w, wo, feed, peak, *grads)


BOTH = ("wide", "tensor")
MESH = pl.DeviceIdType.MESH


def bits_of(groups):
    return groups.bit_length() - 1


def orders_of(nb):
    down = tuple(reversed(range(nb)))
    if nb < 2:
        return (down,)
    half = nb // 2
    swapped = down[:-2] + (down[-1], down[-2])
    return (down, swapped, tuple(range(half)) + tuple(reversed(range(half, nb))))


def cuts_of(width, count):
    tiles = width // 128
    sizes = [(tiles + count - 1 - i) // count for i in range(count)]
    cuts, at = [], 0
    for size in sizes:
        if size:
            cuts.append((at * 128, size * 128))
            at += size
    return cuts


class Place:
    def __init__(self, nb):
        self.nb = nb
        self.w = lax.axis_index("wide")
        self.t = lax.axis_index("tensor")
        self.bit = [self.w // (1 << k) % 2 for k in range(nb)]

    def across(self, k):
        return (self.w + (1 - 2 * self.bit[k]) * (1 << k), self.t)

    def sibling(self):
        return (self.w, 1 - self.t)

    def greet(self):
        barrier = pltpu.get_barrier_semaphore()
        partners = [self.across(k) for k in range(self.nb)] + [self.sibling()]
        for partner in partners:
            pl.semaphore_signal(barrier, inc=1, device_id=partner, device_id_type=MESH)
        pl.semaphore_wait(barrier, len(partners))

    def index(self, chosen):
        return tuple(chosen.get(k, slice(None)) for k in reversed(range(self.nb)))


def remote(src, dst, send, recv, to):
    return pltpu.make_async_remote_copy(
        src_ref=src, dst_ref=dst, send_sem=send, recv_sem=recv, device_id=to, device_id_type=MESH
    )


class Gather:
    def __init__(self, place, owns, bufs, send, recv, near):
        self.place, self.owns, self.bufs = place, owns, bufs
        self.send, self.recv, self.near = send, recv, near
        nb = place.nb
        self.streams = []
        orders = orders_of(nb)
        for own, buf in zip(owns, bufs):
            for (first, size), order in zip(cuts_of(own.shape[1], len(orders)), orders):
                self.streams.append((own, buf, first, size, order))

    @staticmethod
    def copies(nb, count):
        return count * (len(orders_of(nb)) * nb + 1)

    def lanes(self, own):
        width = own.shape[1]
        return pl.ds(pl.multiple_of(self.place.t * width, 128), width)

    def local(self, b):
        own, buf = self.owns[b], self.bufs[b]
        mine = self.place.index(dict(enumerate(self.place.bit)))
        return pltpu.make_async_copy(own, buf.at[(*mine, slice(None), self.lanes(own))], self.near.at[b])

    def wide(self, s, p):
        own, buf, first, size, order = self.streams[s]
        place = self.place
        chosen = {k: place.bit[k] for k in order[p:]}
        lanes = pl.ds(pl.multiple_of(place.t * own.shape[1] + first, 128), size)
        region = buf.at[(*place.index(chosen), slice(None), lanes)]
        src = region if p else own.at[:, pl.ds(first, size)]
        at = s * place.nb + p
        return remote(src, region, self.send.at[at], self.recv.at[at], place.across(order[p]))

    def core(self, b):
        own, buf = self.owns[b], self.bufs[b]
        region = buf.at[(*self.place.index({}), slice(None), self.lanes(own))]
        at = len(self.streams) * self.place.nb + b
        return remote(region, region, self.send.at[at], self.recv.at[at], self.place.sibling())

    def step(self, p):
        nb = self.place.nb
        streams, count = range(len(self.streams)), range(len(self.bufs))
        if p == 0:
            for b in count:
                self.local(b).start()
        elif p == 1:
            for b in count:
                self.local(b).wait()
        if 0 < p <= nb:
            for s in streams:
                self.wide(s, p - 1).wait_recv()
        if p < nb:
            for s in streams:
                self.wide(s, p).start()
        elif p == nb:
            for b in count:
                self.core(b).start()
        else:
            for s in streams:
                for q in range(nb):
                    self.wide(s, q).wait_send()
            for b in count:
                self.core(b).wait()

    def steps(self):
        return self.place.nb + 2


class Scatter:
    def __init__(self, place, streams, send, recv, near):
        self.place, self.streams = place, streams
        self.send, self.recv, self.near = send, recv, near

    @staticmethod
    def arrivals(nb, rows, width):
        return [pltpu.VMEM((2,) * (nb - max(p, 0)) + (rows, width), bf16) for p in range(-1, nb + 1)]

    def local(self, s):
        matrix, first, size, order, (own, *arrive), out = self.streams[s]
        src = matrix.at[(self.place.t, *self.place.index({}), pl.ds(first, size), slice(None))]
        return pltpu.make_async_copy(src, own, self.near.at[s])

    def left(self, order, p):
        return [k for k in reversed(range(self.place.nb)) if k not in order[:p]]

    def copy(self, s, p):
        matrix, first, size, order, (own, *arrive), out = self.streams[s]
        place = self.place
        if p == 0:
            src, to = matrix.at[(1 - place.t, *place.index({}), pl.ds(first, size), slice(None))], place.sibling()
        else:
            k = order[p - 1]
            src = arrive[p - 1].at[self.part(order, p, 1 - place.bit[k])]
            to = place.across(k)
        at = s * (place.nb + 1) + p
        return remote(src, arrive[p], self.send.at[at], self.recv.at[at], to)

    def part(self, order, p, value):
        return tuple(value if k == order[p - 1] else slice(None) for k in self.left(order, p - 1))

    def add(self, s, p):
        matrix, first, size, order, (own, *arrive), out = self.streams[s]
        place = self.place
        left = self.left(order, p)

        def one(i, carry):
            picked = {k: i // (1 << j) % 2 for j, k in enumerate(left)}
            there = (*(picked[k] for k in left), slice(None), slice(None))
            if p == 0:
                here = own[there]
            else:
                picked[order[p - 1]] = place.bit[order[p - 1]]
                before = tuple(picked[k] for k in self.left(order, p - 1))
                here = arrive[p - 1][(*before, slice(None), slice(None))]
            total = here.astype(f32) + arrive[p][there].astype(f32)
            if left:
                arrive[p][there] = total.astype(bf16)
            else:
                out[first : first + size, :] = total
            return carry

        if left:
            lax.fori_loop(0, 1 << len(left), one, 0)
        else:
            one(0, 0)

    def step(self, p):
        nb = self.place.nb
        for s in range(len(self.streams)):
            if p == 0:
                self.local(s).start()
            if p == 1:
                self.local(s).wait()
            if p:
                self.copy(s, p - 1).wait_recv()
                self.add(s, p - 1)
            if p <= nb:
                self.copy(s, p).start()
        if p == nb + 1:
            for s in range(len(self.streams)):
                for q in range(nb + 1):
                    self.copy(s, q).wait_send()

    def steps(self):
        return self.place.nb + 2


GATHER_TIMES = (0.0, 0.07, 0.25, 0.44, 0.75, 0.94)
SCATTER_TIMES = (0.0, 0.13, 0.44, 0.63, 0.82, 1.0)


def run_beside(transfer, at_step, times):
    total = pl.num_programs(0) * pl.num_programs(1)
    for p in range(1, transfer.steps()):
        when = times[min(p, len(times) - 1)]
        if when < 1.0:

            @pl.when(at_step == int(when * 64) * total // 64)
            def _():
                transfer.step(p)


def comm_params(collective_id, **more):
    return pltpu.CompilerParams(
        vmem_limit_bytes=VMEM_LIMIT, collective_id=collective_id, has_side_effects=True, **more
    )


def stream_plan(nb, widths, strip):
    first, second = (tuple(reversed(orders_of(nb)[i])) for i in (0, -1 if nb < 2 else 1))
    plan = []
    for m in range(len(widths)):
        plan.append((m, 0, strip // 2, first))
        plan.append((m, strip // 2, strip // 2, second))
    return plan


def build_streams(plan, matrices, arrive, outs, nb):
    streams = []
    for i, (m, first, size, order) in enumerate(plan):
        streams.append((matrices[m], first, size, order, arrive[i * (nb + 2) : (i + 1) * (nb + 2)], outs[m]))
    return streams


class Sums:
    def __init__(self, place, vec, vec_in, table, table_in, send, recv, base):
        self.place, self.base = place, base
        self.vec, self.vec_in, self.table, self.table_in = vec, vec_in, table, table_in
        self.send, self.recv = send, recv

    def pair(self, p):
        place = self.place
        to = place.across(p - 1) if p else place.sibling()
        at = self.base + 2 * p
        table = self.table.at[1 - place.t] if p == 0 else self.table.at[p + 1]
        return (
            remote(self.vec.at[p], self.vec_in.at[p], self.send.at[at], self.recv.at[at], to),
            remote(table, self.table_in.at[p], self.send.at[at + 1], self.recv.at[at + 1], to),
        )

    def step(self, p, vec_out, table_out):
        nb = self.place.nb
        if p:
            vec, table = self.pair(p - 1)
            vec.wait_recv()
            table.wait_recv()
            mine, theirs = self.vec[p - 1], self.vec_in[p - 1]
            summed = iota(mine.shape, 0) < SUM_ROWS
            total = jnp.where(summed, mine + theirs, jnp.maximum(mine, theirs))
            mine = self.table[self.place.t] if p == 1 else self.table[p]
            table_total = mine.astype(f32) + self.table_in[p - 1].astype(f32)
            if p <= nb:
                self.vec[p] = total
                self.table[p + 1] = table_total.astype(bf16)
            else:
                vec_out[...] = total
                table_out[...] = table_total
        if p <= nb:
            for copy in self.pair(p):
                copy.start()
        else:
            for q in range(nb + 1):
                for copy in self.pair(q):
                    copy.wait_send()


def body(
    inputs, cotangent, window_order, region_ids, clip_threshold, norm1_gain, norm1_shift,
    qkv_weight, qv_bias, rel_table, out_weight, out_bias, norm2_gain, norm2_shift,
    expand_weight, expand_bias, reduce_weight, reduce_bias,
):
    parts = lax.axis_size("tensor")
    groups = lax.axis_size("wide")
    mine = lax.axis_index("tensor")
    own = HEADS // parts
    oc, fc = D // parts, FF // parts
    nw = inputs.shape[0] // WIN
    strip = D // groups
    nb = bits_of(groups)
    paired = parts == 2 and groups == 1 << nb and nb > 0 and strip % 32 == 0

    order = lax.dynamic_slice_in_dim(window_order, mine * nw, nw, 0)
    region = lax.dynamic_slice_in_dim(region_ids, mine * nw * WIN, nw * WIN, 0)
    region = region.reshape(nw, WIN).astype(f32)

    def params(first):
        rows = [norm1_gain, norm1_shift, norm2_gain, norm2_shift, out_bias, reduce_bias]
        rows = jnp.pad(jnp.stack(rows + [jnp.zeros((D,), bf16)]), ((0, 0), (0, VW - D)))
        return jnp.concatenate([first[None], rows], axis=0).astype(f32)

    if paired:
        first = jnp.concatenate([qv_bias[0], jnp.zeros((oc,), bf16), qv_bias[1], expand_bias])
        weights = [params(first), padded_table(rel_table), qkv_weight]
        shards = [out_weight.T, expand_weight, reduce_weight.T]
    else:
        qkv_strip = qkv_weight.reshape(strip, own, 3, HD).transpose(0, 2, 1, 3).reshape(strip, 3 * oc)
        shard = jnp.concatenate([qkv_strip, out_weight.T, expand_weight, reduce_weight.T], axis=1)
        full = lax.all_gather(shard, BOTH, axis=0)
        full = full.reshape(groups, parts, strip, shard.shape[1]).transpose(0, 2, 1, 3)
        full = full.reshape(D, parts, shard.shape[1])
        wqkv = full[:, :, : 3 * oc].reshape(D, parts, 3, oc).transpose(0, 2, 1, 3)
        wqkv = wqkv.reshape(D, 3, 2, HALF).transpose(0, 2, 1, 3).reshape(D, 3 * D)
        wo = full[:, :, 3 * oc : 4 * oc].reshape(D, D)
        we = full[:, :, 4 * oc : 4 * oc + fc].reshape(D, FF)
        wr = full[:, :, 4 * oc + fc :].reshape(D, FF)
        small = jnp.concatenate([qv_bias.reshape(-1), expand_bias, rel_table.reshape(-1)])
        small = lax.all_gather(small, "tensor", axis=0)
        qv = small[:, : 2 * oc].reshape(parts, 2, oc).transpose(1, 0, 2).reshape(2, 2, HALF)
        be = small[:, 2 * oc : 2 * oc + fc].reshape(2, FF // 2)
        zero = jnp.zeros((HALF,), bf16)
        vecs = jnp.stack([params(jnp.concatenate([qv[0, v], zero, qv[1, v], be[v]])) for v in range(2)])
        weights = [vecs, wqkv, table_bias(small[:, 2 * oc + fc :].reshape(HEADS, RT))]
        shards = []
        nb = 0

    (xc, nrm, qkv, e, linv, att, peak, vecs, wqkv), gathered = run_attend(
        nw, nb, order, region, inputs, weights, shards
    )
    if paired:
        wo, we, wr = gathered
    layer_out, mg, gwe, gwr, gwo, feed = run_feed(nw, order, vecs, xc, att, cotangent, wo, we, wr)
    input_grad, sums, table, qkv_own, *summed = run_back(
        nw, nb, order, vecs, xc, nrm, qkv, e, linv, att, mg, wqkv, wo, feed, peak, [gwo, gwe, gwr]
    )
    if paired:
        out_own, expand_own, reduce_own = summed
        qkv_out = qkv_own
    else:
        gw = qkv_own

        def cut(grad, width):
            return grad.transpose(1, 0, 2).reshape(D, parts, width).astype(f32)

        gw = gw.reshape(2, D, 3, HALF).transpose(1, 2, 0, 3).reshape(D, 3, parts, oc)
        gw = gw.transpose(0, 2, 1, 3).reshape(D, parts, 3 * oc).astype(f32)
        grads = jnp.concatenate([gw, cut(gwo, oc), cut(gwe, fc), cut(gwr, fc)], axis=2)
        grads = grads.reshape(groups, strip, parts, 4 * oc + 2 * fc).transpose(0, 2, 1, 3)
        grads = grads.reshape(groups * parts * strip, 4 * oc + 2 * fc)
        grads = lax.psum_scatter(grads, BOTH, scatter_dimension=0, tiled=True)
        qkv_out = grads[:, : 3 * oc].reshape(strip, 3, own, HD).transpose(0, 2, 1, 3).reshape(strip, 3 * oc)
        out_own = grads[:, 3 * oc : 4 * oc]
        expand_own, reduce_own = grads[:, 4 * oc : 4 * oc + fc], grads[:, 4 * oc + fc :]
        table = lax.dynamic_slice_in_dim(lax.psum(table, BOTH), mine * own, own, 0)
        sums = jnp.concatenate(
            [lax.psum(sums[:SUM_ROWS], BOTH), lax.pmax(sums[SUM_ROWS:], BOTH)], axis=0
        )

    table_own = table[:, : 2 * WT - 1, :ROWS].reshape(own, RT)
    dbe_own = lax.dynamic_slice_in_dim(sums[6:10].reshape(FF), mine * fc, fc, 0)
    heads_grad = sums[10:13].reshape(2, 3, HALF)
    bias_grad = jnp.stack([heads_grad[:, 0].reshape(D), heads_grad[:, 2].reshape(D)], axis=0)
    bias_own = lax.dynamic_slice_in_dim(bias_grad, mine * oc, oc, 1)
    peak_own = lax.dynamic_slice_in_dim(sums[SUM_ROWS], mine * own, own, 0)
    factor = jnp.sqrt(clip_threshold / jnp.maximum(peak_own, clip_threshold))
    column_factor = jnp.stack([factor, factor, jnp.ones_like(factor)], axis=1)
    clipped_qkv = (
        qkv_weight.astype(f32).reshape(strip, own, 3, HD) * column_factor[None, :, :, None]
    ).reshape(qkv_weight.shape)
    bias_scale = jnp.stack([jnp.repeat(factor, HD), jnp.ones((own * HD,), f32)], axis=0)
    clipped_bias = qv_bias.astype(f32) * bias_scale
    return (
        layer_out,
        input_grad,
        sums[0],
        sums[1],
        qkv_out,
        bias_own,
        table_own,
        out_own.T,
        sums[5],
        sums[2],
        sums[3],
        expand_own,
        dbe_own,
        reduce_own.T,
        sums[4],
        peak_own,
        clipped_qkv,
        clipped_bias,
    )


def solution(mesh):
    tokens = P(BOTH, None)
    in_specs = (
        tokens, tokens, P("wide", None), P("wide"), P(), P(), P(), P("wide", "tensor"),
        P(None, "tensor"), P("tensor", None), P("tensor", "wide"), P(), P(), P(),
        P("wide", "tensor"), P("tensor"), P("tensor", "wide"), P(),
    )
    out_specs = (
        tokens, tokens, P(), P(), P("wide", "tensor"), P(None, "tensor"), P("tensor", None),
        P("tensor", "wide"), P(), P(), P(), P("wide", "tensor"), P("tensor"),
        P("tensor", "wide"), P(), P("tensor"), P("wide", "tensor"), P(None, "tensor"),
    )
    return jax.shard_map(body, mesh=mesh, in_specs=in_specs, out_specs=out_specs, check_vma=False)
```
